32 devices in a mesh: space: 16 (over z, x, core), sub: 2 (over y).
Axes of the slice: x: 2, y: 2, z: 4, core: 2. Of those that a mesh axis runs over, the one named last changes fastest.
Arguments:
- positions: float32 [3, 32, 4, 3, 128], P(None, 'space', 'sub'), may hold values from 0 to 1
- charges: float32 [32, 4, 3, 128], P('space', 'sub'), may hold values from -0.6 to 0.6
- counts: int32 [32, 4, 3], P('space', 'sub'), may hold values from 64 to 128
Outputs:
- forces: float32 [3, 32, 4, 3, 128], P(None, 'space', 'sub')
The draws below stay inside these ranges and needn't reach their ends.
Inputs may be any that keep to these rules, and one draw needn't show every extreme that they name: `counts`: slots 0 to count - 1 of a cell hold atoms; the others are padding.
All inputs are finite; a program needn't handle non-finite values.
Results may differ from the reference program's by a relative error of at most 0.0003.
Values sent between devices are 32-bit elements; how exact they have to be, the bound alone decides.
No kernel may reach another device: no remote copies, remote signals or barrier semaphores. Data moves between devices by JAX's collectives and lax.ppermute only.
A program may use at most 64 MiB of HBM per device.

```python
import math
import jax
import jax.numpy as jnp
from jax import lax

ATOMS = 128
POINTS = 4
REACH = 4
CELLS_X = 32
CELLS_Y = 4
CELLS_Z = 3


def with_ends(drawn, rng, smallest, top_value):
    dims = drawn.shape
    spot = [jax.random.randint(jax.random.fold_in(rng, axis), (), 0, dims[axis]) for axis in range(len(dims))]
    drawn = drawn.at[tuple(spot)].set(smallest)
    longest = dims.index(max(dims))
    spot[longest] = (spot[longest] + 1) % dims[longest]
    return drawn.at[tuple(spot)].set(top_value)


def levels(rng, extent, cuts, least, high):
    loudness = 1.0
    for position, blocks in cuts:
        heights = jax.random.uniform(jax.random.fold_in(jax.random.fold_in(rng, 6), position), (blocks,), jnp.float32, least / len(cuts), high / len(cuts))
        loudness = loudness * jnp.repeat(jnp.exp(heights), extent[position] // blocks).reshape((-1,) + (1,) * (len(extent) - 1 - position))
    return loudness


def bell_draw(key, extent, scale, bound, cuts=(), dtype=jnp.bfloat16):
    entries = scale * jax.random.normal(key, extent, jnp.float32)
    if cuts:
        entries = entries * levels(key, extent, cuts, -0.22, 0.18)
    return jnp.clip(entries, -bound, bound).astype(dtype)


def setup_inputs(seed: int = 0) -> dict:
    arg_keys = jax.random.split(jax.random.key(seed), 4)
    return {
        "positions": jnp.clip(1.0 * jax.random.uniform(arg_keys[0], (3, CELLS_X, CELLS_Y, CELLS_Z, ATOMS), jnp.float32) ** levels(arg_keys[0], (3, CELLS_X, CELLS_Y, CELLS_Z, ATOMS), ((1, 16), (2, 2)), -0.2, 0.2), 0.0, 1.0),
        "charges": bell_draw(arg_keys[1], (CELLS_X, CELLS_Y, CELLS_Z, ATOMS), 0.1, 0.6, ((0, 16), (1, 2)), jnp.float32),
        "counts": with_ends(jax.random.randint(arg_keys[2], (CELLS_X, CELLS_Y, CELLS_Z), ATOMS // 2, ATOMS + 1), jax.random.fold_in(arg_keys[2], 1), ATOMS // 2, ATOMS).astype(jnp.int32),
    }


SOFT_SQUARE = 0.0625
SPLIT_RATE = 0.8
FINE_WIDTHS = (1.0, 2.0)
FINE_WEIGHTS = (2.0, 0.5)
COARSE_FRACTIONS = (8.0, 4.0)
COARSE_WEIGHTS = (4.0, 2.0)
HIGHEST = lax.Precision.HIGHEST

def pair_force(own_pos, own_charge, other_pos, other_charge, offset_vec):
    shifted = own_pos - offset_vec.reshape((3,) + (1,) * (own_pos.ndim - 1))
    spread = shifted[..., :, None] - other_pos[..., None, :]
    square = lax.optimization_barrier(jnp.sum(spread * spread, axis=0)) + SOFT_SQUARE
    length = jnp.sqrt(square)
    factor = jax.scipy.special.erfc(SPLIT_RATE * length) / (square * length)
    factor = factor + 2.0 * SPLIT_RATE / math.sqrt(math.pi) * jnp.exp(-SPLIT_RATE * SPLIT_RATE * square) / square
    stacked = jnp.concatenate([other_charge[None], other_charge[None] * other_pos], axis=0)
    moments = jnp.einsum('...ab,c...b->c...a', factor, stacked, precision=HIGHEST)
    return own_charge * (shifted * moments[0][None] - moments[1:])

def spline(shifted):
    magnitude = jnp.abs(shifted)
    inner = (4.0 - 6.0 * magnitude * magnitude + 3.0 * magnitude * magnitude * magnitude) / 6.0
    outer = (2.0 - magnitude) * (2.0 - magnitude) * (2.0 - magnitude) / 6.0
    return jnp.where(magnitude < 1.0, inner, jnp.where(magnitude < 2.0, outer, 0.0))

def spline_slope(shifted):
    magnitude = jnp.abs(shifted)
    inner = (9.0 * magnitude * magnitude - 12.0 * magnitude) / 6.0
    outer = -(2.0 - magnitude) * (2.0 - magnitude) / 2.0
    return jnp.sign(shifted) * jnp.where(magnitude < 1.0, inner, jnp.where(magnitude < 2.0, outer, 0.0))

def spline_tables(fraction):
    offsets = lax.iota(jnp.int32, POINTS + 3).astype(jnp.float32) - 1.0
    shifted = POINTS * fraction[..., None] - offsets
    return (spline(shifted), spline_slope(shifted))

def make_boxes(coords, charged):
    weight_x = spline_tables(coords[0])[0]
    weight_y = spline_tables(coords[1])[0]
    weight_z = spline_tables(coords[2])[0]
    first = (charged[..., None] * weight_x)[..., :, None] * weight_y[..., None, :]
    return jnp.einsum('...aef,...ag->...efg', first, weight_z, precision=HIGHEST)

def placement_table():
    shape = (POINTS + 3, POINTS, 3)
    entry = lax.broadcasted_iota(jnp.int32, shape, 0)
    inside = lax.broadcasted_iota(jnp.int32, shape, 1)
    which = lax.broadcasted_iota(jnp.int32, shape, 2)
    return (entry - 1 == (which - 1) * POINTS + inside).astype(jnp.float32)

def pick_table(cells, length, first, period):
    shape = (cells, POINTS + 3, length)
    cell_idx = lax.broadcasted_iota(jnp.int32, shape, 0)
    entry = lax.broadcasted_iota(jnp.int32, shape, 1)
    point = lax.broadcasted_iota(jnp.int32, shape, 2)
    return (jnp.mod(POINTS * cell_idx + first + entry, period) == point).astype(jnp.float32)

def gauss_matrix(length, width, first_row, rows):
    row_idx = first_row + lax.broadcasted_iota(jnp.int32, (rows, length), 0)
    col_idx = lax.broadcasted_iota(jnp.int32, (rows, length), 1)
    dist = jnp.mod(row_idx - col_idx, length)
    dist = jnp.minimum(dist, length - dist).astype(jnp.float32)
    return jnp.exp(-dist * dist / (2.0 * width * width))

def taps_for(width):
    return [math.exp(-(step * step) / (2.0 * width * width)) for step in range(-REACH, REACH + 1)]

def long_forces(coords, charged, point_box):
    weight_x, slope_x = spline_tables(coords[0])
    weight_y, slope_y = spline_tables(coords[1])
    weight_z, slope_z = spline_tables(coords[2])
    along_z = jnp.einsum('xyzag,xyzefg->xyzaef', weight_z, point_box, precision=HIGHEST)
    sloped_z = jnp.einsum('xyzag,xyzefg->xyzaef', slope_z, point_box, precision=HIGHEST)
    force_x = jnp.einsum('xyzae,xyzaf,xyzaef->xyza', slope_x, weight_y, along_z, precision=HIGHEST)
    force_y = jnp.einsum('xyzae,xyzaf,xyzaef->xyza', weight_x, slope_y, along_z, precision=HIGHEST)
    force_z = jnp.einsum('xyzae,xyzaf,xyzaef->xyza', weight_x, weight_y, sloped_z, precision=HIGHEST)
    return -POINTS * charged * jnp.stack([force_x, force_y, force_z])

def reference(positions, charges, counts):
    live_mask = (lax.broadcasted_iota(jnp.int32, charges.shape, 3) < counts[..., None]).astype(jnp.float32)
    charged = charges * live_mask
    short = jnp.zeros(positions.shape, jnp.float32)
    for offset in range(27):
        steps_xyz = (offset // 9 - 1, offset // 3 % 3 - 1, offset % 3 - 1)
        back = tuple((-step for step in steps_xyz))
        near_pos = jnp.roll(positions, back, axis=(1, 2, 3))
        near_charge = jnp.roll(charged, back, axis=(0, 1, 2))
        offset_vec = jnp.array(steps_xyz, jnp.float32)

        def slab_force(members, offset_vec=offset_vec):
            return pair_force(members[0], members[1], members[2], members[3], offset_vec)
        result = lax.map(slab_force, (jnp.moveaxis(positions, 1, 0), charged, jnp.moveaxis(near_pos, 1, 0), near_charge))
        short = short + jnp.moveaxis(result, 0, 1)
    boxes = make_boxes(positions, charged)
    table = placement_table()
    placed_x = sum((jnp.einsum('XYZefg,ej->XYZjfg', jnp.roll(boxes, which - 1, axis=0), table[:, :, which], precision=HIGHEST) for which in range(3)))
    placed_y = sum((jnp.einsum('XYZjfg,fl->XYZjlg', jnp.roll(placed_x, which - 1, axis=1), table[:, :, which], precision=HIGHEST) for which in range(3)))
    placed_z = sum((jnp.einsum('XYZjlg,gm->XYZjlm', jnp.roll(placed_y, which - 1, axis=2), table[:, :, which], precision=HIGHEST) for which in range(3)))
    grid_x, grid_y, grid_z = (POINTS * CELLS_X, POINTS * CELLS_Y, POINTS * CELLS_Z)
    charge_grid = placed_z.transpose(0, 3, 1, 4, 2, 5).reshape(grid_x, grid_y, grid_z)
    fine = jnp.zeros(charge_grid.shape, jnp.float32)
    for width, weight in zip(FINE_WIDTHS, FINE_WEIGHTS):
        taps = taps_for(width)
        section = charge_grid
        for axis_num in range(3):
            section = sum((taps[step + REACH] * jnp.roll(section, -step, axis=axis_num) for step in range(-REACH, REACH + 1)))
        fine = fine + weight * section
    coarse_charge = charge_grid.reshape(grid_x // 2, 2, grid_y // 2, 2, grid_z // 2, 2).sum(axis=(1, 3, 5)) * 0.125
    coarse = jnp.zeros(coarse_charge.shape, jnp.float32)
    for fraction, weight in zip(COARSE_FRACTIONS, COARSE_WEIGHTS):
        matrix_x = gauss_matrix(grid_x // 2, grid_x // 2 / fraction, 0, grid_x // 2)
        matrix_y = gauss_matrix(grid_y // 2, grid_y // 2 / fraction, 0, grid_y // 2)
        matrix_z = gauss_matrix(grid_z // 2, grid_z // 2 / fraction, 0, grid_z // 2)
        section = jnp.einsum('ri,ijk->rjk', matrix_x, coarse_charge, precision=HIGHEST)
        section = jnp.einsum('sj,rjk->rsk', matrix_y, section, precision=HIGHEST)
        section = jnp.einsum('tk,rsk->rst', matrix_z, section, precision=HIGHEST)
        coarse = coarse + weight * section
    lifted = jnp.repeat(jnp.repeat(jnp.repeat(coarse, 2, axis=0), 2, axis=1), 2, axis=2)
    potential = fine + lifted
    pick_x = pick_table(CELLS_X, grid_x, -1, grid_x)
    pick_y = pick_table(CELLS_Y, grid_y, -1, grid_y)
    pick_z = pick_table(CELLS_Z, grid_z, -1, grid_z)
    point_box = jnp.einsum('Xei,ijk->Xejk', pick_x, potential, precision=HIGHEST)
    point_box = jnp.einsum('Yfj,Xejk->XYefk', pick_y, point_box, precision=HIGHEST)
    point_box = jnp.einsum('Zgk,XYefk->XYZefg', pick_z, point_box, precision=HIGHEST)
    return short + long_forces(positions, charged, point_box)
```

```python
import functools
import math

import jax
import jax.numpy as jnp
import numpy as np
from jax import lax
from jax.experimental import pallas as pl
from jax.experimental.pallas import tpu as pltpu
from jax.sharding import PartitionSpec as P

F32 = jnp.float32
BF16 = jnp.bfloat16
HIGHEST = lax.Precision.HIGHEST

POINTS = 4
REACH = 4
TAPS = POINTS + 3
SOFT_SQUARE = 0.0625
FINE_WIDTHS = (1.0, 2.0)
FINE_WEIGHTS = (2.0, 0.5)
COARSE_FRACTIONS = (8.0, 4.0)
COARSE_WEIGHTS = (4.0, 2.0)

DECAY = 0.114
SMOOTH = (
    0.004718840075751518,
    0.06055603768478568,
    0.019918877505712862,
    0.1440338177504446,
    0.014789349197372625,
    0.14113616660836056,
)
SCALE = math.sqrt(DECAY * math.log2(math.e))
LEAD = SMOOTH[-1] / SCALE**3
SHIFT = math.log2(LEAD) / (len(SMOOTH) - 1)
MONIC = tuple(
    coef / SCALE**3 / LEAD ** (power / (len(SMOOTH) - 1)) for power, coef in enumerate(SMOOTH)
)
HALF_CONST = 0.5 * (SHIFT - SCALE * SCALE * SOFT_SQUARE)

FEATURES = 32
SOURCES = 16
COLUMN_ROWS = FEATURES + SOURCES
PIECES = 26


def round_up(value, step):
    return -(-value // step) * step


def mul_t(left, right, precision=None):
    return lax.dot_general(
        left, right, (((1,), (1,)), ((), ())), precision=precision, preferred_element_type=F32
    )


def mul(left, right, precision=None):
    return lax.dot_general(
        left, right, (((1,), (0,)), ((), ())), precision=precision, preferred_element_type=F32
    )


def split(value, count):
    pieces = []
    for _ in range(count - 1):
        piece = value.astype(BF16).astype(F32)
        pieces.append(piece)
        value = value - piece
    pieces.append(value.astype(BF16).astype(F32))
    return pieces


class Brick:
    def __init__(self, shape, n_space, n_sub):
        self.bx, self.by, self.bz, self.atoms = shape
        self.n_space, self.n_sub = n_space, n_sub
        self.cols = self.bx * self.by
        self.lanes = self.bz * self.atoms
        self.wide = (self.bz + 2) * self.atoms
        self.px = POINTS * self.bx + 3
        self.py = round_up(POINTS * (self.by - 1) + 8, 8)
        self.pz = POINTS * self.bz
        self.zpad = round_up(self.pz, 16)
        self.group = 128 // self.zpad
        self.atom_rows = 4 * self.cols
        self.blocks = -(-self.px // self.group)
        self.msg_rows = round_up(self.atom_rows, 8) + self.py
        self.msg_lanes = max(self.lanes, self.blocks * 128)
        self.grid_row = round_up(self.atom_rows, 8)
        self.ci = 2 * self.bx + 2
        self.cj = 2 * self.by + 2
        self.ck = 2 * self.bz
        self.coarse_rows = round_up(self.ci, 8)
        self.coarse_lanes = round_up(self.cj * self.ck, 128)
        self.own_rows = round_up(self.cols, 8)
        self.outside = [
            (x, y)
            for x in range(-1, self.bx + 1)
            for y in range(-1, self.by + 1)
            if not (0 <= x < self.bx and 0 <= y < self.by)
        ]
        self.halo_rows = round_up(len(self.outside), 8)
        self.force_rows = round_up(3 * self.cols, 8)

    def col(self, x, y):
        return x * self.by + y


def spline(shifted):
    size = jnp.abs(shifted)
    outer = jnp.maximum(2.0 - size, 0.0)
    inner = jnp.maximum(1.0 - size, 0.0)
    return (outer * outer * outer) * (1.0 / 6.0) - (inner * inner * inner) * (4.0 / 6.0)


def spline_slope(shifted):
    size = jnp.abs(shifted)
    outer = jnp.maximum(2.0 - size, 0.0)
    inner = jnp.maximum(1.0 - size, 0.0)
    slope = 2.0 * (inner * inner) - 0.5 * (outer * outer)
    return jnp.where(shifted < 0.0, -slope, slope)


def shift_xy(brick, row):
    entry = lax.broadcasted_iota(jnp.int32, (8, brick.lanes), 0).astype(F32)
    return POINTS * row - (entry - 1.0)


def shift_z(brick, row):
    parts = []
    for cell in range(brick.bz):
        point = lax.broadcasted_iota(jnp.int32, (brick.zpad, brick.atoms), 0)
        entry = lax.rem(point - POINTS * cell + 1 + brick.pz, brick.pz) - 1
        entry = jnp.where(point < brick.pz, entry, 100)
        value = row[:, cell * brick.atoms : (cell + 1) * brick.atoms]
        parts.append(POINTS * value - entry.astype(F32))
    return jnp.concatenate(parts, axis=1)


def spread_kernel(brick, counts_ref, pos_ref, charge_ref, msg_ref, coarse_ref, grid_ref):
    atoms = brick.atoms
    lane = lax.broadcasted_iota(jnp.int32, (1, atoms), 1)
    for x in range(brick.bx):
        for y in range(brick.by):
            col = brick.col(x, y)
            for z in range(brick.bz):
                span = slice(z * atoms, (z + 1) * atoms)
                for comp in range(3):
                    row = comp * brick.cols + col
                    msg_ref[row : row + 1, span] = pos_ref[comp, x, y, z : z + 1, :]
                row = 3 * brick.cols + col
                charge = charge_ref[x, y, z : z + 1, :]
                msg_ref[row : row + 1, span] = jnp.where(lane < counts_ref[x, y, z], charge, 0.0)
    grid_ref[...] = jnp.zeros(grid_ref.shape, F32)
    for x in range(brick.bx):
        for y in range(brick.by):
            col = brick.col(x, y)
            rows = [
                msg_ref[k * brick.cols + col : k * brick.cols + col + 1, 0 : brick.lanes]
                for k in range(4)
            ]
            along_x = spline(shift_xy(brick, rows[0])) * rows[3]
            along_y = spline(shift_xy(brick, rows[1]))
            along_z = spline(shift_z(brick, rows[2]))
            outer = jnp.concatenate(
                [along_x[e : e + 1, :] * along_y for e in range(TAPS)], axis=0
            )
            box = mul_t(outer, along_z, HIGHEST)
            for e in range(TAPS):
                place = (POINTS * x + e, slice(POINTS * y, POINTS * y + 8), slice(0, brick.zpad))
                grid_ref[place] = grid_ref[place] + box[8 * e : 8 * e + 8, :]
    for block in range(brick.msg_lanes // 128):
        total = jnp.zeros((brick.py, 128), F32)
        for spot in range(brick.group):
            x = block * brick.group + spot
            if x < brick.px:
                plane = grid_ref[x]
                total = total + (pltpu.roll(plane, spot * brick.zpad, 1) if spot else plane)
        msg_ref[brick.grid_row :, block * 128 : (block + 1) * 128] = total
    planes = []
    for idx in range(brick.ci):
        inside = [x for x in (2 * idx - 1, 2 * idx) if 0 <= x < brick.px]
        planes.append(sum(grid_ref[x, :, 0 : brick.zpad] for x in inside))
    stacked = jnp.concatenate(planes, axis=0)
    shape = (brick.zpad, brick.coarse_lanes)
    z_idx = lax.broadcasted_iota(jnp.int32, shape, 0)
    z_lane = lax.broadcasted_iota(jnp.int32, shape, 1)
    used = z_lane < brick.cj * brick.ck
    pairs = (z_idx // 2 == z_lane % brick.ck) & used & (z_idx < brick.pz)
    folded = mul(stacked, jnp.where(pairs, 0.125, 0.0).astype(F32), HIGHEST)
    shape = (brick.py, brick.coarse_lanes)
    y_idx = lax.broadcasted_iota(jnp.int32, shape, 0)
    y_lane = lax.broadcasted_iota(jnp.int32, shape, 1)
    mask = (y_lane // brick.ck == (y_idx + 1) // 2).astype(F32)
    sums = [
        jnp.sum(folded[i * brick.py : (i + 1) * brick.py] * mask, axis=0, keepdims=True)
        for i in range(brick.ci)
    ]
    if brick.coarse_rows > brick.ci:
        sums.append(jnp.zeros((brick.coarse_rows - brick.ci, brick.coarse_lanes), F32))
    coarse_ref[...] = jnp.broadcast_to(jnp.concatenate(sums, axis=0)[None], coarse_ref.shape)


def other_rows(rows, columns):
    table = np.zeros((COLUMN_ROWS * len(columns), PIECES * rows), np.float32)
    for place, row in enumerate(columns):
        base = COLUMN_ROWS * place
        for comp in range(3):
            for slot, piece in enumerate((0, 1, 2, 0, 1, 0)):
                table[base + 6 * comp + slot, (3 * comp + piece) * rows + row] = 1.0
        for piece in range(3):
            table[base + 18 + piece, 12 * rows + row] = 1.0
            table[base + 21 + piece, (9 + piece) * rows + row] = 1.0
        for source in range(12):
            table[base + FEATURES + source, (13 + source) * rows + row] = 1.0
    return table


def own_rows(brick):
    rows = brick.own_rows
    table = np.zeros((brick.cols, 13 * rows, FEATURES), np.float32)
    for col in range(brick.cols):
        for comp in range(3):
            for slot, piece in enumerate((0, 0, 0, 1, 1, 2)):
                table[col, (3 * comp + piece) * rows + col, 6 * comp + slot] = 2.0
        for piece in range(3):
            table[col, (9 + piece) * rows + col, 18 + piece] = 1.0
            table[col, 12 * rows + col, 21 + piece] = 1.0
    return table


def stack_pieces(brick, rows, values, places, piece_ref, coord_ref=None):
    atoms = brick.atoms

    def extend(value):
        return jnp.concatenate([value[:, -atoms:], value, value[:, :atoms]], axis=1)

    index = lax.broadcasted_iota(jnp.int32, (rows, 1), 0)
    offset_x = jnp.zeros((rows, 1), F32)
    offset_y = jnp.zeros((rows, 1), F32)
    for row, (x, y) in enumerate(places):
        offset_x = jnp.where(index == row, x - 0.5 * brick.bx, offset_x)
        offset_y = jnp.where(index == row, y - 0.5 * brick.by, offset_y)
    along_z = [values[2][:, z * atoms : (z + 1) * atoms] for z in range(brick.bz)]
    along_z = [along_z[-1]] + along_z + [along_z[0]]
    along_z = [value + (z - 1 - 0.5 * brick.bz) for z, value in enumerate(along_z)]
    coords = [
        extend((values[0] + offset_x) * SCALE),
        extend((values[1] + offset_y) * SCALE),
        jnp.concatenate(along_z, axis=1) * SCALE,
    ]
    charge = extend(values[3])
    square = HALF_CONST - (
        coords[0] * coords[0] + coords[1] * coords[1] + coords[2] * coords[2]
    )
    pieces = []
    for value in coords + [square]:
        pieces += split(value, 3)
    pieces.append(jnp.ones((rows, brick.wide), F32))
    for value in [charge] + [charge * coord for coord in coords]:
        pieces += split(value, 3)
    pieces.append(jnp.zeros((rows, brick.wide), F32))
    for number, piece in enumerate(pieces):
        piece_ref[number * rows : (number + 1) * rows, :] = piece
    if coord_ref is not None:
        for comp in range(3):
            coord_ref[comp * rows : (comp + 1) * rows, :] = coords[comp]


def load_own(brick, msg_ref, piece_ref, coord_ref):
    pad = brick.own_rows - brick.cols
    values = []
    for k in range(4):
        value = msg_ref[k * brick.cols : (k + 1) * brick.cols, 0 : brick.lanes]
        if pad:
            value = jnp.concatenate([value, jnp.zeros((pad, brick.lanes), F32)], axis=0)
        values.append(value)
    places = [(x, y) for x in range(brick.bx) for y in range(brick.by)]
    stack_pieces(brick, brick.own_rows, values, places, piece_ref, coord_ref)


def load_left(brick, piece_ref, own_table_ref, left_ref):
    span = slice(brick.atoms, brick.atoms + brick.lanes)
    rows = 13 * brick.own_rows
    full = round_up(rows, 128)
    turned = piece_ref[0:full, span].T[:, 0:rows].astype(BF16)
    for col in range(brick.cols):
        left_ref[col] = mul(turned, own_table_ref[col]).astype(BF16)


def pair_factor(left, right):
    power = mul(left, right)
    inverse = lax.rsqrt(SHIFT - power)
    base = jnp.exp2(power)
    smooth = base + MONIC[4]
    for coef in MONIC[3::-1]:
        smooth = smooth * base + coef
    factor = inverse * (inverse * inverse) - smooth
    high = factor.astype(BF16)
    low = (factor - high.astype(F32)).astype(BF16)
    return high, low


def sources(other_ref, place, span):
    base = COLUMN_ROWS * place
    return other_ref[base + FEATURES : base + COLUMN_ROWS, span]


def features(other_ref, place, span):
    base = COLUMN_ROWS * place
    return other_ref[base : base + FEATURES, span]


def moments(total, quantity):
    base = 3 * quantity
    return total[base : base + 1] + total[base + 1 : base + 2] + total[base + 2 : base + 3]


def inner_kernel(
    brick,
    msg_ref,
    own_table_ref,
    other_table_ref,
    force_ref,
    piece_ref,
    coord_ref,
    left_ref,
    other_ref,
    total_ref,
):
    atoms = brick.atoms
    load_own(brick, msg_ref, piece_ref, coord_ref)
    load_left(brick, piece_ref, own_table_ref, left_ref)
    other_ref[...] = mul(other_table_ref[...], piece_ref[...].astype(BF16)).astype(BF16)
    total_ref[...] = jnp.zeros(total_ref.shape, F32)
    force_ref[...] = jnp.zeros(force_ref.shape, F32)

    def block(col, other, z, span, first_back):
        own_span = slice((z + 1) * atoms, (z + 2) * atoms)
        left = left_ref[col, z * atoms : (z + 1) * atoms, :]
        high, low = pair_factor(left, features(other_ref, other, span))
        source = sources(other_ref, other, span)
        total_ref[col, :, own_span] += mul_t(source, high) + mul_t(source, low)
        back = sources(other_ref, col, own_span)
        back_span = slice(span.start + first_back, span.stop)
        total_ref[other, :, back_span] += mul(back, high[:, first_back:]) + mul(
            back, low[:, first_back:]
        )

    cells = [(x, y) for x in range(brick.bx) for y in range(brick.by)]
    for first, (x, y) in enumerate(cells):
        for second in range(first + 1, len(cells)):
            if max(abs(x - cells[second][0]), abs(y - cells[second][1])) > 1:
                continue
            for z in range(brick.bz):
                block(first, second, z, slice(z * atoms, (z + 3) * atoms), 0)
    for col in range(brick.cols):
        for z in range(brick.bz):
            block(col, col, z, slice((z + 1) * atoms, (z + 3) * atoms), atoms)

    for col in range(brick.cols):
        total = total_ref[col]
        charge = msg_ref[3 * brick.cols + col : 3 * brick.cols + col + 1, 0 : brick.lanes]
        weight = moments(total, 0)
        for comp in range(3):
            row = comp * brick.own_rows + col
            wide = coord_ref[row : row + 1, :] * weight - moments(total, 1 + comp)
            parts = [wide[:, (z + 1) * atoms : (z + 2) * atoms] for z in range(brick.bz)]
            parts[-1] = parts[-1] + wide[:, :atoms]
            parts[0] = parts[0] + wide[:, -atoms:]
            row = comp * brick.cols + col
            force_ref[row : row + 1, :] = (
                jnp.concatenate(parts, axis=1) * charge * (SCALE * SCALE)
            )


def halo_kernel(brick, sender, n_msgs, *refs):
    atoms = brick.atoms
    msg_ref = refs[0]
    other_msgs = refs[1 : 1 + n_msgs]
    own_table_ref, other_table_ref, part_ref, force_ref = refs[1 + n_msgs : 5 + n_msgs]
    piece_ref, coord_ref, left_ref, row_ref, halo_ref, other_ref = refs[5 + n_msgs :]
    load_own(brick, msg_ref, piece_ref, coord_ref)
    load_left(brick, piece_ref, own_table_ref, left_ref)
    rows = brick.halo_rows
    row_ref[...] = jnp.zeros(row_ref.shape, F32)
    for place, (x, y) in enumerate(brick.outside):
        near = other_msgs[sender[(x // brick.bx, y // brick.by)]]
        col = brick.col(x % brick.bx, y % brick.by)
        for k in range(4):
            row_ref[k * rows + place : k * rows + place + 1, :] = near[
                k * brick.cols + col : k * brick.cols + col + 1, 0 : brick.lanes
            ]
    values = [row_ref[k * rows : (k + 1) * rows, :] for k in range(4)]
    stack_pieces(brick, rows, values, brick.outside, halo_ref)
    other_ref[...] = mul(other_table_ref[...], halo_ref[...].astype(BF16)).astype(BF16)
    force_ref[...] = part_ref[...]
    for x in range(brick.bx):
        for y in range(brick.by):
            col = brick.col(x, y)
            near = [
                place
                for place, (ox, oy) in enumerate(brick.outside)
                if max(abs(ox - x), abs(oy - y)) <= 1
            ]
            for z in range(brick.bz):
                span = slice(z * atoms, (z + 3) * atoms)
                own_span = slice(z * atoms, (z + 1) * atoms)
                left = left_ref[col, own_span, :]
                total = jnp.zeros((SOURCES, atoms), F32)
                for place in near:
                    high, low = pair_factor(left, features(other_ref, place, span))
                    source = sources(other_ref, place, span)
                    total = total + (mul_t(source, high) + mul_t(source, low))
                charge = msg_ref[3 * brick.cols + col : 3 * brick.cols + col + 1, own_span]
                weight = moments(total, 0)
                for comp in range(3):
                    row = comp * brick.own_rows + col
                    coord = coord_ref[row : row + 1, (z + 1) * atoms : (z + 2) * atoms]
                    value = (coord * weight - moments(total, 1 + comp)) * charge
                    row = comp * brick.cols + col
                    force_ref[row : row + 1, own_span] += value * (SCALE * SCALE)


def fine_tables(brick):
    ext_x = brick.px + 2 * REACH
    rows_y = brick.py + POINTS * brick.by
    along_z = np.zeros((128, 128 * len(FINE_WIDTHS)), np.float32)
    along_xy = np.zeros((brick.px * brick.py, len(FINE_WIDTHS) * ext_x * rows_y), np.float32)

    def tap(dist, width):
        return np.where(np.abs(dist) <= REACH, np.exp(-(dist * dist) / (2.0 * width * width)), 0.0)

    for number, (width, weight) in enumerate(zip(FINE_WIDTHS, FINE_WEIGHTS)):
        for step in range(-REACH, REACH + 1):
            for z in range(brick.pz):
                along_z[(z + step) % brick.pz, 128 * number + z] += weight * tap(
                    np.float64(step), width
                )
        out_x = np.arange(brick.px) - 1.0
        in_x = np.arange(ext_x) - 1.0 - REACH
        out_y = np.arange(brick.py) - 1.0
        in_y = np.arange(rows_y) - 1.0 - POINTS * brick.by
        mat_x = tap(out_x[:, None] - in_x[None, :], width)
        mat_y = tap(out_y[:, None] - in_y[None, :], width)
        mat_y[POINTS * brick.by + 3 :] = 0.0
        size = ext_x * rows_y
        along_xy[:, number * size : (number + 1) * size] = np.kron(mat_x, mat_y)
    return along_xy, along_z


def coarse_table(brick):
    table = np.zeros((len(COARSE_WEIGHTS) * brick.coarse_lanes, 128), np.float32)
    length = brick.ck
    for number, (fraction, weight) in enumerate(zip(COARSE_FRACTIONS, COARSE_WEIGHTS)):
        width = length / fraction
        for row in range(brick.cj * brick.ck):
            for z in range(brick.pz):
                dist = (row - z // 2) % length
                dist = min(dist, length - dist)
                table[number * brick.coarse_lanes + row, z] = weight * math.exp(
                    -(dist * dist) / (2.0 * width * width)
                )
    return table


def gauss(row, col, length, fraction):
    dist = lax.rem(row - col + 2 * length, length)
    dist = jnp.minimum(dist, length - dist).astype(F32)
    width = length / fraction
    return jnp.exp(dist * dist * (-1.0 / (2.0 * width * width)))


def potential_kernel(brick, sender, n_msgs, *refs):
    atoms = brick.atoms
    place_ref, msg_ref = refs[0:2]
    other_msgs = refs[2 : 2 + n_msgs]
    (
        whole_ref,
        short_ref,
        xy_high_ref,
        xy_low_ref,
        z_ref,
        coarse_z_ref,
        out_ref,
        ext_ref,
        pot_ref,
    ) = refs[2 + n_msgs :]
    step_y = POINTS * brick.by
    rows_y = brick.py + step_y
    ext_x = brick.px + 2 * REACH
    planes = {}
    for dx in (-1, 0, 1):
        grids = []
        for dy in (-1, 0, 1):
            source = msg_ref if (dx, dy) == (0, 0) else other_msgs[sender[(dx, dy)]]
            grids.append(source[brick.grid_row :, 0 : brick.blocks * 128])
        full = brick.py + 2 * step_y
        tiles = [None] * (full // 8)
        for number, grid in enumerate(grids):
            for tile in range(brick.py // 8):
                spot = tile + number * step_y // 8
                value = grid[8 * tile : 8 * tile + 8]
                tiles[spot] = value if tiles[spot] is None else tiles[spot] + value
        column = jnp.concatenate(tiles[: rows_y // 8], axis=0)
        for x in range(brick.px):
            spot = x + POINTS * brick.bx * dx + REACH
            if 0 <= spot < ext_x:
                block, shift = divmod(x, brick.group)
                value = column[:, block * 128 : (block + 1) * 128]
                if shift:
                    value = pltpu.roll(value, 128 - shift * brick.zpad, 1)
                planes[spot] = planes[spot] + value if spot in planes else value
    for spot in range(ext_x):
        ext_ref[spot * rows_y : (spot + 1) * rows_y, :] = planes[spot]
    along = mul(ext_ref[...], z_ref[...], HIGHEST)
    along = jnp.concatenate([along[:, :128], along[:, 128:]], axis=0)
    high = along.astype(BF16)
    low = (along - high.astype(F32)).astype(BF16)
    potential = mul(xy_high_ref[...], high) + (
        mul(xy_high_ref[...], low) + mul(xy_low_ref[...], high)
    )

    total_x = 2 * brick.bx * brick.n_space
    total_y = 2 * brick.by * brick.n_sub
    first_x = place_ref[0] * (2 * brick.bx)
    first_y = place_ref[1] * (2 * brick.by)
    out_rows = round_up(brick.px, 8)
    shape = (out_rows, brick.n_space * brick.coarse_rows)
    point = lax.broadcasted_iota(jnp.int32, shape, 0)
    lane = lax.broadcasted_iota(jnp.int32, shape, 1)
    row_x = first_x + (point + 1) // 2 - 1
    col_x = lane // brick.coarse_rows * (2 * brick.bx) + lane % brick.coarse_rows - 1
    live = lane % brick.coarse_rows < brick.ci
    mats_x = jnp.concatenate(
        [
            jnp.where(live, gauss(row_x, col_x, total_x, fraction), 0.0)
            for fraction in COARSE_FRACTIONS
        ],
        axis=0,
    )
    shape = (brick.py, brick.coarse_lanes)
    point = lax.broadcasted_iota(jnp.int32, shape, 0)
    lane = lax.broadcasted_iota(jnp.int32, shape, 1)
    row_y = first_y + (point + 1) // 2 - 1
    live = lane < brick.cj * brick.ck
    lefts = [[None] * brick.px for _ in COARSE_FRACTIONS]
    for sub in range(brick.n_sub):
        part = whole_ref[:, sub].reshape(
            brick.n_space * brick.coarse_rows, brick.coarse_lanes
        )
        mixed = mul(mats_x, part, HIGHEST)
        col_y = sub * (2 * brick.by) + lane // brick.ck - 1
        for number, fraction in enumerate(COARSE_FRACTIONS):
            mat_y = jnp.where(live, gauss(row_y, col_y, total_y, fraction), 0.0)
            for x in range(brick.px):
                row = number * out_rows + x
                value = mixed[row : row + 1] * mat_y
                done = lefts[number][x]
                lefts[number][x] = value if done is None else done + value
    left = jnp.concatenate([jnp.concatenate(rows, axis=0) for rows in lefts], axis=1)
    potential = potential + mul(left, coarse_z_ref[...], HIGHEST)
    for x in range(brick.px):
        pot_ref[x] = potential[x * brick.py : (x + 1) * brick.py]

    for x in range(brick.bx):
        for y in range(brick.by):
            col = brick.col(x, y)
            rows = [
                msg_ref[k * brick.cols + col : k * brick.cols + col + 1, 0 : brick.lanes]
                for k in range(4)
            ]
            shifted = [
                shift_xy(brick, rows[0]),
                shift_xy(brick, rows[1]),
                shift_z(brick, rows[2]),
            ]
            weights = [spline(value) for value in shifted]
            slopes = [spline_slope(value) for value in shifted]
            box = jnp.concatenate(
                [
                    pot_ref[POINTS * x + e, POINTS * y : POINTS * y + 8, 0 : brick.zpad]
                    for e in range(TAPS)
                ],
                axis=0,
            )
            both = mul(box, jnp.concatenate([weights[2], slopes[2]], axis=1), HIGHEST)
            along_z = both[:, : brick.lanes]
            sloped_z = both[:, brick.lanes :]
            sums = [0.0, 0.0, 0.0]
            for e in range(TAPS):
                weight = weights[0][e : e + 1]
                slope = slopes[0][e : e + 1]
                flat = along_z[8 * e : 8 * e + 8]
                steep = sloped_z[8 * e : 8 * e + 8]
                sums[0] = sums[0] + flat * slope
                sums[1] = sums[1] + flat * weight
                sums[2] = sums[2] + steep * weight
            across = (weights[1], slopes[1], weights[1])
            for comp in range(3):
                force = jnp.sum(sums[comp] * across[comp], axis=0, keepdims=True)
                row = comp * brick.cols + col
                force = short_ref[row : row + 1, :] - POINTS * (rows[3] * force)
                for z in range(brick.bz):
                    out_ref[comp, x, y, z : z + 1, :] = force[:, z * atoms : (z + 1) * atoms]


VMEM = pl.BlockSpec(memory_space=pltpu.VMEM)
SMEM = pl.BlockSpec(memory_space=pltpu.SMEM)


def call(kernel, out_shape, in_specs, scratch, flops, *args):
    single = not isinstance(out_shape, (list, tuple))
    return pl.pallas_call(
        kernel,
        out_shape=out_shape,
        in_specs=in_specs,
        out_specs=VMEM if single else [VMEM] * len(out_shape),
        scratch_shapes=scratch,
        compiler_params=pltpu.CompilerParams(vmem_limit_bytes=40 * 1024 * 1024),
        cost_estimate=pl.CostEstimate(flops=flops, bytes_accessed=10**5, transcendentals=0),
    )(*args)


def neighbours(brick, msg):
    found = {}
    sender = {}
    msgs = []
    for dx in (-1, 0, 1):
        for dy in (-1, 0, 1):
            if (dx, dy) == (0, 0):
                continue
            key = (dx % brick.n_space, dy % brick.n_sub)
            if key not in found:
                found[key] = len(msgs)
                pairs = []
                for i in range(brick.n_space):
                    for j in range(brick.n_sub):
                        source = (i + dx) % brick.n_space * brick.n_sub + (j + dy) % brick.n_sub
                        pairs.append((source, i * brick.n_sub + j))
                msgs.append(lax.ppermute(msg, ("space", "sub"), pairs))
            sender[(dx, dy)] = found[key]
    return sender, msgs


def body(n_space, n_sub, positions, charges, counts):
    brick = Brick(charges.shape, n_space, n_sub)
    n_dev = n_space * n_sub
    own_table = jnp.asarray(own_rows(brick), BF16)
    inner_table = jnp.asarray(other_rows(brick.own_rows, range(brick.cols)), BF16)
    outer_table = jnp.asarray(other_rows(brick.halo_rows, range(len(brick.outside))), BF16)
    along_xy, along_z = fine_tables(brick)
    xy_high = along_xy.astype(BF16)
    xy_low = (along_xy - xy_high.astype(np.float32)).astype(BF16)
    coarse_z = coarse_table(brick)
    place = jnp.stack([lax.axis_index("space"), lax.axis_index("sub")]).astype(jnp.int32)

    msg, coarse = call(
        functools.partial(spread_kernel, brick),
        [
            jax.ShapeDtypeStruct((brick.msg_rows, brick.msg_lanes), F32),
            jax.ShapeDtypeStruct((n_dev, brick.coarse_rows, brick.coarse_lanes), F32),
        ],
        [SMEM, VMEM, VMEM],
        [pltpu.VMEM((brick.px, brick.py, 128), F32)],
        10**7,
        counts,
        positions,
        charges,
    )
    sender, msgs = neighbours(brick, msg)
    whole = lax.all_to_all(coarse, ("space", "sub"), 0, 0, tiled=True)
    whole = whole.reshape(n_space, n_sub, brick.coarse_rows, brick.coarse_lanes)

    own_scratch = [
        pltpu.VMEM((PIECES * brick.own_rows, brick.wide), F32),
        pltpu.VMEM((3 * brick.own_rows, brick.wide), F32),
        pltpu.VMEM((brick.cols, brick.lanes, FEATURES), BF16),
    ]
    force_shape = jax.ShapeDtypeStruct((brick.force_rows, brick.lanes), F32)
    part = call(
        functools.partial(inner_kernel, brick),
        force_shape,
        [VMEM] * 3,
        own_scratch
        + [
            pltpu.VMEM((COLUMN_ROWS * brick.cols, brick.wide), BF16),
            pltpu.VMEM((brick.cols, SOURCES, brick.wide), F32),
        ],
        10**10,
        msg,
        own_table,
        inner_table,
    )
    n_out = len(brick.outside)
    short = call(
        functools.partial(halo_kernel, brick, sender, len(msgs)),
        force_shape,
        [VMEM] * (4 + len(msgs)),
        own_scratch
        + [
            pltpu.VMEM((4 * brick.halo_rows, brick.lanes), F32),
            pltpu.VMEM((PIECES * brick.halo_rows, brick.wide), F32),
            pltpu.VMEM((COLUMN_ROWS * n_out, brick.wide), BF16),
        ],
        10**10,
        msg,
        *msgs,
        own_table,
        outer_table,
        part,
    )
    ext_x = brick.px + 2 * REACH
    rows_y = brick.py + POINTS * brick.by
    return call(
        functools.partial(potential_kernel, brick, sender, len(msgs)),
        jax.ShapeDtypeStruct(positions.shape, F32),
        [SMEM] + [VMEM] * (7 + len(msgs)),
        [
            pltpu.VMEM((ext_x * rows_y, 128), F32),
            pltpu.VMEM((brick.px, brick.py, 128), F32),
        ],
        10**8,
        place,
        msg,
        *msgs,
        whole,
        short,
        xy_high,
        xy_low,
        jnp.asarray(along_z),
        jnp.asarray(coarse_z),
    )


def solution(mesh):
    in_specs = (
        P(None, "space", "sub", None, None),
        P("space", "sub", None, None),
        P("space", "sub", None),
    )
    out_specs = P(None, "space", "sub", None, None)
    run = functools.partial(body, mesh.shape["space"], mesh.shape["sub"])
    return jax.shard_map(run, mesh=mesh, in_specs=in_specs, out_specs=out_specs, check_vma=False)
```

```python
import functools
import math

import jax
import jax.numpy as jnp
import numpy as np
from jax import lax
from jax.experimental import pallas as pl
from jax.experimental.pallas import tpu as pltpu
from jax.sharding import PartitionSpec as P

F32 = jnp.float32
BF16 = jnp.bfloat16
HIGHEST = lax.Precision.HIGHEST

POINTS = 4
REACH = 4
TAPS = POINTS + 3
SOFT_SQUARE = 0.0625
FINE_WIDTHS = (1.0, 2.0)
FINE_WEIGHTS = (2.0, 0.5)
COARSE_FRACTIONS = (8.0, 4.0)
COARSE_WEIGHTS = (4.0, 2.0)

DECAY = 0.114
SMOOTH = (
    0.004718840075751518,
    0.06055603768478568,
    0.019918877505712862,
    0.1440338177504446,
    0.014789349197372625,
    0.14113616660836056,
)
SCALE = math.sqrt(DECAY * math.log2(math.e))
LEAD = SMOOTH[-1] / SCALE**3
SHIFT = math.log2(LEAD) / (len(SMOOTH) - 1)
MONIC = tuple(
    coef / SCALE**3 / LEAD ** (power / (len(SMOOTH) - 1)) for power, coef in enumerate(SMOOTH)
)
HALF_CONST = 0.5 * (SHIFT - SCALE * SCALE * SOFT_SQUARE)

FEATURES = 32
SOURCES = 16


def round_up(value, step):
    return -(-value // step) * step


def mul_t(left, right, precision=None):
    return lax.dot_general(
        left, right, (((1,), (1,)), ((), ())), precision=precision, preferred_element_type=F32
    )


def mul(left, right, precision=None):
    return lax.dot_general(
        left, right, (((1,), (0,)), ((), ())), precision=precision, preferred_element_type=F32
    )


def split(value, count):
    pieces = []
    for _ in range(count - 1):
        piece = value.astype(BF16).astype(F32)
        pieces.append(piece)
        value = value - piece
    pieces.append(value.astype(BF16).astype(F32))
    return pieces


class Brick:
    def __init__(self, shape, n_space, n_sub):
        self.bx, self.by, self.bz, self.atoms = shape
        self.n_space, self.n_sub = n_space, n_sub
        self.cols = self.bx * self.by
        self.lanes = self.bz * self.atoms
        self.wide = (self.bz + 2) * self.atoms
        self.px = POINTS * self.bx + 3
        self.py = round_up(POINTS * (self.by - 1) + 8, 8)
        self.pz = POINTS * self.bz
        self.zpad = round_up(self.pz, 16)
        self.group = 128 // self.zpad
        self.atom_rows = 4 * self.cols
        self.blocks = -(-self.px // self.group)
        self.msg_rows = round_up(self.atom_rows, 8) + self.py
        self.msg_lanes = max(self.lanes, self.blocks * 128)
        self.grid_row = round_up(self.atom_rows, 8)
        self.ci = 2 * self.bx + 2
        self.cj = 2 * self.by + 2
        self.ck = 2 * self.bz
        self.coarse_rows = round_up(self.ci, 8)
        self.coarse_lanes = round_up(self.cj * self.ck, 128)
        self.own_rows = round_up(self.cols, 8)
        self.columns = [
            (x, y) for x in range(-1, self.bx + 1) for y in range(-1, self.by + 1)
        ]
        self.ext_rows = round_up(len(self.columns), 8)
        self.force_rows = round_up(3 * self.cols, 8)

    def col(self, x, y):
        return x * self.by + y


def spline(shifted):
    size = jnp.abs(shifted)
    outer = jnp.maximum(2.0 - size, 0.0)
    inner = jnp.maximum(1.0 - size, 0.0)
    return (outer * outer * outer) * (1.0 / 6.0) - (inner * inner * inner) * (4.0 / 6.0)


def spline_slope(shifted):
    size = jnp.abs(shifted)
    outer = jnp.maximum(2.0 - size, 0.0)
    inner = jnp.maximum(1.0 - size, 0.0)
    slope = 2.0 * (inner * inner) - 0.5 * (outer * outer)
    return jnp.where(shifted < 0.0, -slope, slope)


def shift_xy(brick, row):
    entry = lax.broadcasted_iota(jnp.int32, (8, brick.lanes), 0).astype(F32)
    return POINTS * row - (entry - 1.0)


def shift_z(brick, row):
    parts = []
    for cell in range(brick.bz):
        point = lax.broadcasted_iota(jnp.int32, (brick.zpad, brick.atoms), 0)
        entry = lax.rem(point - POINTS * cell + 1 + brick.pz, brick.pz) - 1
        entry = jnp.where(point < brick.pz, entry, 100)
        value = row[:, cell * brick.atoms : (cell + 1) * brick.atoms]
        parts.append(POINTS * value - entry.astype(F32))
    return jnp.concatenate(parts, axis=1)


def spread_kernel(brick, counts_ref, pos_ref, charge_ref, msg_ref, coarse_ref, grid_ref):
    atoms = brick.atoms
    lane = lax.broadcasted_iota(jnp.int32, (1, atoms), 1)
    for x in range(brick.bx):
        for y in range(brick.by):
            col = brick.col(x, y)
            for z in range(brick.bz):
                span = slice(z * atoms, (z + 1) * atoms)
                for comp in range(3):
                    row = comp * brick.cols + col
                    msg_ref[row : row + 1, span] = pos_ref[comp, x, y, z : z + 1, :]
                row = 3 * brick.cols + col
                charge = charge_ref[x, y, z : z + 1, :]
                msg_ref[row : row + 1, span] = jnp.where(lane < counts_ref[x, y, z], charge, 0.0)
    grid_ref[...] = jnp.zeros(grid_ref.shape, F32)
    for x in range(brick.bx):
        for y in range(brick.by):
            col = brick.col(x, y)
            rows = [
                msg_ref[k * brick.cols + col : k * brick.cols + col + 1, 0 : brick.lanes]
                for k in range(4)
            ]
            along_x = spline(shift_xy(brick, rows[0])) * rows[3]
            along_y = spline(shift_xy(brick, rows[1]))
            along_z = spline(shift_z(brick, rows[2]))
            outer = jnp.concatenate(
                [along_x[e : e + 1, :] * along_y for e in range(TAPS)], axis=0
            )
            box = mul_t(outer, along_z, HIGHEST)
            for e in range(TAPS):
                place = (POINTS * x + e, slice(POINTS * y, POINTS * y + 8), slice(0, brick.zpad))
                grid_ref[place] = grid_ref[place] + box[8 * e : 8 * e + 8, :]
    for block in range(brick.msg_lanes // 128):
        total = jnp.zeros((brick.py, 128), F32)
        for spot in range(brick.group):
            x = block * brick.group + spot
            if x < brick.px:
                plane = grid_ref[x]
                total = total + (pltpu.roll(plane, spot * brick.zpad, 1) if spot else plane)
        msg_ref[brick.grid_row :, block * 128 : (block + 1) * 128] = total
    planes = []
    for idx in range(brick.ci):
        inside = [x for x in (2 * idx - 1, 2 * idx) if 0 <= x < brick.px]
        planes.append(sum(grid_ref[x, :, 0 : brick.zpad] for x in inside))
    stacked = jnp.concatenate(planes, axis=0)
    shape = (brick.zpad, brick.coarse_lanes)
    z_idx = lax.broadcasted_iota(jnp.int32, shape, 0)
    z_lane = lax.broadcasted_iota(jnp.int32, shape, 1)
    used = z_lane < brick.cj * brick.ck
    pairs = (z_idx // 2 == z_lane % brick.ck) & used & (z_idx < brick.pz)
    folded = mul(stacked, jnp.where(pairs, 0.125, 0.0).astype(F32), HIGHEST)
    shape = (brick.py, brick.coarse_lanes)
    y_idx = lax.broadcasted_iota(jnp.int32, shape, 0)
    y_lane = lax.broadcasted_iota(jnp.int32, shape, 1)
    mask = (y_lane // brick.ck == (y_idx + 1) // 2).astype(F32)
    sums = [
        jnp.sum(folded[i * brick.py : (i + 1) * brick.py] * mask, axis=0, keepdims=True)
        for i in range(brick.ci)
    ]
    if brick.coarse_rows > brick.ci:
        sums.append(jnp.zeros((brick.coarse_rows - brick.ci, brick.coarse_lanes), F32))
    coarse_ref[...] = jnp.broadcast_to(jnp.concatenate(sums, axis=0)[None], coarse_ref.shape)


def store_pieces(piece_ref, rows, arrays):
    for number, value in enumerate(arrays):
        for block in range(piece_ref.shape[0]):
            piece_ref[block, number * rows : (number + 1) * rows, :] = value[
                :, block * 128 : (block + 1) * 128
            ]


def load_pieces(piece_ref, rows, row, count):
    parts = [
        piece_ref[block, pl.ds(row, count, stride=rows), :] for block in range(piece_ref.shape[0])
    ]
    return jnp.concatenate(parts, axis=1)


def feature_arrays(coords, square, order, square_first):
    rows = coords[0].shape
    arrays = []
    for value in coords:
        pieces = split(value, 3)
        arrays += [pieces[piece] for piece in order]
    squares = split(square, 3)
    ones = [jnp.ones(rows, F32)] * 3
    arrays += squares + ones if square_first else ones + squares
    return arrays + [jnp.zeros(rows, F32)] * (FEATURES - len(arrays))


def source_arrays(coords, charge):
    arrays = []
    for value in [charge] + [charge * coord for coord in coords]:
        arrays += split(value, 3)
    return arrays + [jnp.zeros(charge.shape, F32)] * (SOURCES - len(arrays))


def minus_square(coords):
    return HALF_CONST - (coords[0] * coords[0] + coords[1] * coords[1] + coords[2] * coords[2])


def pair_factor(left, right):
    power = mul(left, right)
    inverse = lax.rsqrt(SHIFT - power)
    base = jnp.exp2(power)
    smooth = base + MONIC[4]
    for coef in MONIC[3::-1]:
        smooth = smooth * base + coef
    factor = inverse * (inverse * inverse) - smooth
    high = factor.astype(BF16)
    low = (factor - high.astype(F32)).astype(BF16)
    return high, low


def moments(total, quantity):
    base = 3 * quantity
    return total[base : base + 1] + total[base + 1 : base + 2] + total[base + 2 : base + 3]


def pairs_kernel(brick, sender, n_msgs, *refs):
    atoms, lanes = brick.atoms, brick.lanes
    msg_ref = refs[0]
    other_msgs = refs[1 : 1 + n_msgs]
    force_ref = refs[1 + n_msgs]
    (
        row_ref,
        other_piece_ref,
        source_piece_ref,
        own_piece_ref,
        own_source_ref,
        left_ref,
        source_ref,
        right_ref,
        back_ref,
        back_sum_ref,
    ) = refs[2 + n_msgs :]
    half = 0.5 * brick.bz

    rows = brick.ext_rows
    if rows > len(brick.columns):
        row_ref[...] = jnp.zeros(row_ref.shape, F32)
    for place, (x, y) in enumerate(brick.columns):
        shift = (x // brick.bx, y // brick.by)
        near = msg_ref if shift == (0, 0) else other_msgs[sender[shift]]
        col = brick.col(x % brick.bx, y % brick.by)
        for k in range(4):
            row_ref[k * rows + place : k * rows + place + 1, :] = near[
                k * brick.cols + col : k * brick.cols + col + 1, 0:lanes
            ]
    index = lax.broadcasted_iota(jnp.int32, (rows, 1), 0)
    ext_y = brick.by + 2
    offset_x = (index // ext_y - 1).astype(F32) - 0.5 * brick.bx
    offset_y = (index % ext_y - 1).astype(F32) - 0.5 * brick.by
    lane_z = (lax.broadcasted_iota(jnp.int32, (1, lanes), 1) // atoms).astype(F32)
    coords = [
        (row_ref[0:rows, :] + offset_x) * SCALE,
        (row_ref[rows : 2 * rows, :] + offset_y) * SCALE,
        (row_ref[2 * rows : 3 * rows, :] + (lane_z - half)) * SCALE,
    ]
    charge = row_ref[3 * rows : 4 * rows, :]
    store_pieces(
        other_piece_ref,
        rows,
        feature_arrays(coords, minus_square(coords), (0, 1, 2, 0, 1, 0), False),
    )
    store_pieces(source_piece_ref, rows, source_arrays(coords, charge))
    for place in range(len(brick.columns)):
        feature = load_pieces(other_piece_ref, rows, place, FEATURES)
        left_ref[place] = feature.T.astype(BF16)
        source = load_pieces(source_piece_ref, rows, place, SOURCES).astype(BF16)
        for z in range(brick.bz):
            part = source[:, z * atoms : (z + 1) * atoms]
            source_ref[place, z] = jnp.concatenate([part, part], axis=1)

    rows = brick.own_rows
    own = []
    for k in range(4):
        value = msg_ref[k * brick.cols : (k + 1) * brick.cols, 0:lanes]
        if rows > brick.cols:
            value = jnp.concatenate([value, jnp.zeros((rows - brick.cols, lanes), F32)], axis=0)
        own.append(value)
    index = lax.broadcasted_iota(jnp.int32, (rows, 1), 0)
    own_x = (own[0] + ((index // brick.by).astype(F32) - 0.5 * brick.bx)) * SCALE
    own_y = (own[1] + ((index % brick.by).astype(F32) - 0.5 * brick.by)) * SCALE
    own_z = []
    for other_z in range(brick.bz):
        step = other_z - lane_z
        step = jnp.where(step > half, step - brick.bz, step)
        step = jnp.where(step < -half, step + brick.bz, step)
        own_z.append((own[2] + (other_z - step - half)) * SCALE)
        coords = [own_x, own_y, own_z[-1]]
        arrays = feature_arrays(coords, minus_square(coords), (0, 0, 0, 1, 1, 2), True)
        arrays = [2.0 * value for value in arrays[:18]] + arrays[18:]
        store_pieces(own_piece_ref, rows, arrays)
        store_pieces(own_source_ref, rows, source_arrays(coords, own[3]))
        for col in range(brick.cols):
            part = load_pieces(own_piece_ref, rows, col, FEATURES)
            right_ref[col, other_z] = part.astype(BF16)
            part = load_pieces(own_source_ref, rows, col, SOURCES).astype(BF16)
            back_ref[col, other_z] = jnp.concatenate([part, part], axis=1)

    back_sum_ref[...] = jnp.zeros(back_sum_ref.shape, F32)
    for x in range(brick.bx):
        for y in range(brick.by):
            col = brick.col(x, y)
            here = brick.columns.index((x, y))
            forces = [0.0, 0.0, 0.0]
            for z in range(brick.bz):
                total = jnp.zeros((SOURCES, lanes), F32)
                right = right_ref[col, z]
                back = back_ref[col, z]
                for place, (ox, oy) in enumerate(brick.columns):
                    if max(abs(ox - x), abs(oy - y)) > 1:
                        continue
                    inside = 0 <= ox < brick.bx and 0 <= oy < brick.by
                    if inside and place < here:
                        continue
                    left = left_ref[place, z * atoms : (z + 1) * atoms, :]
                    if place != here:
                        high, low = pair_factor(left, right)
                        total = total + mul(
                            source_ref[place, z], jnp.concatenate([high, low], axis=0)
                        )
                        if inside:
                            back_sum_ref[brick.col(ox, oy), z] += mul_t(
                                back, jnp.concatenate([high, low], axis=1)
                            )
                        continue
                    after = (z + 1) % brick.bz
                    spans = [slice(cell * atoms, (cell + 1) * atoms) for cell in (z, after)]
                    both = jnp.concatenate([right[:, span] for span in spans], axis=1)
                    high, low = pair_factor(left, both)
                    part = mul(source_ref[place, z], jnp.concatenate([high, low], axis=0))
                    parts = [jnp.zeros((SOURCES, atoms), F32)] * brick.bz
                    parts[z] = part[:, :atoms]
                    parts[after] = part[:, atoms:]
                    total = total + jnp.concatenate(parts, axis=1)
                    back_sum_ref[col, z] += mul_t(
                        jnp.concatenate([back[:, spans[1]]] * 2, axis=1),
                        jnp.concatenate([high[:, atoms:], low[:, atoms:]], axis=1),
                    )
                weight = moments(total, 0)
                for comp, coord in enumerate((own_x, own_y, own_z[z])):
                    value = coord[col : col + 1] * weight - moments(total, 1 + comp)
                    forces[comp] = forces[comp] + value
            for comp in range(3):
                row = comp * brick.cols + col
                force_ref[row : row + 1, :] = forces[comp]
    for col in range(brick.cols):
        total = jnp.concatenate([back_sum_ref[col, z] for z in range(brick.bz)], axis=1)
        weight = moments(total, 0)
        home = (own[2] + (lane_z - half)) * SCALE
        for comp, coord in enumerate((own_x, own_y, home)):
            row = comp * brick.cols + col
            value = coord[col : col + 1] * weight - moments(total, 1 + comp)
            value = value + force_ref[row : row + 1, :]
            force_ref[row : row + 1, :] = value * (own[3][col : col + 1] * (SCALE * SCALE))


def fine_tables(brick):
    ext_x = brick.px + 2 * REACH
    rows_y = brick.py + POINTS * brick.by
    along_z = np.zeros((128, 128 * len(FINE_WIDTHS)), np.float32)
    along_xy = np.zeros((brick.px * brick.py, len(FINE_WIDTHS) * ext_x * rows_y), np.float32)

    def tap(dist, width):
        return np.where(np.abs(dist) <= REACH, np.exp(-(dist * dist) / (2.0 * width * width)), 0.0)

    for number, (width, weight) in enumerate(zip(FINE_WIDTHS, FINE_WEIGHTS)):
        for step in range(-REACH, REACH + 1):
            for z in range(brick.pz):
                along_z[(z + step) % brick.pz, 128 * number + z] += weight * tap(
                    np.float64(step), width
                )
        out_x = np.arange(brick.px) - 1.0
        in_x = np.arange(ext_x) - 1.0 - REACH
        out_y = np.arange(brick.py) - 1.0
        in_y = np.arange(rows_y) - 1.0 - POINTS * brick.by
        mat_x = tap(out_x[:, None] - in_x[None, :], width)
        mat_y = tap(out_y[:, None] - in_y[None, :], width)
        mat_y[POINTS * brick.by + 3 :] = 0.0
        size = ext_x * rows_y
        along_xy[:, number * size : (number + 1) * size] = np.kron(mat_x, mat_y)
    return along_xy, along_z


def coarse_table(brick):
    table = np.zeros((len(COARSE_WEIGHTS) * brick.coarse_lanes, 128), np.float32)
    length = brick.ck
    for number, (fraction, weight) in enumerate(zip(COARSE_FRACTIONS, COARSE_WEIGHTS)):
        width = length / fraction
        for row in range(brick.cj * brick.ck):
            for z in range(brick.pz):
                dist = (row - z // 2) % length
                dist = min(dist, length - dist)
                table[number * brick.coarse_lanes + row, z] = weight * math.exp(
                    -(dist * dist) / (2.0 * width * width)
                )
    return table


def gauss(row, col, length, fraction):
    dist = lax.rem(row - col + 2 * length, length)
    dist = jnp.minimum(dist, length - dist).astype(F32)
    width = length / fraction
    return jnp.exp(dist * dist * (-1.0 / (2.0 * width * width)))


def potential_kernel(brick, sender, n_msgs, *refs):
    atoms = brick.atoms
    place_ref, msg_ref = refs[0:2]
    other_msgs = refs[2 : 2 + n_msgs]
    (
        whole_ref,
        short_ref,
        xy_high_ref,
        xy_low_ref,
        z_ref,
        coarse_z_ref,
        out_ref,
        ext_ref,
        pot_ref,
    ) = refs[2 + n_msgs :]
    step_y = POINTS * brick.by
    rows_y = brick.py + step_y
    ext_x = brick.px + 2 * REACH
    planes = {}
    for dx in (-1, 0, 1):
        grids = []
        for dy in (-1, 0, 1):
            source = msg_ref if (dx, dy) == (0, 0) else other_msgs[sender[(dx, dy)]]
            grids.append(source[brick.grid_row :, 0 : brick.blocks * 128])
        full = brick.py + 2 * step_y
        tiles = [None] * (full // 8)
        for number, grid in enumerate(grids):
            for tile in range(brick.py // 8):
                spot = tile + number * step_y // 8
                value = grid[8 * tile : 8 * tile + 8]
                tiles[spot] = value if tiles[spot] is None else tiles[spot] + value
        column = jnp.concatenate(tiles[: rows_y // 8], axis=0)
        for x in range(brick.px):
            spot = x + POINTS * brick.bx * dx + REACH
            if 0 <= spot < ext_x:
                block, shift = divmod(x, brick.group)
                value = column[:, block * 128 : (block + 1) * 128]
                if shift:
                    value = pltpu.roll(value, 128 - shift * brick.zpad, 1)
                planes[spot] = planes[spot] + value if spot in planes else value
    for spot in range(ext_x):
        ext_ref[spot * rows_y : (spot + 1) * rows_y, :] = planes[spot]
    along = mul(ext_ref[...], z_ref[...], HIGHEST)
    along = jnp.concatenate([along[:, :128], along[:, 128:]], axis=0)
    high = along.astype(BF16)
    low = (along - high.astype(F32)).astype(BF16)
    potential = mul(xy_high_ref[...], high) + (
        mul(xy_high_ref[...], low) + mul(xy_low_ref[...], high)
    )

    total_x = 2 * brick.bx * brick.n_space
    total_y = 2 * brick.by * brick.n_sub
    first_x = place_ref[0] * (2 * brick.bx)
    first_y = place_ref[1] * (2 * brick.by)
    out_rows = round_up(brick.px, 8)
    shape = (out_rows, brick.n_space * brick.coarse_rows)
    point = lax.broadcasted_iota(jnp.int32, shape, 0)
    lane = lax.broadcasted_iota(jnp.int32, shape, 1)
    row_x = first_x + (point + 1) // 2 - 1
    col_x = lane // brick.coarse_rows * (2 * brick.bx) + lane % brick.coarse_rows - 1
    live = lane % brick.coarse_rows < brick.ci
    mats_x = jnp.concatenate(
        [
            jnp.where(live, gauss(row_x, col_x, total_x, fraction), 0.0)
            for fraction in COARSE_FRACTIONS
        ],
        axis=0,
    )
    shape = (brick.py, brick.coarse_lanes)
    point = lax.broadcasted_iota(jnp.int32, shape, 0)
    lane = lax.broadcasted_iota(jnp.int32, shape, 1)
    row_y = first_y + (point + 1) // 2 - 1
    live = lane < brick.cj * brick.ck
    lefts = [[None] * brick.px for _ in COARSE_FRACTIONS]
    for sub in range(brick.n_sub):
        part = whole_ref[:, sub].reshape(
            brick.n_space * brick.coarse_rows, brick.coarse_lanes
        )
        mixed = mul(mats_x, part, HIGHEST)
        col_y = sub * (2 * brick.by) + lane // brick.ck - 1
        for number, fraction in enumerate(COARSE_FRACTIONS):
            mat_y = jnp.where(live, gauss(row_y, col_y, total_y, fraction), 0.0)
            for x in range(brick.px):
                row = number * out_rows + x
                value = mixed[row : row + 1] * mat_y
                done = lefts[number][x]
                lefts[number][x] = value if done is None else done + value
    left = jnp.concatenate([jnp.concatenate(rows, axis=0) for rows in lefts], axis=1)
    potential = potential + mul(left, coarse_z_ref[...], HIGHEST)
    for x in range(brick.px):
        pot_ref[x] = potential[x * brick.py : (x + 1) * brick.py]

    for x in range(brick.bx):
        for y in range(brick.by):
            col = brick.col(x, y)
            rows = [
                msg_ref[k * brick.cols + col : k * brick.cols + col + 1, 0 : brick.lanes]
                for k in range(4)
            ]
            shifted = [
                shift_xy(brick, rows[0]),
                shift_xy(brick, rows[1]),
                shift_z(brick, rows[2]),
            ]
            weights = [spline(value) for value in shifted]
            slopes = [spline_slope(value) for value in shifted]
            box = jnp.concatenate(
                [
                    pot_ref[POINTS * x + e, POINTS * y : POINTS * y + 8, 0 : brick.zpad]
                    for e in range(TAPS)
                ],
                axis=0,
            )
            both = mul(box, jnp.concatenate([weights[2], slopes[2]], axis=1), HIGHEST)
            along_z = both[:, : brick.lanes]
            sloped_z = both[:, brick.lanes :]
            sums = [0.0, 0.0, 0.0]
            for e in range(TAPS):
                weight = weights[0][e : e + 1]
                slope = slopes[0][e : e + 1]
                flat = along_z[8 * e : 8 * e + 8]
                steep = sloped_z[8 * e : 8 * e + 8]
                sums[0] = sums[0] + flat * slope
                sums[1] = sums[1] + flat * weight
                sums[2] = sums[2] + steep * weight
            across = (weights[1], slopes[1], weights[1])
            for comp in range(3):
                force = jnp.sum(sums[comp] * across[comp], axis=0, keepdims=True)
                row = comp * brick.cols + col
                force = short_ref[row : row + 1, :] - POINTS * (rows[3] * force)
                for z in range(brick.bz):
                    out_ref[comp, x, y, z : z + 1, :] = force[:, z * atoms : (z + 1) * atoms]


VMEM = pl.BlockSpec(memory_space=pltpu.VMEM)
SMEM = pl.BlockSpec(memory_space=pltpu.SMEM)


def call(kernel, out_shape, in_specs, scratch, flops, *args):
    single = not isinstance(out_shape, (list, tuple))
    return pl.pallas_call(
        kernel,
        out_shape=out_shape,
        in_specs=in_specs,
        out_specs=VMEM if single else [VMEM] * len(out_shape),
        scratch_shapes=scratch,
        compiler_params=pltpu.CompilerParams(vmem_limit_bytes=40 * 1024 * 1024),
        cost_estimate=pl.CostEstimate(flops=flops, bytes_accessed=10**5, transcendentals=0),
    )(*args)


def neighbours(brick, msg):
    found = {}
    sender = {}
    msgs = []
    for dx in (-1, 0, 1):
        for dy in (-1, 0, 1):
            if (dx, dy) == (0, 0):
                continue
            key = (dx % brick.n_space, dy % brick.n_sub)
            if key not in found:
                found[key] = len(msgs)
                pairs = []
                for i in range(brick.n_space):
                    for j in range(brick.n_sub):
                        source = (i + dx) % brick.n_space * brick.n_sub + (j + dy) % brick.n_sub
                        pairs.append((source, i * brick.n_sub + j))
                msgs.append(lax.ppermute(msg, ("space", "sub"), pairs))
            sender[(dx, dy)] = found[key]
    return sender, msgs


def body(n_space, n_sub, positions, charges, counts):
    brick = Brick(charges.shape, n_space, n_sub)
    n_dev = n_space * n_sub
    along_xy, along_z = fine_tables(brick)
    xy_high = along_xy.astype(BF16)
    xy_low = (along_xy - xy_high.astype(np.float32)).astype(BF16)
    coarse_z = coarse_table(brick)
    place = jnp.stack([lax.axis_index("space"), lax.axis_index("sub")]).astype(jnp.int32)

    msg, coarse = call(
        functools.partial(spread_kernel, brick),
        [
            jax.ShapeDtypeStruct((brick.msg_rows, brick.msg_lanes), F32),
            jax.ShapeDtypeStruct((n_dev, brick.coarse_rows, brick.coarse_lanes), F32),
        ],
        [SMEM, VMEM, VMEM],
        [pltpu.VMEM((brick.px, brick.py, 128), F32)],
        10**7,
        counts,
        positions,
        charges,
    )
    sender, msgs = neighbours(brick, msg)
    whole = lax.all_to_all(coarse, ("space", "sub"), 0, 0, tiled=True)
    whole = whole.reshape(n_space, n_sub, brick.coarse_rows, brick.coarse_lanes)

    n_col = len(brick.columns)
    short = call(
        functools.partial(pairs_kernel, brick, sender, len(msgs)),
        jax.ShapeDtypeStruct((brick.force_rows, brick.lanes), F32),
        [VMEM] * (1 + len(msgs)),
        [
            pltpu.VMEM((4 * brick.ext_rows, brick.lanes), F32),
            pltpu.VMEM((brick.lanes // 128, FEATURES * brick.ext_rows, 128), F32),
            pltpu.VMEM((brick.lanes // 128, SOURCES * brick.ext_rows, 128), F32),
            pltpu.VMEM((brick.lanes // 128, FEATURES * brick.own_rows, 128), F32),
            pltpu.VMEM((brick.lanes // 128, SOURCES * brick.own_rows, 128), F32),
            pltpu.VMEM((n_col, brick.lanes, FEATURES), BF16),
            pltpu.VMEM((n_col, brick.bz, SOURCES, 2 * brick.atoms), BF16),
            pltpu.VMEM((brick.cols, brick.bz, FEATURES, brick.lanes), BF16),
            pltpu.VMEM((brick.cols, brick.bz, SOURCES, 2 * brick.lanes), BF16),
            pltpu.VMEM((brick.cols, brick.bz, SOURCES, brick.atoms), F32),
        ],
        10**10,
        msg,
        *msgs,
    )
    ext_x = brick.px + 2 * REACH
    rows_y = brick.py + POINTS * brick.by
    return call(
        functools.partial(potential_kernel, brick, sender, len(msgs)),
        jax.ShapeDtypeStruct(positions.shape, F32),
        [SMEM] + [VMEM] * (7 + len(msgs)),
        [
            pltpu.VMEM((ext_x * rows_y, 128), F32),
            pltpu.VMEM((brick.px, brick.py, 128), F32),
        ],
        10**8,
        place,
        msg,
        *msgs,
        whole,
        short,
        xy_high,
        xy_low,
        jnp.asarray(along_z),
        jnp.asarray(coarse_z),
    )


def solution(mesh):
    in_specs = (
        P(None, "space", "sub", None, None),
        P("space", "sub", None, None),
        P("space", "sub", None),
    )
    out_specs = P(None, "space", "sub", None, None)
    run = functools.partial(body, mesh.shape["space"], mesh.shape["sub"])
    return jax.shard_map(run, mesh=mesh, in_specs=in_specs, out_specs=out_specs, check_vma=False)
```

```python
import functools
import math

import jax
import jax.numpy as jnp
import numpy as np
from jax import lax
from jax.experimental import pallas as pl
from jax.experimental.pallas import tpu as pltpu
from jax.sharding import PartitionSpec as P

F32 = jnp.float32
BF16 = jnp.bfloat16
HIGHEST = lax.Precision.HIGHEST

POINTS = 4
REACH = 4
TAPS = POINTS + 3
SOFT_SQUARE = 0.0625
FINE_WIDTHS = (1.0, 2.0)
FINE_WEIGHTS = (2.0, 0.5)
COARSE_FRACTIONS = (8.0, 4.0)
COARSE_WEIGHTS = (4.0, 2.0)

DECAY = 0.114
SMOOTH = (
    0.004718840075751518,
    0.06055603768478568,
    0.019918877505712862,
    0.1440338177504446,
    0.014789349197372625,
    0.14113616660836056,
)
SCALE = math.sqrt(DECAY * math.log2(math.e))
LEAD = SMOOTH[-1] / SCALE**3
SHIFT = math.log2(LEAD) / (len(SMOOTH) - 1)
MONIC = tuple(
    coef / SCALE**3 / LEAD ** (power / (len(SMOOTH) - 1)) for power, coef in enumerate(SMOOTH)
)
HALF_CONST = 0.5 * (SHIFT - SCALE * SCALE * SOFT_SQUARE)

FEATURES = 32
SOURCES = 16


def round_up(value, step):
    return -(-value // step) * step


def mul_t(left, right, precision=None):
    return lax.dot_general(
        left, right, (((1,), (1,)), ((), ())), precision=precision, preferred_element_type=F32
    )


def mul(left, right, precision=None):
    return lax.dot_general(
        left, right, (((1,), (0,)), ((), ())), precision=precision, preferred_element_type=F32
    )


def split(value, count):
    pieces = []
    for _ in range(count - 1):
        piece = value.astype(BF16).astype(F32)
        pieces.append(piece)
        value = value - piece
    pieces.append(value.astype(BF16).astype(F32))
    return pieces


class Brick:
    def __init__(self, shape, n_space, n_sub):
        self.bx, self.by, self.bz, self.atoms = shape
        self.n_space, self.n_sub = n_space, n_sub
        self.cols = self.bx * self.by
        self.lanes = self.bz * self.atoms
        self.wide = (self.bz + 2) * self.atoms
        self.px = POINTS * self.bx + 3
        self.py = round_up(POINTS * (self.by - 1) + 8, 8)
        self.pz = POINTS * self.bz
        self.zpad = round_up(self.pz, 16)
        self.group = 128 // self.zpad
        self.atom_rows = 4 * self.cols
        self.blocks = -(-self.px // self.group)
        self.msg_rows = round_up(self.atom_rows, 8) + self.py
        self.msg_lanes = max(self.lanes, self.blocks * 128)
        self.grid_row = round_up(self.atom_rows, 8)
        self.ci = 2 * self.bx + 2
        self.cj = 2 * self.by + 2
        self.ck = 2 * self.bz
        self.coarse_rows = round_up(self.ci, 8)
        self.coarse_lanes = round_up(self.cj * self.ck, 128)
        self.own_rows = round_up(self.cols, 8)
        self.columns = [
            (x, y) for x in range(-1, self.bx + 1) for y in range(-1, self.by + 1)
        ]
        self.ext_rows = round_up(len(self.columns), 8)
        self.kept = 2 * self.atoms * (1 + self.bz * (self.cols - 1))
        self.force_rows = round_up(3 * self.cols, 8)

    def col(self, x, y):
        return x * self.by + y


def spline(shifted):
    size = jnp.abs(shifted)
    outer = jnp.maximum(2.0 - size, 0.0)
    inner = jnp.maximum(1.0 - size, 0.0)
    return (outer * outer * outer) * (1.0 / 6.0) - (inner * inner * inner) * (4.0 / 6.0)


def spline_slope(shifted):
    size = jnp.abs(shifted)
    outer = jnp.maximum(2.0 - size, 0.0)
    inner = jnp.maximum(1.0 - size, 0.0)
    slope = 2.0 * (inner * inner) - 0.5 * (outer * outer)
    return jnp.where(shifted < 0.0, -slope, slope)


def shift_xy(brick, row):
    entry = lax.broadcasted_iota(jnp.int32, (8, brick.lanes), 0).astype(F32)
    return POINTS * row - (entry - 1.0)


def shift_z(brick, row):
    parts = []
    for cell in range(brick.bz):
        point = lax.broadcasted_iota(jnp.int32, (brick.zpad, brick.atoms), 0)
        entry = lax.rem(point - POINTS * cell + 1 + brick.pz, brick.pz) - 1
        entry = jnp.where(point < brick.pz, entry, 100)
        value = row[:, cell * brick.atoms : (cell + 1) * brick.atoms]
        parts.append(POINTS * value - entry.astype(F32))
    return jnp.concatenate(parts, axis=1)


def spread_kernel(brick, counts_ref, pos_ref, charge_ref, msg_ref, coarse_ref, grid_ref):
    atoms = brick.atoms
    lane = lax.broadcasted_iota(jnp.int32, (1, atoms), 1)
    for x in range(brick.bx):
        for y in range(brick.by):
            col = brick.col(x, y)
            for z in range(brick.bz):
                span = slice(z * atoms, (z + 1) * atoms)
                for comp in range(3):
                    row = comp * brick.cols + col
                    msg_ref[row : row + 1, span] = pos_ref[comp, x, y, z : z + 1, :]
                row = 3 * brick.cols + col
                charge = charge_ref[x, y, z : z + 1, :]
                msg_ref[row : row + 1, span] = jnp.where(lane < counts_ref[x, y, z], charge, 0.0)
    grid_ref[...] = jnp.zeros(grid_ref.shape, F32)
    for x in range(brick.bx):
        for y in range(brick.by):
            col = brick.col(x, y)
            rows = [
                msg_ref[k * brick.cols + col : k * brick.cols + col + 1, 0 : brick.lanes]
                for k in range(4)
            ]
            along_x = spline(shift_xy(brick, rows[0])) * rows[3]
            along_y = spline(shift_xy(brick, rows[1]))
            along_z = spline(shift_z(brick, rows[2]))
            outer = jnp.concatenate(
                [along_x[e : e + 1, :] * along_y for e in range(TAPS)], axis=0
            )
            box = mul_t(outer, along_z, HIGHEST)
            for e in range(TAPS):
                place = (POINTS * x + e, slice(POINTS * y, POINTS * y + 8), slice(0, brick.zpad))
                grid_ref[place] = grid_ref[place] + box[8 * e : 8 * e + 8, :]
    for block in range(brick.msg_lanes // 128):
        total = jnp.zeros((brick.py, 128), F32)
        for spot in range(brick.group):
            x = block * brick.group + spot
            if x < brick.px:
                plane = grid_ref[x]
                total = total + (pltpu.roll(plane, spot * brick.zpad, 1) if spot else plane)
        msg_ref[brick.grid_row :, block * 128 : (block + 1) * 128] = total
    planes = []
    for idx in range(brick.ci):
        inside = [x for x in (2 * idx - 1, 2 * idx) if 0 <= x < brick.px]
        planes.append(sum(grid_ref[x, :, 0 : brick.zpad] for x in inside))
    stacked = jnp.concatenate(planes, axis=0)
    shape = (brick.zpad, brick.coarse_lanes)
    z_idx = lax.broadcasted_iota(jnp.int32, shape, 0)
    z_lane = lax.broadcasted_iota(jnp.int32, shape, 1)
    used = z_lane < brick.cj * brick.ck
    pairs = (z_idx // 2 == z_lane % brick.ck) & used & (z_idx < brick.pz)
    folded = mul(stacked, jnp.where(pairs, 0.125, 0.0).astype(F32), HIGHEST)
    shape = (brick.py, brick.coarse_lanes)
    y_idx = lax.broadcasted_iota(jnp.int32, shape, 0)
    y_lane = lax.broadcasted_iota(jnp.int32, shape, 1)
    mask = (y_lane // brick.ck == (y_idx + 1) // 2).astype(F32)
    sums = [
        jnp.sum(folded[i * brick.py : (i + 1) * brick.py] * mask, axis=0, keepdims=True)
        for i in range(brick.ci)
    ]
    if brick.coarse_rows > brick.ci:
        sums.append(jnp.zeros((brick.coarse_rows - brick.ci, brick.coarse_lanes), F32))
    coarse_ref[...] = jnp.broadcast_to(jnp.concatenate(sums, axis=0)[None], coarse_ref.shape)


def store_pieces(piece_ref, rows, arrays):
    for number, value in enumerate(arrays):
        for block in range(piece_ref.shape[0]):
            piece_ref[block, number * rows : (number + 1) * rows, :] = value[
                :, block * 128 : (block + 1) * 128
            ]


def load_pieces(piece_ref, rows, row, count):
    parts = [
        piece_ref[block, pl.ds(row, count, stride=rows), :] for block in range(piece_ref.shape[0])
    ]
    return jnp.concatenate(parts, axis=1)


def feature_arrays(coords, square, order, square_first):
    rows = coords[0].shape
    arrays = []
    for value in coords:
        pieces = split(value, 3)
        arrays += [pieces[piece] for piece in order]
    squares = split(square, 3)
    ones = [jnp.ones(rows, F32)] * 3
    arrays += squares + ones if square_first else ones + squares
    return arrays + [jnp.zeros(rows, F32)] * (FEATURES - len(arrays))


def source_arrays(coords, charge):
    arrays = []
    for value in [charge] + [charge * coord for coord in coords]:
        arrays += split(value, 3)
    return arrays + [jnp.zeros(charge.shape, F32)] * (SOURCES - len(arrays))


def minus_square(coords):
    return HALF_CONST - (coords[0] * coords[0] + coords[1] * coords[1] + coords[2] * coords[2])


def pair_factor(left, right):
    power = mul(left, right)
    inverse = lax.rsqrt(SHIFT - power)
    base = jnp.exp2(power)
    smooth = base + MONIC[4]
    for coef in MONIC[3::-1]:
        smooth = smooth * base + coef
    factor = inverse * (inverse * inverse) - smooth
    high = factor.astype(BF16)
    low = (factor - high.astype(F32)).astype(BF16)
    return high, low


def moments(total, quantity):
    base = 3 * quantity
    return total[base : base + 1] + total[base + 1 : base + 2] + total[base + 2 : base + 3]


def pairs_kernel(brick, sender, n_msgs, *refs):
    atoms, lanes = brick.atoms, brick.lanes
    msg_ref = refs[0]
    other_msgs = refs[1 : 1 + n_msgs]
    force_ref = refs[1 + n_msgs]
    (
        row_ref,
        other_piece_ref,
        source_piece_ref,
        own_piece_ref,
        own_source_ref,
        left_ref,
        source_ref,
        right_ref,
        back_ref,
        total_ref,
        kept_ref,
    ) = refs[2 + n_msgs :]
    half = 0.5 * brick.bz

    rows = brick.ext_rows
    if rows > len(brick.columns):
        row_ref[...] = jnp.zeros(row_ref.shape, F32)
    for place, (x, y) in enumerate(brick.columns):
        shift = (x // brick.bx, y // brick.by)
        near = msg_ref if shift == (0, 0) else other_msgs[sender[shift]]
        col = brick.col(x % brick.bx, y % brick.by)
        for k in range(4):
            row_ref[k * rows + place : k * rows + place + 1, :] = near[
                k * brick.cols + col : k * brick.cols + col + 1, 0:lanes
            ]
    index = lax.broadcasted_iota(jnp.int32, (rows, 1), 0)
    ext_y = brick.by + 2
    offset_x = (index // ext_y - 1).astype(F32) - 0.5 * brick.bx
    offset_y = (index % ext_y - 1).astype(F32) - 0.5 * brick.by
    lane_z = (lax.broadcasted_iota(jnp.int32, (1, lanes), 1) // atoms).astype(F32)
    coords = [
        (row_ref[0:rows, :] + offset_x) * SCALE,
        (row_ref[rows : 2 * rows, :] + offset_y) * SCALE,
        (row_ref[2 * rows : 3 * rows, :] + (lane_z - half)) * SCALE,
    ]
    charge = row_ref[3 * rows : 4 * rows, :]
    store_pieces(
        other_piece_ref,
        rows,
        feature_arrays(coords, minus_square(coords), (0, 1, 2, 0, 1, 0), False),
    )
    store_pieces(source_piece_ref, rows, source_arrays(coords, charge))
    for place in range(len(brick.columns)):
        feature = load_pieces(other_piece_ref, rows, place, FEATURES)
        left_ref[place] = feature.T.astype(BF16)
        source = load_pieces(source_piece_ref, rows, place, SOURCES).astype(BF16)
        for z in range(brick.bz):
            part = source[:, z * atoms : (z + 1) * atoms]
            source_ref[place, z] = jnp.concatenate([part, part], axis=1)

    rows = brick.own_rows
    own = []
    for k in range(4):
        value = msg_ref[k * brick.cols : (k + 1) * brick.cols, 0:lanes]
        if rows > brick.cols:
            value = jnp.concatenate([value, jnp.zeros((rows - brick.cols, lanes), F32)], axis=0)
        own.append(value)
    index = lax.broadcasted_iota(jnp.int32, (rows, 1), 0)
    own_x = (own[0] + ((index // brick.by).astype(F32) - 0.5 * brick.bx)) * SCALE
    own_y = (own[1] + ((index % brick.by).astype(F32) - 0.5 * brick.by)) * SCALE
    own_z_coords = []
    for other_z in range(brick.bz):
        step = other_z - lane_z
        step = jnp.where(step > half, step - brick.bz, step)
        step = jnp.where(step < -half, step + brick.bz, step)
        own_z_coords.append((own[2] + (other_z - step - half)) * SCALE)
        coords = [own_x, own_y, own_z_coords[-1]]
        arrays = feature_arrays(coords, minus_square(coords), (0, 0, 0, 1, 1, 2), True)
        arrays = [2.0 * value for value in arrays[:18]] + arrays[18:]
        store_pieces(own_piece_ref, rows, arrays)
        store_pieces(own_source_ref, rows, source_arrays(coords, own[3]))
        for col in range(brick.cols):
            part = load_pieces(own_piece_ref, rows, col, FEATURES)
            right_ref[col, other_z] = part.astype(BF16)
            part = load_pieces(own_source_ref, rows, col, SOURCES).astype(BF16)
            for z in range(brick.bz):
                cell = part[:, z * atoms : (z + 1) * atoms]
                back_ref[col, other_z, z] = jnp.concatenate([cell, cell], axis=1)

    total_ref[...] = jnp.zeros(total_ref.shape, F32)
    cells = [(x, y) for x in range(brick.bx) for y in range(brick.by)]
    mirrors = {(col, z): [] for col in range(brick.cols) for z in range(brick.bz)}

    def block(place, z, col, own_z, mirrored=None):
        span = slice(own_z * atoms, (own_z + 1) * atoms)
        left = left_ref[place, z * atoms : (z + 1) * atoms, :]
        high, low = pair_factor(left, right_ref[col, z, :, span])
        total_ref[col, z, :, span] += mul(
            source_ref[place, z], jnp.concatenate([high, low], axis=0)
        )
        if mirrored is not None:
            spot = 2 * atoms * len(mirrors[(mirrored, z)])
            mirrors[(mirrored, z)].append((col, own_z))
            kept_ref[mirrored, z, :, spot : spot + atoms] = high
            kept_ref[mirrored, z, :, spot + atoms : spot + 2 * atoms] = low

    def visit(place, x, y):
        inside = (x, y) in cells
        for z in range(brick.bz):
            for col, (cell_x, cell_y) in enumerate(cells):
                if max(abs(cell_x - x), abs(cell_y - y)) > 1:
                    continue
                if not inside:
                    for own_z in range(brick.bz):
                        block(place, z, col, own_z)
                elif col == brick.col(x, y):
                    block(place, z, col, z)
                    block(place, z, col, (z + 1) % brick.bz, col)
                elif col < brick.col(x, y):
                    for own_z in range(brick.bz):
                        block(place, z, col, own_z, brick.col(x, y))

    order = sorted(enumerate(brick.columns), key=lambda item: item[1] not in cells)
    for place, (x, y) in order:
        visit(place, x, y)
    back_sums = {}
    for (col, z), list_of in mirrors.items():
        back = jnp.concatenate([back_ref[c, z, own_z] for c, own_z in list_of], axis=1)
        back_sums[(col, z)] = mul_t(kept_ref[col, z, :, 0 : back.shape[1]], back).T

    for col in range(brick.cols):
        forces = [0.0, 0.0, 0.0]
        for z in range(brick.bz):
            total = total_ref[col, z]
            weight = moments(total, 0)
            for comp, coord in enumerate((own_x, own_y, own_z_coords[z])):
                value = coord[col : col + 1] * weight - moments(total, 1 + comp)
                forces[comp] = forces[comp] + value
        total = jnp.concatenate([back_sums[(col, z)] for z in range(brick.bz)], axis=1)
        weight = moments(total, 0)
        home = (own[2] + (lane_z - half)) * SCALE
        for comp, coord in enumerate((own_x, own_y, home)):
            row = comp * brick.cols + col
            value = coord[col : col + 1] * weight - moments(total, 1 + comp)
            value = value + forces[comp]
            force_ref[row : row + 1, :] = value * (own[3][col : col + 1] * (SCALE * SCALE))


def fine_tables(brick):
    ext_x = brick.px + 2 * REACH
    rows_y = brick.py + POINTS * brick.by
    along_z = np.zeros((128, 128 * len(FINE_WIDTHS)), np.float32)
    along_xy = np.zeros((brick.px * brick.py, len(FINE_WIDTHS) * ext_x * rows_y), np.float32)

    def tap(dist, width):
        return np.where(np.abs(dist) <= REACH, np.exp(-(dist * dist) / (2.0 * width * width)), 0.0)

    for number, (width, weight) in enumerate(zip(FINE_WIDTHS, FINE_WEIGHTS)):
        for step in range(-REACH, REACH + 1):
            for z in range(brick.pz):
                along_z[(z + step) % brick.pz, 128 * number + z] += weight * tap(
                    np.float64(step), width
                )
        out_x = np.arange(brick.px) - 1.0
        in_x = np.arange(ext_x) - 1.0 - REACH
        out_y = np.arange(brick.py) - 1.0
        in_y = np.arange(rows_y) - 1.0 - POINTS * brick.by
        mat_x = tap(out_x[:, None] - in_x[None, :], width)
        mat_y = tap(out_y[:, None] - in_y[None, :], width)
        mat_y[POINTS * brick.by + 3 :] = 0.0
        size = ext_x * rows_y
        along_xy[:, number * size : (number + 1) * size] = np.kron(mat_x, mat_y)
    return along_xy, along_z


def coarse_table(brick):
    table = np.zeros((len(COARSE_WEIGHTS) * brick.coarse_lanes, 128), np.float32)
    length = brick.ck
    for number, (fraction, weight) in enumerate(zip(COARSE_FRACTIONS, COARSE_WEIGHTS)):
        width = length / fraction
        for row in range(brick.cj * brick.ck):
            for z in range(brick.pz):
                dist = (row - z // 2) % length
                dist = min(dist, length - dist)
                table[number * brick.coarse_lanes + row, z] = weight * math.exp(
                    -(dist * dist) / (2.0 * width * width)
                )
    return table


def gauss(row, col, length, fraction):
    dist = lax.rem(row - col + 2 * length, length)
    dist = jnp.minimum(dist, length - dist).astype(F32)
    width = length / fraction
    return jnp.exp(dist * dist * (-1.0 / (2.0 * width * width)))


def potential_kernel(brick, sender, n_msgs, *refs):
    atoms = brick.atoms
    place_ref, msg_ref = refs[0:2]
    other_msgs = refs[2 : 2 + n_msgs]
    (
        whole_ref,
        short_ref,
        xy_high_ref,
        xy_low_ref,
        z_ref,
        coarse_z_ref,
        out_ref,
        ext_ref,
        pot_ref,
    ) = refs[2 + n_msgs :]
    step_y = POINTS * brick.by
    rows_y = brick.py + step_y
    ext_x = brick.px + 2 * REACH
    planes = {}
    for dx in (-1, 0, 1):
        grids = []
        for dy in (-1, 0, 1):
            source = msg_ref if (dx, dy) == (0, 0) else other_msgs[sender[(dx, dy)]]
            grids.append(source[brick.grid_row :, 0 : brick.blocks * 128])
        full = brick.py + 2 * step_y
        tiles = [None] * (full // 8)
        for number, grid in enumerate(grids):
            for tile in range(brick.py // 8):
                spot = tile + number * step_y // 8
                value = grid[8 * tile : 8 * tile + 8]
                tiles[spot] = value if tiles[spot] is None else tiles[spot] + value
        column = jnp.concatenate(tiles[: rows_y // 8], axis=0)
        for x in range(brick.px):
            spot = x + POINTS * brick.bx * dx + REACH
            if 0 <= spot < ext_x:
                block, shift = divmod(x, brick.group)
                value = column[:, block * 128 : (block + 1) * 128]
                if shift:
                    value = pltpu.roll(value, 128 - shift * brick.zpad, 1)
                planes[spot] = planes[spot] + value if spot in planes else value
    for spot in range(ext_x):
        ext_ref[spot * rows_y : (spot + 1) * rows_y, :] = planes[spot]
    along = mul(ext_ref[...], z_ref[...], HIGHEST)
    along = jnp.concatenate([along[:, :128], along[:, 128:]], axis=0)
    high = along.astype(BF16)
    low = (along - high.astype(F32)).astype(BF16)
    potential = mul(xy_high_ref[...], high) + (
        mul(xy_high_ref[...], low) + mul(xy_low_ref[...], high)
    )

    total_x = 2 * brick.bx * brick.n_space
    total_y = 2 * brick.by * brick.n_sub
    first_x = place_ref[0] * (2 * brick.bx)
    first_y = place_ref[1] * (2 * brick.by)
    out_rows = round_up(brick.px, 8)
    shape = (out_rows, brick.n_space * brick.coarse_rows)
    point = lax.broadcasted_iota(jnp.int32, shape, 0)
    lane = lax.broadcasted_iota(jnp.int32, shape, 1)
    row_x = first_x + (point + 1) // 2 - 1
    col_x = lane // brick.coarse_rows * (2 * brick.bx) + lane % brick.coarse_rows - 1
    live = lane % brick.coarse_rows < brick.ci
    mats_x = jnp.concatenate(
        [
            jnp.where(live, gauss(row_x, col_x, total_x, fraction), 0.0)
            for fraction in COARSE_FRACTIONS
        ],
        axis=0,
    )
    shape = (brick.py, brick.coarse_lanes)
    point = lax.broadcasted_iota(jnp.int32, shape, 0)
    lane = lax.broadcasted_iota(jnp.int32, shape, 1)
    row_y = first_y + (point + 1) // 2 - 1
    live = lane < brick.cj * brick.ck
    lefts = [[None] * brick.px for _ in COARSE_FRACTIONS]
    for sub in range(brick.n_sub):
        part = whole_ref[:, sub].reshape(
            brick.n_space * brick.coarse_rows, brick.coarse_lanes
        )
        mixed = mul(mats_x, part, HIGHEST)
        col_y = sub * (2 * brick.by) + lane // brick.ck - 1
        for number, fraction in enumerate(COARSE_FRACTIONS):
            mat_y = jnp.where(live, gauss(row_y, col_y, total_y, fraction), 0.0)
            for x in range(brick.px):
                row = number * out_rows + x
                value = mixed[row : row + 1] * mat_y
                done = lefts[number][x]
                lefts[number][x] = value if done is None else done + value
    left = jnp.concatenate([jnp.concatenate(rows, axis=0) for rows in lefts], axis=1)
    potential = potential + mul(left, coarse_z_ref[...], HIGHEST)
    for x in range(brick.px):
        pot_ref[x] = potential[x * brick.py : (x + 1) * brick.py]

    for x in range(brick.bx):
        for y in range(brick.by):
            col = brick.col(x, y)
            rows = [
                msg_ref[k * brick.cols + col : k * brick.cols + col + 1, 0 : brick.lanes]
                for k in range(4)
            ]
            shifted = [
                shift_xy(brick, rows[0]),
                shift_xy(brick, rows[1]),
                shift_z(brick, rows[2]),
            ]
            weights = [spline(value) for value in shifted]
            slopes = [spline_slope(value) for value in shifted]
            box = jnp.concatenate(
                [
                    pot_ref[POINTS * x + e, POINTS * y : POINTS * y + 8, 0 : brick.zpad]
                    for e in range(TAPS)
                ],
                axis=0,
            )
            both = mul(box, jnp.concatenate([weights[2], slopes[2]], axis=1), HIGHEST)
            along_z = both[:, : brick.lanes]
            sloped_z = both[:, brick.lanes :]
            sums = [0.0, 0.0, 0.0]
            for e in range(TAPS):
                weight = weights[0][e : e + 1]
                slope = slopes[0][e : e + 1]
                flat = along_z[8 * e : 8 * e + 8]
                steep = sloped_z[8 * e : 8 * e + 8]
                sums[0] = sums[0] + flat * slope
                sums[1] = sums[1] + flat * weight
                sums[2] = sums[2] + steep * weight
            across = (weights[1], slopes[1], weights[1])
            for comp in range(3):
                force = jnp.sum(sums[comp] * across[comp], axis=0, keepdims=True)
                row = comp * brick.cols + col
                force = short_ref[row : row + 1, :] - POINTS * (rows[3] * force)
                for z in range(brick.bz):
                    out_ref[comp, x, y, z : z + 1, :] = force[:, z * atoms : (z + 1) * atoms]


VMEM = pl.BlockSpec(memory_space=pltpu.VMEM)
SMEM = pl.BlockSpec(memory_space=pltpu.SMEM)


def call(kernel, out_shape, in_specs, scratch, flops, *args):
    single = not isinstance(out_shape, (list, tuple))
    return pl.pallas_call(
        kernel,
        out_shape=out_shape,
        in_specs=in_specs,
        out_specs=VMEM if single else [VMEM] * len(out_shape),
        scratch_shapes=scratch,
        compiler_params=pltpu.CompilerParams(vmem_limit_bytes=40 * 1024 * 1024),
        cost_estimate=pl.CostEstimate(flops=flops, bytes_accessed=10**5, transcendentals=0),
    )(*args)


def neighbours(brick, msg):
    found = {}
    sender = {}
    msgs = []
    for dx in (-1, 0, 1):
        for dy in (-1, 0, 1):
            if (dx, dy) == (0, 0):
                continue
            key = (dx % brick.n_space, dy % brick.n_sub)
            if key not in found:
                found[key] = len(msgs)
                pairs = []
                for i in range(brick.n_space):
                    for j in range(brick.n_sub):
                        source = (i + dx) % brick.n_space * brick.n_sub + (j + dy) % brick.n_sub
                        pairs.append((source, i * brick.n_sub + j))
                msgs.append(lax.ppermute(msg, ("space", "sub"), pairs))
            sender[(dx, dy)] = found[key]
    return sender, msgs


def body(n_space, n_sub, positions, charges, counts):
    brick = Brick(charges.shape, n_space, n_sub)
    n_dev = n_space * n_sub
    along_xy, along_z = fine_tables(brick)
    xy_high = along_xy.astype(BF16)
    xy_low = (along_xy - xy_high.astype(np.float32)).astype(BF16)
    coarse_z = coarse_table(brick)
    place = jnp.stack([lax.axis_index("space"), lax.axis_index("sub")]).astype(jnp.int32)

    msg, coarse = call(
        functools.partial(spread_kernel, brick),
        [
            jax.ShapeDtypeStruct((brick.msg_rows, brick.msg_lanes), F32),
            jax.ShapeDtypeStruct((n_dev, brick.coarse_rows, brick.coarse_lanes), F32),
        ],
        [SMEM, VMEM, VMEM],
        [pltpu.VMEM((brick.px, brick.py, 128), F32)],
        10**7,
        counts,
        positions,
        charges,
    )
    sender, msgs = neighbours(brick, msg)
    whole = lax.all_to_all(coarse, ("space", "sub"), 0, 0, tiled=True)
    whole = whole.reshape(n_space, n_sub, brick.coarse_rows, brick.coarse_lanes)

    n_col = len(brick.columns)
    short = call(
        functools.partial(pairs_kernel, brick, sender, len(msgs)),
        jax.ShapeDtypeStruct((brick.force_rows, brick.lanes), F32),
        [VMEM] * (1 + len(msgs)),
        [
            pltpu.VMEM((4 * brick.ext_rows, brick.lanes), F32),
            pltpu.VMEM((brick.lanes // 128, FEATURES * brick.ext_rows, 128), F32),
            pltpu.VMEM((brick.lanes // 128, SOURCES * brick.ext_rows, 128), F32),
            pltpu.VMEM((brick.lanes // 128, FEATURES * brick.own_rows, 128), F32),
            pltpu.VMEM((brick.lanes // 128, SOURCES * brick.own_rows, 128), F32),
            pltpu.VMEM((n_col, brick.lanes, FEATURES), BF16),
            pltpu.VMEM((n_col, brick.bz, SOURCES, 2 * brick.atoms), BF16),
            pltpu.VMEM((brick.cols, brick.bz, FEATURES, brick.lanes), BF16),
            pltpu.VMEM((brick.cols, brick.bz, brick.bz, SOURCES, 2 * brick.atoms), BF16),
            pltpu.VMEM((brick.cols, brick.bz, SOURCES, brick.lanes), F32),
            pltpu.VMEM((brick.cols, brick.bz, brick.atoms, brick.kept), BF16),
        ],
        10**10,
        msg,
        *msgs,
    )
    ext_x = brick.px + 2 * REACH
    rows_y = brick.py + POINTS * brick.by
    return call(
        functools.partial(potential_kernel, brick, sender, len(msgs)),
        jax.ShapeDtypeStruct(positions.shape, F32),
        [SMEM] + [VMEM] * (7 + len(msgs)),
        [
            pltpu.VMEM((ext_x * rows_y, 128), F32),
            pltpu.VMEM((brick.px, brick.py, 128), F32),
        ],
        10**8,
        place,
        msg,
        *msgs,
        whole,
        short,
        xy_high,
        xy_low,
        jnp.asarray(along_z),
        jnp.asarray(coarse_z),
    )


def solution(mesh):
    in_specs = (
        P(None, "space", "sub", None, None),
        P("space", "sub", None, None),
        P("space", "sub", None),
    )
    out_specs = P(None, "space", "sub", None, None)
    run = functools.partial(body, mesh.shape["space"], mesh.shape["sub"])
    return jax.shard_map(run, mesh=mesh, in_specs=in_specs, out_specs=out_specs, check_vma=False)
```

```python
import functools
import math

import jax
import jax.numpy as jnp
import numpy as np
from jax import lax
from jax.experimental import pallas as pl
from jax.experimental.pallas import tpu as pltpu
from jax.sharding import PartitionSpec as P

F32 = jnp.float32
BF16 = jnp.bfloat16
HIGHEST = lax.Precision.HIGHEST

POINTS = 4
REACH = 4
TAPS = POINTS + 3
SOFT_SQUARE = 0.0625
FINE_WIDTHS = (1.0, 2.0)
FINE_WEIGHTS = (2.0, 0.5)
COARSE_FRACTIONS = (8.0, 4.0)
COARSE_WEIGHTS = (4.0, 2.0)

DECAY = 0.11446730730706552
LEAD = 0.13637726630426547
SMOOTH = (1.0312317180277653, 0.44426879021665455, 0.1544174241571791, -0.004580112368867706)
SCALE = math.sqrt(DECAY * math.log2(math.e))
STRETCH = (LEAD / SCALE**3) ** 0.2
SHIFT = math.log2(STRETCH)
QUARTIC = (SMOOTH[0] * STRETCH**2, SMOOTH[1] * STRETCH**4, SMOOTH[2] * STRETCH)
LEVEL = SMOOTH[3] / SCALE**3
HALF_CONST = 0.5 * (SHIFT - SCALE * SCALE * SOFT_SQUARE)

FEATURES = 32
SOURCES = 16


def round_up(value, step):
    return -(-value // step) * step


def mul_t(left, right, precision=None):
    return lax.dot_general(
        left, right, (((1,), (1,)), ((), ())), precision=precision, preferred_element_type=F32
    )


def mul(left, right, precision=None):
    return lax.dot_general(
        left, right, (((1,), (0,)), ((), ())), precision=precision, preferred_element_type=F32
    )


def split(value, count):
    pieces = []
    for _ in range(count - 1):
        piece = value.astype(BF16).astype(F32)
        pieces.append(piece)
        value = value - piece
    pieces.append(value.astype(BF16).astype(F32))
    return pieces


class Brick:
    def __init__(self, shape, n_space, n_sub):
        self.bx, self.by, self.bz, self.atoms = shape
        self.n_space, self.n_sub = n_space, n_sub
        self.cols = self.bx * self.by
        self.lanes = self.bz * self.atoms
        self.wide = (self.bz + 2) * self.atoms
        self.px = POINTS * self.bx + 3
        self.py = round_up(POINTS * (self.by - 1) + 8, 8)
        self.pz = POINTS * self.bz
        self.zpad = round_up(self.pz, 16)
        self.group = 128 // self.zpad
        self.atom_rows = 4 * self.cols
        self.blocks = -(-self.px // self.group)
        self.msg_rows = round_up(self.atom_rows, 8) + self.py
        self.msg_lanes = max(self.lanes, self.blocks * 128)
        self.grid_row = round_up(self.atom_rows, 8)
        self.ci = 2 * self.bx + 2
        self.cj = 2 * self.by + 2
        self.ck = 2 * self.bz
        self.coarse_rows = round_up(self.ci, 8)
        self.coarse_lanes = round_up(self.cj * self.ck, 128)
        self.own_rows = round_up(self.cols, 8)
        self.columns = [
            (x, y) for x in range(-1, self.bx + 1) for y in range(-1, self.by + 1)
        ]
        self.ext_rows = round_up(len(self.columns), 8)
        self.kept = 2 * self.atoms * (1 + self.bz * (self.cols - 1))
        self.force_rows = round_up(3 * self.cols, 8)

    def col(self, x, y):
        return x * self.by + y


def spline(shifted):
    size = jnp.abs(shifted)
    outer = jnp.maximum(2.0 - size, 0.0)
    inner = jnp.maximum(1.0 - size, 0.0)
    return (outer * outer * outer) * (1.0 / 6.0) - (inner * inner * inner) * (4.0 / 6.0)


def spline_slope(shifted):
    size = jnp.abs(shifted)
    outer = jnp.maximum(2.0 - size, 0.0)
    inner = jnp.maximum(1.0 - size, 0.0)
    slope = 2.0 * (inner * inner) - 0.5 * (outer * outer)
    return jnp.where(shifted < 0.0, -slope, slope)


def shift_xy(brick, row):
    entry = lax.broadcasted_iota(jnp.int32, (8, brick.lanes), 0).astype(F32)
    return POINTS * row - (entry - 1.0)


def shift_z(brick, row):
    parts = []
    for cell in range(brick.bz):
        point = lax.broadcasted_iota(jnp.int32, (brick.zpad, brick.atoms), 0)
        entry = lax.rem(point - POINTS * cell + 1 + brick.pz, brick.pz) - 1
        entry = jnp.where(point < brick.pz, entry, 100)
        value = row[:, cell * brick.atoms : (cell + 1) * brick.atoms]
        parts.append(POINTS * value - entry.astype(F32))
    return jnp.concatenate(parts, axis=1)


def spread_kernel(brick, *refs):
    inputs, (msg_ref, coarse_ref), held = refs[0:3], refs[3:5], refs[5:8]
    grid_ref, arrived = refs[8:]
    counts_ref, pos_ref, charge_ref = held
    copies = [
        pltpu.make_async_copy(source, target, arrived.at[number])
        for number, (source, target) in enumerate(zip(inputs, held))
    ]
    for copy in copies:
        copy.start()
    grid_ref[...] = jnp.zeros(grid_ref.shape, F32)
    for copy in copies:
        copy.wait()
    atoms = brick.atoms
    lane = lax.broadcasted_iota(jnp.int32, (1, atoms), 1)
    for x in range(brick.bx):
        for y in range(brick.by):
            col = brick.col(x, y)
            for z in range(brick.bz):
                span = slice(z * atoms, (z + 1) * atoms)
                for comp in range(3):
                    row = comp * brick.cols + col
                    msg_ref[row : row + 1, span] = pos_ref[comp, x, z, y : y + 1, :]
                row = 3 * brick.cols + col
                charge = charge_ref[x, z, y : y + 1, :]
                msg_ref[row : row + 1, span] = jnp.where(lane < counts_ref[x, y, z], charge, 0.0)
    for x in range(brick.bx):
        for y in range(brick.by):
            col = brick.col(x, y)
            rows = [
                msg_ref[k * brick.cols + col : k * brick.cols + col + 1, 0 : brick.lanes]
                for k in range(4)
            ]
            along_x = spline(shift_xy(brick, rows[0])) * rows[3]
            along_y = spline(shift_xy(brick, rows[1]))
            along_z = spline(shift_z(brick, rows[2]))
            outer = jnp.concatenate(
                [along_x[e : e + 1, :] * along_y for e in range(TAPS)], axis=0
            )
            box = mul_t(outer, along_z, HIGHEST)
            for e in range(TAPS):
                place = (POINTS * x + e, slice(POINTS * y, POINTS * y + 8), slice(0, brick.zpad))
                grid_ref[place] = grid_ref[place] + box[8 * e : 8 * e + 8, :]
    for block in range(brick.msg_lanes // 128):
        total = jnp.zeros((brick.py, 128), F32)
        for spot in range(brick.group):
            x = block * brick.group + spot
            if x < brick.px:
                plane = grid_ref[x]
                total = total + (pltpu.roll(plane, spot * brick.zpad, 1) if spot else plane)
        msg_ref[brick.grid_row :, block * 128 : (block + 1) * 128] = total
    planes = []
    for idx in range(brick.ci):
        inside = [x for x in (2 * idx - 1, 2 * idx) if 0 <= x < brick.px]
        planes.append(sum(grid_ref[x, :, 0 : brick.zpad] for x in inside))
    stacked = jnp.concatenate(planes, axis=0)
    shape = (brick.zpad, brick.coarse_lanes)
    z_idx = lax.broadcasted_iota(jnp.int32, shape, 0)
    z_lane = lax.broadcasted_iota(jnp.int32, shape, 1)
    used = z_lane < brick.cj * brick.ck
    pairs = (z_idx // 2 == z_lane % brick.ck) & used & (z_idx < brick.pz)
    folded = mul(stacked, jnp.where(pairs, 0.125, 0.0).astype(F32), HIGHEST)
    shape = (brick.py, brick.coarse_lanes)
    y_idx = lax.broadcasted_iota(jnp.int32, shape, 0)
    y_lane = lax.broadcasted_iota(jnp.int32, shape, 1)
    mask = (y_lane // brick.ck == (y_idx + 1) // 2).astype(F32)
    sums = [
        jnp.sum(folded[i * brick.py : (i + 1) * brick.py] * mask, axis=0, keepdims=True)
        for i in range(brick.ci)
    ]
    if brick.coarse_rows > brick.ci:
        sums.append(jnp.zeros((brick.coarse_rows - brick.ci, brick.coarse_lanes), F32))
    coarse_ref[...] = jnp.broadcast_to(jnp.concatenate(sums, axis=0)[None], coarse_ref.shape)


def store_pieces(piece_ref, rows, arrays):
    for number, value in enumerate(arrays):
        for block in range(piece_ref.shape[0]):
            piece_ref[block, number * rows : (number + 1) * rows, :] = value[
                :, block * 128 : (block + 1) * 128
            ]


def load_pieces(piece_ref, rows, row, count):
    parts = [
        piece_ref[block, pl.ds(row, count, stride=rows), :] for block in range(piece_ref.shape[0])
    ]
    return jnp.concatenate(parts, axis=1)


def feature_arrays(coords, square, order, square_first):
    rows = coords[0].shape
    arrays = []
    for value in coords:
        pieces = split(value, 3)
        arrays += [pieces[piece] for piece in order]
    squares = split(square, 3)
    ones = [jnp.ones(rows, F32)] * 3
    arrays += squares + ones if square_first else ones + squares
    return arrays + [jnp.zeros(rows, F32)] * (FEATURES - len(arrays))


def source_arrays(coords, charge):
    arrays = []
    for value in [charge] + [charge * coord for coord in coords]:
        arrays += split(value, 3)
    return arrays + [jnp.zeros(charge.shape, F32)] * (SOURCES - len(arrays))


def minus_square(coords):
    return HALF_CONST - (coords[0] * coords[0] + coords[1] * coords[1] + coords[2] * coords[2])


def pair_factor(left, right):
    power = mul(left, right)
    inverse = lax.rsqrt(SHIFT - power)
    base = jnp.exp2(power)
    square = base * base
    smooth = ((square + QUARTIC[0]) * square + QUARTIC[1]) * (base + QUARTIC[2])
    factor = inverse * (inverse * inverse) - smooth
    high = factor.astype(BF16)
    low = (factor - high.astype(F32)).astype(BF16)
    return high, low


def moments(total, quantity):
    base = 3 * quantity
    return total[base : base + 1] + total[base + 1 : base + 2] + total[base + 2 : base + 3]


def pairs_kernel(brick, sender, n_msgs, *refs):
    atoms, lanes = brick.atoms, brick.lanes
    msg_ref = refs[0]
    other_msgs = refs[1 : 1 + n_msgs]
    force_ref = refs[1 + n_msgs]
    (
        row_ref,
        other_piece_ref,
        source_piece_ref,
        own_piece_ref,
        own_source_ref,
        left_ref,
        source_ref,
        right_ref,
        back_ref,
        total_ref,
        kept_ref,
    ) = refs[2 + n_msgs :]
    half = 0.5 * brick.bz

    rows = brick.ext_rows
    if rows > len(brick.columns):
        row_ref[...] = jnp.zeros(row_ref.shape, F32)
    for place, (x, y) in enumerate(brick.columns):
        shift = (x // brick.bx, y // brick.by)
        near = msg_ref if shift == (0, 0) else other_msgs[sender[shift]]
        col = brick.col(x % brick.bx, y % brick.by)
        for k in range(4):
            row_ref[k * rows + place : k * rows + place + 1, :] = near[
                k * brick.cols + col : k * brick.cols + col + 1, 0:lanes
            ]
    index = lax.broadcasted_iota(jnp.int32, (rows, 1), 0)
    ext_y = brick.by + 2
    offset_x = (index // ext_y - 1).astype(F32) - 0.5 * brick.bx
    offset_y = (index % ext_y - 1).astype(F32) - 0.5 * brick.by
    lane_z = (lax.broadcasted_iota(jnp.int32, (1, lanes), 1) // atoms).astype(F32)
    coords = [
        (row_ref[0:rows, :] + offset_x) * SCALE,
        (row_ref[rows : 2 * rows, :] + offset_y) * SCALE,
        (row_ref[2 * rows : 3 * rows, :] + (lane_z - half)) * SCALE,
    ]
    charge = row_ref[3 * rows : 4 * rows, :]
    store_pieces(
        other_piece_ref,
        rows,
        feature_arrays(coords, minus_square(coords), (0, 1, 2, 0, 1, 0), False),
    )
    store_pieces(source_piece_ref, rows, source_arrays(coords, charge))
    level_sums = {}
    for place in range(len(brick.columns)):
        feature = load_pieces(other_piece_ref, rows, place, FEATURES)
        left_ref[place] = feature.T.astype(BF16)
        source = load_pieces(source_piece_ref, rows, place, SOURCES)
        for z in range(brick.bz):
            part = source[:, z * atoms : (z + 1) * atoms]
            level_sums[(place, z)] = -LEVEL * jnp.sum(part, axis=1, keepdims=True)
            part = part.astype(BF16)
            source_ref[place, z] = jnp.concatenate([part, part], axis=1)

    rows = brick.own_rows
    own = []
    for k in range(4):
        value = msg_ref[k * brick.cols : (k + 1) * brick.cols, 0:lanes]
        if rows > brick.cols:
            value = jnp.concatenate([value, jnp.zeros((rows - brick.cols, lanes), F32)], axis=0)
        own.append(value)
    index = lax.broadcasted_iota(jnp.int32, (rows, 1), 0)
    own_x = (own[0] + ((index // brick.by).astype(F32) - 0.5 * brick.bx)) * SCALE
    own_y = (own[1] + ((index % brick.by).astype(F32) - 0.5 * brick.by)) * SCALE
    own_z_coords = []
    for other_z in range(brick.bz):
        step = other_z - lane_z
        step = jnp.where(step > half, step - brick.bz, step)
        step = jnp.where(step < -half, step + brick.bz, step)
        own_z_coords.append((own[2] + (other_z - step - half)) * SCALE)
        coords = [own_x, own_y, own_z_coords[-1]]
        arrays = feature_arrays(coords, minus_square(coords), (0, 0, 0, 1, 1, 2), True)
        arrays = [2.0 * value for value in arrays[:18]] + arrays[18:]
        store_pieces(own_piece_ref, rows, arrays)
        store_pieces(own_source_ref, rows, source_arrays(coords, own[3]))
        for col in range(brick.cols):
            part = load_pieces(own_piece_ref, rows, col, FEATURES)
            right_ref[col, other_z] = part.astype(BF16)
            part = load_pieces(own_source_ref, rows, col, SOURCES).astype(BF16)
            for z in range(brick.bz):
                cell = part[:, z * atoms : (z + 1) * atoms]
                back_ref[col, other_z, z] = jnp.concatenate([cell, cell], axis=1)

    cells = [(x, y) for x in range(brick.bx) for y in range(brick.by)]
    tiles = []
    for place, (x, y) in sorted(enumerate(brick.columns), key=lambda item: item[1] not in cells):
        home = cells.index((x, y)) if (x, y) in cells else None
        for z in range(brick.bz):
            for col, (cell_x, cell_y) in enumerate(cells):
                if max(abs(cell_x - x), abs(cell_y - y)) > 1 or (home is not None and col > home):
                    continue
                if col == home:
                    tiles.append((place, z, col, z, None))
                    tiles.append((place, z, col, (z + 1) % brick.bz, home))
                else:
                    tiles += [(place, z, col, own_z, home) for own_z in range(brick.bz)]

    for col in range(brick.cols):
        for z in range(brick.bz):
            for own_z in range(brick.bz):
                level = sum(
                    level_sums[(tile[0], z)] for tile in tiles if tile[1:4] == (z, col, own_z)
                )
                span = slice(own_z * atoms, (own_z + 1) * atoms)
                total_ref[col, z, :, span] = jnp.broadcast_to(level, (SOURCES, atoms))

    mirrors = {(col, z): [] for col in range(brick.cols) for z in range(brick.bz)}
    for place, z, col, own_z, home in tiles:
        span = slice(own_z * atoms, (own_z + 1) * atoms)
        left = left_ref[place, z * atoms : (z + 1) * atoms, :]
        high, low = pair_factor(left, right_ref[col, z, :, span])
        total_ref[col, z, :, span] += mul(
            source_ref[place, z], jnp.concatenate([high, low], axis=0)
        )
        if home is not None:
            spot = 2 * atoms * len(mirrors[(home, z)])
            mirrors[(home, z)].append((col, own_z))
            kept_ref[home, z, :, spot : spot + atoms] = high
            kept_ref[home, z, :, spot + atoms : spot + 2 * atoms] = low
    back_sums = {}
    for (col, z), found in mirrors.items():
        back = jnp.concatenate([back_ref[c, z, own_z] for c, own_z in found], axis=1)
        level = (-0.5 * LEVEL) * jnp.sum(back.astype(F32), axis=1, keepdims=True)
        back_sums[(col, z)] = mul_t(kept_ref[col, z, :, 0 : back.shape[1]], back).T + level

    for col in range(brick.cols):
        forces = [0.0, 0.0, 0.0]
        for z in range(brick.bz):
            total = total_ref[col, z]
            weight = moments(total, 0)
            for comp, coord in enumerate((own_x, own_y, own_z_coords[z])):
                value = coord[col : col + 1] * weight - moments(total, 1 + comp)
                forces[comp] = forces[comp] + value
        total = jnp.concatenate([back_sums[(col, z)] for z in range(brick.bz)], axis=1)
        weight = moments(total, 0)
        home = (own[2] + (lane_z - half)) * SCALE
        for comp, coord in enumerate((own_x, own_y, home)):
            row = comp * brick.cols + col
            value = coord[col : col + 1] * weight - moments(total, 1 + comp)
            value = value + forces[comp]
            force_ref[row : row + 1, :] = value * (own[3][col : col + 1] * (SCALE * SCALE))


def fine_tables(brick):
    ext_x = brick.px + 2 * REACH
    rows_y = brick.py + POINTS * brick.by
    along_z = np.zeros((128, 128 * len(FINE_WIDTHS)), np.float32)
    along_xy = np.zeros((brick.px * brick.py, len(FINE_WIDTHS) * ext_x * rows_y), np.float32)

    def tap(dist, width):
        return np.where(np.abs(dist) <= REACH, np.exp(-(dist * dist) / (2.0 * width * width)), 0.0)

    for number, (width, weight) in enumerate(zip(FINE_WIDTHS, FINE_WEIGHTS)):
        for step in range(-REACH, REACH + 1):
            for z in range(brick.pz):
                along_z[(z + step) % brick.pz, 128 * number + z] += weight * tap(
                    np.float64(step), width
                )
        out_x = np.arange(brick.px) - 1.0
        in_x = np.arange(ext_x) - 1.0 - REACH
        out_y = np.arange(brick.py) - 1.0
        in_y = np.arange(rows_y) - 1.0 - POINTS * brick.by
        mat_x = tap(out_x[:, None] - in_x[None, :], width)
        mat_y = tap(out_y[:, None] - in_y[None, :], width)
        mat_y[POINTS * brick.by + 3 :] = 0.0
        size = ext_x * rows_y
        along_xy[:, number * size : (number + 1) * size] = np.kron(mat_x, mat_y)
    return along_xy, along_z


def coarse_table(brick):
    table = np.zeros((len(COARSE_WEIGHTS) * brick.coarse_lanes, 128), np.float32)
    length = brick.ck
    for number, (fraction, weight) in enumerate(zip(COARSE_FRACTIONS, COARSE_WEIGHTS)):
        width = length / fraction
        for row in range(brick.cj * brick.ck):
            for z in range(brick.pz):
                dist = (row - z // 2) % length
                dist = min(dist, length - dist)
                table[number * brick.coarse_lanes + row, z] = weight * math.exp(
                    -(dist * dist) / (2.0 * width * width)
                )
    return table


def gauss(row, col, length, fraction):
    dist = lax.rem(row - col + 2 * length, length)
    dist = jnp.minimum(dist, length - dist).astype(F32)
    width = length / fraction
    return jnp.exp(dist * dist * (-1.0 / (2.0 * width * width)))


def potential_kernel(brick, sender, n_msgs, *refs):
    atoms = brick.atoms
    place_ref, msg_ref = refs[0:2]
    other_msgs = refs[2 : 2 + n_msgs]
    (
        whole_ref,
        short_ref,
        xy_high_ref,
        xy_low_ref,
        z_ref,
        coarse_z_ref,
        out_ref,
        ext_ref,
        pot_ref,
    ) = refs[2 + n_msgs :]
    step_y = POINTS * brick.by
    rows_y = brick.py + step_y
    ext_x = brick.px + 2 * REACH
    planes = {}
    for dx in (-1, 0, 1):
        grids = []
        for dy in (-1, 0, 1):
            source = msg_ref if (dx, dy) == (0, 0) else other_msgs[sender[(dx, dy)]]
            grids.append(source[brick.grid_row :, 0 : brick.blocks * 128])
        full = brick.py + 2 * step_y
        tiles = [None] * (full // 8)
        for number, grid in enumerate(grids):
            for tile in range(brick.py // 8):
                spot = tile + number * step_y // 8
                value = grid[8 * tile : 8 * tile + 8]
                tiles[spot] = value if tiles[spot] is None else tiles[spot] + value
        column = jnp.concatenate(tiles[: rows_y // 8], axis=0)
        for x in range(brick.px):
            spot = x + POINTS * brick.bx * dx + REACH
            if 0 <= spot < ext_x:
                block, shift = divmod(x, brick.group)
                value = column[:, block * 128 : (block + 1) * 128]
                if shift:
                    value = pltpu.roll(value, 128 - shift * brick.zpad, 1)
                planes[spot] = planes[spot] + value if spot in planes else value
    for spot in range(ext_x):
        ext_ref[spot * rows_y : (spot + 1) * rows_y, :] = planes[spot]
    along = mul(ext_ref[...], z_ref[...], HIGHEST)
    along = jnp.concatenate([along[:, :128], along[:, 128:]], axis=0)
    high = along.astype(BF16)
    low = (along - high.astype(F32)).astype(BF16)
    potential = mul(xy_high_ref[...], high) + (
        mul(xy_high_ref[...], low) + mul(xy_low_ref[...], high)
    )

    total_x = 2 * brick.bx * brick.n_space
    total_y = 2 * brick.by * brick.n_sub
    first_x = place_ref[0] * (2 * brick.bx)
    first_y = place_ref[1] * (2 * brick.by)
    out_rows = round_up(brick.px, 8)
    shape = (out_rows, brick.n_space * brick.coarse_rows)
    point = lax.broadcasted_iota(jnp.int32, shape, 0)
    lane = lax.broadcasted_iota(jnp.int32, shape, 1)
    row_x = first_x + (point + 1) // 2 - 1
    col_x = lane // brick.coarse_rows * (2 * brick.bx) + lane % brick.coarse_rows - 1
    live = lane % brick.coarse_rows < brick.ci
    mats_x = jnp.concatenate(
        [
            jnp.where(live, gauss(row_x, col_x, total_x, fraction), 0.0)
            for fraction in COARSE_FRACTIONS
        ],
        axis=0,
    )
    shape = (brick.py, brick.coarse_lanes)
    point = lax.broadcasted_iota(jnp.int32, shape, 0)
    lane = lax.broadcasted_iota(jnp.int32, shape, 1)
    row_y = first_y + (point + 1) // 2 - 1
    live = lane < brick.cj * brick.ck
    lefts = [[None] * brick.px for _ in COARSE_FRACTIONS]
    for sub in range(brick.n_sub):
        part = whole_ref[:, sub].reshape(
            brick.n_space * brick.coarse_rows, brick.coarse_lanes
        )
        mixed = mul(mats_x, part, HIGHEST)
        col_y = sub * (2 * brick.by) + lane // brick.ck - 1
        for number, fraction in enumerate(COARSE_FRACTIONS):
            mat_y = jnp.where(live, gauss(row_y, col_y, total_y, fraction), 0.0)
            for x in range(brick.px):
                row = number * out_rows + x
                value = mixed[row : row + 1] * mat_y
                done = lefts[number][x]
                lefts[number][x] = value if done is None else done + value
    left = jnp.concatenate([jnp.concatenate(rows, axis=0) for rows in lefts], axis=1)
    potential = potential + mul(left, coarse_z_ref[...], HIGHEST)
    for x in range(brick.px):
        pot_ref[x] = potential[x * brick.py : (x + 1) * brick.py]

    for x in range(brick.bx):
        for y in range(brick.by):
            col = brick.col(x, y)
            rows = [
                msg_ref[k * brick.cols + col : k * brick.cols + col + 1, 0 : brick.lanes]
                for k in range(4)
            ]
            shifted = [
                shift_xy(brick, rows[0]),
                shift_xy(brick, rows[1]),
                shift_z(brick, rows[2]),
            ]
            weights = [spline(value) for value in shifted]
            slopes = [spline_slope(value) for value in shifted]
            box = jnp.concatenate(
                [
                    pot_ref[POINTS * x + e, POINTS * y : POINTS * y + 8, 0 : brick.zpad]
                    for e in range(TAPS)
                ],
                axis=0,
            )
            both = mul(box, jnp.concatenate([weights[2], slopes[2]], axis=1), HIGHEST)
            along_z = both[:, : brick.lanes]
            sloped_z = both[:, brick.lanes :]
            sums = [0.0, 0.0, 0.0]
            for e in range(TAPS):
                weight = weights[0][e : e + 1]
                slope = slopes[0][e : e + 1]
                flat = along_z[8 * e : 8 * e + 8]
                steep = sloped_z[8 * e : 8 * e + 8]
                sums[0] = sums[0] + flat * slope
                sums[1] = sums[1] + flat * weight
                sums[2] = sums[2] + steep * weight
            across = (weights[1], slopes[1], weights[1])
            for comp in range(3):
                force = jnp.sum(sums[comp] * across[comp], axis=0, keepdims=True)
                row = comp * brick.cols + col
                force = short_ref[row : row + 1, :] - POINTS * (rows[3] * force)
                for z in range(brick.bz):
                    out_ref[comp, x, z, y : y + 1, :] = force[:, z * atoms : (z + 1) * atoms]


VMEM = pl.BlockSpec(memory_space=pltpu.VMEM)
SMEM = pl.BlockSpec(memory_space=pltpu.SMEM)
ANY = pl.BlockSpec(memory_space=pl.ANY)
WHOLE = pl.BlockSpec()


def call(kernel, out_shape, in_specs, scratch, flops, *args, out_spec=VMEM):
    single = not isinstance(out_shape, (list, tuple))
    return pl.pallas_call(
        kernel,
        out_shape=out_shape,
        in_specs=in_specs,
        out_specs=out_spec if single else [out_spec] * len(out_shape),
        scratch_shapes=scratch,
        compiler_params=pltpu.CompilerParams(vmem_limit_bytes=40 * 1024 * 1024),
        cost_estimate=pl.CostEstimate(flops=flops, bytes_accessed=10**5, transcendentals=0),
    )(*args)


def neighbours(brick, msg):
    found = {}
    sender = {}
    msgs = []
    for dx in (-1, 0, 1):
        for dy in (-1, 0, 1):
            if (dx, dy) == (0, 0):
                continue
            key = (dx % brick.n_space, dy % brick.n_sub)
            if key not in found:
                found[key] = len(msgs)
                pairs = []
                for i in range(brick.n_space):
                    for j in range(brick.n_sub):
                        source = (i + dx) % brick.n_space * brick.n_sub + (j + dy) % brick.n_sub
                        pairs.append((source, i * brick.n_sub + j))
                msgs.append(lax.ppermute(msg, ("space", "sub"), pairs))
            sender[(dx, dy)] = found[key]
    return sender, msgs


def body(n_space, n_sub, positions, charges, counts):
    brick = Brick(charges.shape, n_space, n_sub)
    n_dev = n_space * n_sub
    along_xy, along_z = fine_tables(brick)
    xy_high = along_xy.astype(BF16)
    xy_low = (along_xy - xy_high.astype(np.float32)).astype(BF16)
    coarse_z = coarse_table(brick)
    place = jnp.stack([lax.axis_index("space"), lax.axis_index("sub")]).astype(jnp.int32)

    turned = (positions.transpose(0, 1, 3, 2, 4), charges.transpose(0, 2, 1, 3))
    msg, coarse = call(
        functools.partial(spread_kernel, brick),
        [
            jax.ShapeDtypeStruct((brick.msg_rows, brick.msg_lanes), F32),
            jax.ShapeDtypeStruct((n_dev, brick.coarse_rows, brick.coarse_lanes), F32),
        ],
        [ANY, ANY, ANY],
        [
            pltpu.SMEM(counts.shape, jnp.int32),
            pltpu.VMEM(turned[0].shape, F32),
            pltpu.VMEM(turned[1].shape, F32),
            pltpu.VMEM((brick.px, brick.py, 128), F32),
            pltpu.SemaphoreType.DMA((3,)),
        ],
        10**7,
        counts,
        *turned,
    )
    sender, msgs = neighbours(brick, msg)
    whole = lax.all_to_all(coarse, ("space", "sub"), 0, 0, tiled=True)
    whole = whole.reshape(n_space, n_sub, brick.coarse_rows, brick.coarse_lanes)

    n_col = len(brick.columns)
    short = call(
        functools.partial(pairs_kernel, brick, sender, len(msgs)),
        jax.ShapeDtypeStruct((brick.force_rows, brick.lanes), F32),
        [VMEM] * (1 + len(msgs)),
        [
            pltpu.VMEM((4 * brick.ext_rows, brick.lanes), F32),
            pltpu.VMEM((brick.lanes // 128, FEATURES * brick.ext_rows, 128), F32),
            pltpu.VMEM((brick.lanes // 128, SOURCES * brick.ext_rows, 128), F32),
            pltpu.VMEM((brick.lanes // 128, FEATURES * brick.own_rows, 128), F32),
            pltpu.VMEM((brick.lanes // 128, SOURCES * brick.own_rows, 128), F32),
            pltpu.VMEM((n_col, brick.lanes, FEATURES), BF16),
            pltpu.VMEM((n_col, brick.bz, SOURCES, 2 * brick.atoms), BF16),
            pltpu.VMEM((brick.cols, brick.bz, FEATURES, brick.lanes), BF16),
            pltpu.VMEM((brick.cols, brick.bz, brick.bz, SOURCES, 2 * brick.atoms), BF16),
            pltpu.VMEM((brick.cols, brick.bz, SOURCES, brick.lanes), F32),
            pltpu.VMEM((brick.cols, brick.bz, brick.atoms, brick.kept), BF16),
        ],
        10**10,
        msg,
        *msgs,
    )
    ext_x = brick.px + 2 * REACH
    rows_y = brick.py + POINTS * brick.by
    comps, size_x, size_y, size_z, atoms = positions.shape
    forces = call(
        functools.partial(potential_kernel, brick, sender, len(msgs)),
        jax.ShapeDtypeStruct((comps, size_x, size_z, size_y, atoms), F32),
        [SMEM] + [VMEM] * (7 + len(msgs)),
        [
            pltpu.VMEM((ext_x * rows_y, 128), F32),
            pltpu.VMEM((brick.px, brick.py, 128), F32),
        ],
        10**8,
        place,
        msg,
        *msgs,
        whole,
        short,
        xy_high,
        xy_low,
        jnp.asarray(along_z),
        jnp.asarray(coarse_z),
        out_spec=WHOLE,
    )
    return forces.transpose(0, 1, 3, 2, 4)


def solution(mesh):
    in_specs = (
        P(None, "space", "sub", None, None),
        P("space", "sub", None, None),
        P("space", "sub", None),
    )
    out_specs = P(None, "space", "sub", None, None)
    run = functools.partial(body, mesh.shape["space"], mesh.shape["sub"])
    return jax.shard_map(run, mesh=mesh, in_specs=in_specs, out_specs=out_specs, check_vma=False)
```

```python
import functools
import math

import jax
import jax.numpy as jnp
import numpy as np
from jax import lax
from jax.experimental import pallas as pl
from jax.experimental.pallas import tpu as pltpu
from jax.sharding import PartitionSpec as P

F32 = jnp.float32
BF16 = jnp.bfloat16
HIGHEST = lax.Precision.HIGHEST

POINTS = 4
REACH = 4
TAPS = POINTS + 3
SOFT_SQUARE = 0.0625
FINE_WIDTHS = (1.0, 2.0)
FINE_WEIGHTS = (2.0, 0.5)
COARSE_FRACTIONS = (8.0, 4.0)
COARSE_WEIGHTS = (4.0, 2.0)

DECAY = 0.11446730730706552
LEAD = 0.13637726630426547
SMOOTH = (1.0312317180277653, 0.44426879021665455, 0.1544174241571791, -0.004580112368867706)
SCALE = math.sqrt(DECAY * math.log2(math.e))
STRETCH = (LEAD / SCALE**3) ** 0.2
SHIFT = math.log2(STRETCH)
QUARTIC = (SMOOTH[0] * STRETCH**2, SMOOTH[1] * STRETCH**4, SMOOTH[2] * STRETCH)
LEVEL = SMOOTH[3] / SCALE**3
HALF_CONST = 0.5 * (SHIFT - SCALE * SCALE * SOFT_SQUARE)

FEATURES = 32
SOURCES = 16


def round_up(value, step):
    return -(-value // step) * step


def mul_t(left, right, precision=None):
    return lax.dot_general(
        left, right, (((1,), (1,)), ((), ())), precision=precision, preferred_element_type=F32
    )


def mul(left, right, precision=None):
    return lax.dot_general(
        left, right, (((1,), (0,)), ((), ())), precision=precision, preferred_element_type=F32
    )


def split(value, count):
    pieces = []
    for _ in range(count - 1):
        piece = value.astype(BF16).astype(F32)
        pieces.append(piece)
        value = value - piece
    pieces.append(value.astype(BF16).astype(F32))
    return pieces


class Brick:
    def __init__(self, shape, n_space, n_sub):
        self.bx, self.by, self.bz, self.atoms = shape
        self.n_space, self.n_sub = n_space, n_sub
        self.cols = self.bx * self.by
        self.lanes = self.bz * self.atoms
        self.wide = (self.bz + 2) * self.atoms
        self.px = POINTS * self.bx + 3
        self.py = round_up(POINTS * (self.by - 1) + 8, 8)
        self.pz = POINTS * self.bz
        self.zpad = round_up(self.pz, 16)
        self.group = 128 // self.zpad
        self.atom_rows = 4 * self.cols
        self.blocks = -(-self.px // self.group)
        self.msg_rows = round_up(self.atom_rows, 8) + self.py
        self.msg_lanes = max(self.lanes, self.blocks * 128)
        self.grid_row = round_up(self.atom_rows, 8)
        self.ci = 2 * self.bx + 2
        self.cj = 2 * self.by + 2
        self.ck = 2 * self.bz
        self.coarse_rows = round_up(self.ci, 8)
        self.coarse_lanes = round_up(self.cj * self.ck, 128)
        self.own_rows = round_up(self.cols, 8)
        self.columns = [
            (x, y) for x in range(-1, self.bx + 1) for y in range(-1, self.by + 1)
        ]
        self.ext_rows = round_up(len(self.columns), 8)
        self.kept = 2 * self.atoms * (1 + self.bz * (self.cols - 1))
        self.force_rows = round_up(3 * self.cols, 8)

    def col(self, x, y):
        return x * self.by + y


def spline(shifted):
    size = jnp.abs(shifted)
    outer = jnp.maximum(2.0 - size, 0.0)
    inner = jnp.maximum(1.0 - size, 0.0)
    return (outer * outer * outer) * (1.0 / 6.0) - (inner * inner * inner) * (4.0 / 6.0)


def spline_slope(shifted):
    size = jnp.abs(shifted)
    outer = jnp.maximum(2.0 - size, 0.0)
    inner = jnp.maximum(1.0 - size, 0.0)
    slope = 2.0 * (inner * inner) - 0.5 * (outer * outer)
    return jnp.where(shifted < 0.0, -slope, slope)


def shift_xy(brick, row):
    entry = lax.broadcasted_iota(jnp.int32, (8, brick.lanes), 0).astype(F32)
    return POINTS * row - (entry - 1.0)


def shift_z(brick, row):
    parts = []
    for cell in range(brick.bz):
        point = lax.broadcasted_iota(jnp.int32, (brick.zpad, brick.atoms), 0)
        entry = lax.rem(point - POINTS * cell + 1 + brick.pz, brick.pz) - 1
        entry = jnp.where(point < brick.pz, entry, 100)
        value = row[:, cell * brick.atoms : (cell + 1) * brick.atoms]
        parts.append(POINTS * value - entry.astype(F32))
    return jnp.concatenate(parts, axis=1)


def spread_kernel(brick, *refs):
    inputs, (msg_ref, coarse_ref), held = refs[0:3], refs[3:5], refs[5:8]
    grid_ref, arrived = refs[8:]
    counts_ref, pos_ref, charge_ref = held
    copies = [
        pltpu.make_async_copy(source, target, arrived.at[number])
        for number, (source, target) in enumerate(zip(inputs, held))
    ]
    for copy in copies:
        copy.start()
    grid_ref[...] = jnp.zeros(grid_ref.shape, F32)
    for copy in copies:
        copy.wait()
    atoms = brick.atoms
    lane = lax.broadcasted_iota(jnp.int32, (1, atoms), 1)
    for x in range(brick.bx):
        for y in range(brick.by):
            col = brick.col(x, y)
            for z in range(brick.bz):
                span = slice(z * atoms, (z + 1) * atoms)
                for comp in range(3):
                    row = comp * brick.cols + col
                    msg_ref[row : row + 1, span] = pos_ref[comp, x, z, y : y + 1, :]
                row = 3 * brick.cols + col
                charge = charge_ref[x, z, y : y + 1, :]
                msg_ref[row : row + 1, span] = jnp.where(lane < counts_ref[x, y, z], charge, 0.0)
    for x in range(brick.bx):
        for y in range(brick.by):
            col = brick.col(x, y)
            rows = [
                msg_ref[k * brick.cols + col : k * brick.cols + col + 1, 0 : brick.lanes]
                for k in range(4)
            ]
            along_x = spline(shift_xy(brick, rows[0])) * rows[3]
            along_y = spline(shift_xy(brick, rows[1]))
            along_z = spline(shift_z(brick, rows[2]))
            outer = jnp.concatenate(
                [along_x[e : e + 1, :] * along_y for e in range(TAPS)], axis=0
            )
            box = mul_t(outer, along_z, HIGHEST)
            for e in range(TAPS):
                place = (POINTS * x + e, slice(POINTS * y, POINTS * y + 8), slice(0, brick.zpad))
                grid_ref[place] = grid_ref[place] + box[8 * e : 8 * e + 8, :]
    for block in range(brick.msg_lanes // 128):
        total = jnp.zeros((brick.py, 128), F32)
        for spot in range(brick.group):
            x = block * brick.group + spot
            if x < brick.px:
                plane = grid_ref[x]
                total = total + (pltpu.roll(plane, spot * brick.zpad, 1) if spot else plane)
        msg_ref[brick.grid_row :, block * 128 : (block + 1) * 128] = total
    planes = []
    for idx in range(brick.ci):
        inside = [x for x in (2 * idx - 1, 2 * idx) if 0 <= x < brick.px]
        planes.append(sum(grid_ref[x, :, 0 : brick.zpad] for x in inside))
    stacked = jnp.concatenate(planes, axis=0)
    shape = (brick.zpad, brick.coarse_lanes)
    z_idx = lax.broadcasted_iota(jnp.int32, shape, 0)
    z_lane = lax.broadcasted_iota(jnp.int32, shape, 1)
    used = z_lane < brick.cj * brick.ck
    pairs = (z_idx // 2 == z_lane % brick.ck) & used & (z_idx < brick.pz)
    folded = mul(stacked, jnp.where(pairs, 0.125, 0.0).astype(F32), HIGHEST)
    shape = (brick.py, brick.coarse_lanes)
    y_idx = lax.broadcasted_iota(jnp.int32, shape, 0)
    y_lane = lax.broadcasted_iota(jnp.int32, shape, 1)
    mask = (y_lane // brick.ck == (y_idx + 1) // 2).astype(F32)
    sums = [
        jnp.sum(folded[i * brick.py : (i + 1) * brick.py] * mask, axis=0, keepdims=True)
        for i in range(brick.ci)
    ]
    if brick.coarse_rows > brick.ci:
        sums.append(jnp.zeros((brick.coarse_rows - brick.ci, brick.coarse_lanes), F32))
    coarse_ref[...] = jnp.broadcast_to(jnp.concatenate(sums, axis=0)[None], coarse_ref.shape)


def store_pieces(piece_ref, rows, arrays):
    for number, value in enumerate(arrays):
        for block in range(piece_ref.shape[0]):
            piece_ref[block, number * rows : (number + 1) * rows, :] = value[
                :, block * 128 : (block + 1) * 128
            ]


def load_pieces(piece_ref, rows, row, count):
    parts = [
        piece_ref[block, pl.ds(row, count, stride=rows), :] for block in range(piece_ref.shape[0])
    ]
    return jnp.concatenate(parts, axis=1)


def feature_arrays(coords, square, order, square_first):
    rows = coords[0].shape
    arrays = []
    for value in coords:
        pieces = split(value, 3)
        arrays += [pieces[piece] for piece in order]
    squares = split(square, 3)
    ones = [jnp.ones(rows, F32)] * 3
    arrays += squares + ones if square_first else ones + squares
    return arrays + [jnp.zeros(rows, F32)] * (FEATURES - len(arrays))


def source_arrays(coords, charge):
    arrays = []
    for value in [charge] + [charge * coord for coord in coords]:
        arrays += split(value, 3)
    return arrays + [jnp.zeros(charge.shape, F32)] * (SOURCES - len(arrays))


def minus_square(coords):
    return HALF_CONST - (coords[0] * coords[0] + coords[1] * coords[1] + coords[2] * coords[2])


def pair_factor(left, right):
    power = mul(left, right)
    inverse = lax.rsqrt(SHIFT - power)
    base = jnp.exp2(power)
    square = base * base
    smooth = ((square + QUARTIC[0]) * square + QUARTIC[1]) * (base + QUARTIC[2])
    factor = inverse * (inverse * inverse) - smooth
    high = factor.astype(BF16)
    low = (factor - high.astype(F32)).astype(BF16)
    return high, low


def moments(total, quantity):
    base = 3 * quantity
    return total[base : base + 1] + total[base + 1 : base + 2] + total[base + 2 : base + 3]


def pairs_kernel(brick, sender, n_msgs, *refs):
    atoms, lanes = brick.atoms, brick.lanes
    place_ref, msg_ref = refs[0:2]
    other_msgs = refs[2 : 2 + n_msgs]
    force_ref = refs[2 + n_msgs]
    (
        row_ref,
        other_piece_ref,
        source_piece_ref,
        own_piece_ref,
        own_source_ref,
        left_ref,
        source_ref,
        right_ref,
        back_ref,
        total_ref,
        kept_ref,
    ) = refs[3 + n_msgs :]
    even = place_ref[0] % 2 == 0
    half = 0.5 * brick.bz

    rows = brick.ext_rows
    if rows > len(brick.columns):
        row_ref[...] = jnp.zeros(row_ref.shape, F32)
    for place, (x, y) in enumerate(brick.columns):
        shift = (x // brick.bx, y // brick.by)
        col = brick.col(x % brick.bx, y % brick.by)
        for k in range(4):
            near = slice(k * brick.cols + col, k * brick.cols + col + 1)
            if shift == (0, 0):
                value = msg_ref[near, 0:lanes]
            else:
                value = near_rows(other_msgs, sender[shift], even, near, slice(0, lanes))
            row_ref[k * rows + place : k * rows + place + 1, :] = value
    index = lax.broadcasted_iota(jnp.int32, (rows, 1), 0)
    ext_y = brick.by + 2
    offset_x = (index // ext_y - 1).astype(F32) - 0.5 * brick.bx
    offset_y = (index % ext_y - 1).astype(F32) - 0.5 * brick.by
    lane_z = (lax.broadcasted_iota(jnp.int32, (1, lanes), 1) // atoms).astype(F32)
    coords = [
        (row_ref[0:rows, :] + offset_x) * SCALE,
        (row_ref[rows : 2 * rows, :] + offset_y) * SCALE,
        (row_ref[2 * rows : 3 * rows, :] + (lane_z - half)) * SCALE,
    ]
    charge = row_ref[3 * rows : 4 * rows, :]
    store_pieces(
        other_piece_ref,
        rows,
        feature_arrays(coords, minus_square(coords), (0, 1, 2, 0, 1, 0), False),
    )
    store_pieces(source_piece_ref, rows, source_arrays(coords, charge))
    level_sums = {}
    for place in range(len(brick.columns)):
        feature = load_pieces(other_piece_ref, rows, place, FEATURES)
        left_ref[place] = feature.T.astype(BF16)
        source = load_pieces(source_piece_ref, rows, place, SOURCES)
        for z in range(brick.bz):
            part = source[:, z * atoms : (z + 1) * atoms]
            level_sums[(place, z)] = -LEVEL * jnp.sum(part, axis=1, keepdims=True)
            part = part.astype(BF16)
            source_ref[place, z] = jnp.concatenate([part, part], axis=1)

    rows = brick.own_rows
    own = []
    for k in range(4):
        value = msg_ref[k * brick.cols : (k + 1) * brick.cols, 0:lanes]
        if rows > brick.cols:
            value = jnp.concatenate([value, jnp.zeros((rows - brick.cols, lanes), F32)], axis=0)
        own.append(value)
    index = lax.broadcasted_iota(jnp.int32, (rows, 1), 0)
    own_x = (own[0] + ((index // brick.by).astype(F32) - 0.5 * brick.bx)) * SCALE
    own_y = (own[1] + ((index % brick.by).astype(F32) - 0.5 * brick.by)) * SCALE
    own_z_coords = []
    for other_z in range(brick.bz):
        step = other_z - lane_z
        step = jnp.where(step > half, step - brick.bz, step)
        step = jnp.where(step < -half, step + brick.bz, step)
        own_z_coords.append((own[2] + (other_z - step - half)) * SCALE)
        coords = [own_x, own_y, own_z_coords[-1]]
        arrays = feature_arrays(coords, minus_square(coords), (0, 0, 0, 1, 1, 2), True)
        arrays = [2.0 * value for value in arrays[:18]] + arrays[18:]
        store_pieces(own_piece_ref, rows, arrays)
        store_pieces(own_source_ref, rows, source_arrays(coords, own[3]))
        for col in range(brick.cols):
            part = load_pieces(own_piece_ref, rows, col, FEATURES)
            right_ref[col, other_z] = part.astype(BF16)
            part = load_pieces(own_source_ref, rows, col, SOURCES).astype(BF16)
            for z in range(brick.bz):
                cell = part[:, z * atoms : (z + 1) * atoms]
                back_ref[col, other_z, z] = jnp.concatenate([cell, cell], axis=1)

    cells = [(x, y) for x in range(brick.bx) for y in range(brick.by)]
    tiles = []
    for place, (x, y) in sorted(enumerate(brick.columns), key=lambda item: item[1] not in cells):
        home = cells.index((x, y)) if (x, y) in cells else None
        for z in range(brick.bz):
            for col, (cell_x, cell_y) in enumerate(cells):
                if max(abs(cell_x - x), abs(cell_y - y)) > 1 or (home is not None and col > home):
                    continue
                if col == home:
                    tiles.append((place, z, col, z, None))
                    tiles.append((place, z, col, (z + 1) % brick.bz, home))
                else:
                    tiles += [(place, z, col, own_z, home) for own_z in range(brick.bz)]

    for col in range(brick.cols):
        for z in range(brick.bz):
            for own_z in range(brick.bz):
                level = sum(
                    level_sums[(tile[0], z)] for tile in tiles if tile[1:4] == (z, col, own_z)
                )
                span = slice(own_z * atoms, (own_z + 1) * atoms)
                total_ref[col, z, :, span] = jnp.broadcast_to(level, (SOURCES, atoms))

    mirrors = {(col, z): [] for col in range(brick.cols) for z in range(brick.bz)}
    for place, z, col, own_z, home in tiles:
        span = slice(own_z * atoms, (own_z + 1) * atoms)
        left = left_ref[place, z * atoms : (z + 1) * atoms, :]
        high, low = pair_factor(left, right_ref[col, z, :, span])
        total_ref[col, z, :, span] += mul(
            source_ref[place, z], jnp.concatenate([high, low], axis=0)
        )
        if home is not None:
            spot = 2 * atoms * len(mirrors[(home, z)])
            mirrors[(home, z)].append((col, own_z))
            kept_ref[home, z, :, spot : spot + atoms] = high
            kept_ref[home, z, :, spot + atoms : spot + 2 * atoms] = low
    back_sums = {}
    for (col, z), found in mirrors.items():
        back = jnp.concatenate([back_ref[c, z, own_z] for c, own_z in found], axis=1)
        level = (-0.5 * LEVEL) * jnp.sum(back.astype(F32), axis=1, keepdims=True)
        back_sums[(col, z)] = mul_t(kept_ref[col, z, :, 0 : back.shape[1]], back).T + level

    for col in range(brick.cols):
        forces = [0.0, 0.0, 0.0]
        for z in range(brick.bz):
            total = total_ref[col, z]
            weight = moments(total, 0)
            for comp, coord in enumerate((own_x, own_y, own_z_coords[z])):
                value = coord[col : col + 1] * weight - moments(total, 1 + comp)
                forces[comp] = forces[comp] + value
        total = jnp.concatenate([back_sums[(col, z)] for z in range(brick.bz)], axis=1)
        weight = moments(total, 0)
        home = (own[2] + (lane_z - half)) * SCALE
        for comp, coord in enumerate((own_x, own_y, home)):
            row = comp * brick.cols + col
            value = coord[col : col + 1] * weight - moments(total, 1 + comp)
            value = value + forces[comp]
            force_ref[row : row + 1, :] = value * (own[3][col : col + 1] * (SCALE * SCALE))


def fine_tables(brick):
    ext_x = brick.px + 2 * REACH
    rows_y = brick.py + POINTS * brick.by
    along_z = np.zeros((128, 128 * len(FINE_WIDTHS)), np.float32)
    along_xy = np.zeros((brick.px * brick.py, len(FINE_WIDTHS) * ext_x * rows_y), np.float32)

    def tap(dist, width):
        return np.where(np.abs(dist) <= REACH, np.exp(-(dist * dist) / (2.0 * width * width)), 0.0)

    for number, (width, weight) in enumerate(zip(FINE_WIDTHS, FINE_WEIGHTS)):
        for step in range(-REACH, REACH + 1):
            for z in range(brick.pz):
                along_z[(z + step) % brick.pz, 128 * number + z] += weight * tap(
                    np.float64(step), width
                )
        out_x = np.arange(brick.px) - 1.0
        in_x = np.arange(ext_x) - 1.0 - REACH
        out_y = np.arange(brick.py) - 1.0
        in_y = np.arange(rows_y) - 1.0 - POINTS * brick.by
        mat_x = tap(out_x[:, None] - in_x[None, :], width)
        mat_y = tap(out_y[:, None] - in_y[None, :], width)
        mat_y[POINTS * brick.by + 3 :] = 0.0
        size = ext_x * rows_y
        along_xy[:, number * size : (number + 1) * size] = np.kron(mat_x, mat_y)
    return along_xy, along_z


def coarse_table(brick):
    table = np.zeros((len(COARSE_WEIGHTS) * brick.coarse_lanes, 128), np.float32)
    length = brick.ck
    for number, (fraction, weight) in enumerate(zip(COARSE_FRACTIONS, COARSE_WEIGHTS)):
        width = length / fraction
        for row in range(brick.cj * brick.ck):
            for z in range(brick.pz):
                dist = (row - z // 2) % length
                dist = min(dist, length - dist)
                table[number * brick.coarse_lanes + row, z] = weight * math.exp(
                    -(dist * dist) / (2.0 * width * width)
                )
    return table


def gauss(row, col, length, fraction):
    dist = lax.rem(row - col + 2 * length, length)
    dist = jnp.minimum(dist, length - dist).astype(F32)
    width = length / fraction
    return jnp.exp(dist * dist * (-1.0 / (2.0 * width * width)))


def potential_kernel(brick, sender, n_msgs, *refs):
    atoms = brick.atoms
    place_ref, msg_ref = refs[0:2]
    other_msgs = refs[2 : 2 + n_msgs]
    (
        whole_ref,
        short_ref,
        xy_high_ref,
        xy_low_ref,
        z_ref,
        coarse_z_ref,
        out_ref,
        ext_ref,
        pot_ref,
    ) = refs[2 + n_msgs :]
    even = place_ref[0] % 2 == 0
    step_y = POINTS * brick.by
    rows_y = brick.py + step_y
    ext_x = brick.px + 2 * REACH
    planes = {}
    for dx in (-1, 0, 1):
        grids = []
        for dy in (-1, 0, 1):
            near = slice(brick.grid_row, brick.msg_rows)
            span = slice(0, brick.blocks * 128)
            if (dx, dy) == (0, 0):
                grids.append(msg_ref[near, span])
            else:
                grids.append(near_rows(other_msgs, sender[(dx, dy)], even, near, span))
        full = brick.py + 2 * step_y
        tiles = [None] * (full // 8)
        for number, grid in enumerate(grids):
            for tile in range(brick.py // 8):
                spot = tile + number * step_y // 8
                value = grid[8 * tile : 8 * tile + 8]
                tiles[spot] = value if tiles[spot] is None else tiles[spot] + value
        column = jnp.concatenate(tiles[: rows_y // 8], axis=0)
        for x in range(brick.px):
            spot = x + POINTS * brick.bx * dx + REACH
            if 0 <= spot < ext_x:
                block, shift = divmod(x, brick.group)
                value = column[:, block * 128 : (block + 1) * 128]
                if shift:
                    value = pltpu.roll(value, 128 - shift * brick.zpad, 1)
                planes[spot] = planes[spot] + value if spot in planes else value
    for spot in range(ext_x):
        ext_ref[spot * rows_y : (spot + 1) * rows_y, :] = planes[spot]
    along = mul(ext_ref[...], z_ref[...], HIGHEST)
    along = jnp.concatenate([along[:, :128], along[:, 128:]], axis=0)
    high = along.astype(BF16)
    low = (along - high.astype(F32)).astype(BF16)
    potential = mul(xy_high_ref[...], high) + (
        mul(xy_high_ref[...], low) + mul(xy_low_ref[...], high)
    )

    total_x = 2 * brick.bx * brick.n_space
    total_y = 2 * brick.by * brick.n_sub
    first_x = place_ref[0] * (2 * brick.bx)
    first_y = place_ref[1] * (2 * brick.by)
    out_rows = round_up(brick.px, 8)
    shape = (out_rows, brick.n_space * brick.coarse_rows)
    point = lax.broadcasted_iota(jnp.int32, shape, 0)
    lane = lax.broadcasted_iota(jnp.int32, shape, 1)
    row_x = first_x + (point + 1) // 2 - 1
    col_x = lane // brick.coarse_rows * (2 * brick.bx) + lane % brick.coarse_rows - 1
    live = lane % brick.coarse_rows < brick.ci
    mats_x = jnp.concatenate(
        [
            jnp.where(live, gauss(row_x, col_x, total_x, fraction), 0.0)
            for fraction in COARSE_FRACTIONS
        ],
        axis=0,
    )
    shape = (brick.py, brick.coarse_lanes)
    point = lax.broadcasted_iota(jnp.int32, shape, 0)
    lane = lax.broadcasted_iota(jnp.int32, shape, 1)
    row_y = first_y + (point + 1) // 2 - 1
    live = lane < brick.cj * brick.ck
    lefts = [[None] * brick.px for _ in COARSE_FRACTIONS]
    for sub in range(brick.n_sub):
        part = whole_ref[:, sub].reshape(
            brick.n_space * brick.coarse_rows, brick.coarse_lanes
        )
        mixed = mul(mats_x, part, HIGHEST)
        col_y = sub * (2 * brick.by) + lane // brick.ck - 1
        for number, fraction in enumerate(COARSE_FRACTIONS):
            mat_y = jnp.where(live, gauss(row_y, col_y, total_y, fraction), 0.0)
            for x in range(brick.px):
                row = number * out_rows + x
                value = mixed[row : row + 1] * mat_y
                done = lefts[number][x]
                lefts[number][x] = value if done is None else done + value
    left = jnp.concatenate([jnp.concatenate(rows, axis=0) for rows in lefts], axis=1)
    potential = potential + mul(left, coarse_z_ref[...], HIGHEST)
    for x in range(brick.px):
        pot_ref[x] = potential[x * brick.py : (x + 1) * brick.py]

    for x in range(brick.bx):
        for y in range(brick.by):
            col = brick.col(x, y)
            rows = [
                msg_ref[k * brick.cols + col : k * brick.cols + col + 1, 0 : brick.lanes]
                for k in range(4)
            ]
            shifted = [
                shift_xy(brick, rows[0]),
                shift_xy(brick, rows[1]),
                shift_z(brick, rows[2]),
            ]
            weights = [spline(value) for value in shifted]
            slopes = [spline_slope(value) for value in shifted]
            box = jnp.concatenate(
                [
                    pot_ref[POINTS * x + e, POINTS * y : POINTS * y + 8, 0 : brick.zpad]
                    for e in range(TAPS)
                ],
                axis=0,
            )
            both = mul(box, jnp.concatenate([weights[2], slopes[2]], axis=1), HIGHEST)
            along_z = both[:, : brick.lanes]
            sloped_z = both[:, brick.lanes :]
            sums = [0.0, 0.0, 0.0]
            for e in range(TAPS):
                weight = weights[0][e : e + 1]
                slope = slopes[0][e : e + 1]
                flat = along_z[8 * e : 8 * e + 8]
                steep = sloped_z[8 * e : 8 * e + 8]
                sums[0] = sums[0] + flat * slope
                sums[1] = sums[1] + flat * weight
                sums[2] = sums[2] + steep * weight
            across = (weights[1], slopes[1], weights[1])
            for comp in range(3):
                force = jnp.sum(sums[comp] * across[comp], axis=0, keepdims=True)
                row = comp * brick.cols + col
                force = short_ref[row : row + 1, :] - POINTS * (rows[3] * force)
                for z in range(brick.bz):
                    out_ref[comp, x, z, y : y + 1, :] = force[:, z * atoms : (z + 1) * atoms]


VMEM = pl.BlockSpec(memory_space=pltpu.VMEM)
SMEM = pl.BlockSpec(memory_space=pltpu.SMEM)
ANY = pl.BlockSpec(memory_space=pl.ANY)
WHOLE = pl.BlockSpec()


def call(kernel, out_shape, in_specs, scratch, flops, *args, out_spec=VMEM, grant=40):
    single = not isinstance(out_shape, (list, tuple))
    return pl.pallas_call(
        kernel,
        out_shape=out_shape,
        in_specs=in_specs,
        out_specs=out_spec if single else [out_spec] * len(out_shape),
        scratch_shapes=scratch,
        compiler_params=pltpu.CompilerParams(vmem_limit_bytes=grant * 1024 * 1024),
        cost_estimate=pl.CostEstimate(flops=flops, bytes_accessed=10**5, transcendentals=0),
    )(*args)


def neighbours(brick, msg):
    size, wide = brick.n_space, brick.n_sub
    pairings = {
        0: lambda i: i,
        1: lambda i: i ^ 1,
        2: lambda i: (((i + 1) % size ^ 1) - 1) % size,
    }
    found = {}
    sender = {}
    msgs = []
    for dx in (0, -1, 1):
        for dy in (0, -1, 1):
            if (dx, dy) == (0, 0):
                continue
            numbers = []
            for parity in (0, 1):
                pairing = 0 if dx == 0 else 1 if (dx == 1) == (parity == 0) else 2
                key = (pairing, dy % wide)
                if key not in found:
                    found[key] = len(msgs)
                    pairs = [
                        (pairings[pairing](i) * wide + (j + dy) % wide, i * wide + j)
                        for i in range(size)
                        for j in range(wide)
                    ]
                    msgs.append(lax.ppermute(msg, ("space", "sub"), pairs))
                numbers.append(found[key])
            sender[(dx, dy)] = tuple(numbers)
    return sender, msgs


def near_rows(msgs, numbers, even, rows, span):
    first = msgs[numbers[0]][rows, span]
    if numbers[0] == numbers[1]:
        return first
    return jnp.where(even, first, msgs[numbers[1]][rows, span])


def body(n_space, n_sub, positions, charges, counts):
    brick = Brick(charges.shape, n_space, n_sub)
    n_dev = n_space * n_sub
    along_xy, along_z = fine_tables(brick)
    xy_high = along_xy.astype(BF16)
    xy_low = (along_xy - xy_high.astype(np.float32)).astype(BF16)
    coarse_z = coarse_table(brick)
    place = jnp.stack([lax.axis_index("space"), lax.axis_index("sub")]).astype(jnp.int32)

    turned = (positions.transpose(0, 1, 3, 2, 4), charges.transpose(0, 2, 1, 3))
    msg, coarse = call(
        functools.partial(spread_kernel, brick),
        [
            jax.ShapeDtypeStruct((brick.msg_rows, brick.msg_lanes), F32),
            jax.ShapeDtypeStruct((n_dev, brick.coarse_rows, brick.coarse_lanes), F32),
        ],
        [ANY, ANY, ANY],
        [
            pltpu.SMEM(counts.shape, jnp.int32),
            pltpu.VMEM(turned[0].shape, F32),
            pltpu.VMEM(turned[1].shape, F32),
            pltpu.VMEM((brick.px, brick.py, 128), F32),
            pltpu.SemaphoreType.DMA((3,)),
        ],
        10**7,
        counts,
        *turned,
        grant=64,
    )
    sender, msgs = neighbours(brick, msg)
    whole = lax.all_to_all(coarse, ("space", "sub"), 0, 0, tiled=True)
    whole = whole.reshape(n_space, n_sub, brick.coarse_rows, brick.coarse_lanes)

    n_col = len(brick.columns)
    short = call(
        functools.partial(pairs_kernel, brick, sender, len(msgs)),
        jax.ShapeDtypeStruct((brick.force_rows, brick.lanes), F32),
        [SMEM] + [VMEM] * (1 + len(msgs)),
        [
            pltpu.VMEM((4 * brick.ext_rows, brick.lanes), F32),
            pltpu.VMEM((brick.lanes // 128, FEATURES * brick.ext_rows, 128), F32),
            pltpu.VMEM((brick.lanes // 128, SOURCES * brick.ext_rows, 128), F32),
            pltpu.VMEM((brick.lanes // 128, FEATURES * brick.own_rows, 128), F32),
            pltpu.VMEM((brick.lanes // 128, SOURCES * brick.own_rows, 128), F32),
            pltpu.VMEM((n_col, brick.lanes, FEATURES), BF16),
            pltpu.VMEM((n_col, brick.bz, SOURCES, 2 * brick.atoms), BF16),
            pltpu.VMEM((brick.cols, brick.bz, FEATURES, brick.lanes), BF16),
            pltpu.VMEM((brick.cols, brick.bz, brick.bz, SOURCES, 2 * brick.atoms), BF16),
            pltpu.VMEM((brick.cols, brick.bz, SOURCES, brick.lanes), F32),
            pltpu.VMEM((brick.cols, brick.bz, brick.atoms, brick.kept), BF16),
        ],
        10**10,
        place,
        msg,
        *msgs,
    )
    ext_x = brick.px + 2 * REACH
    rows_y = brick.py + POINTS * brick.by
    comps, size_x, size_y, size_z, atoms = positions.shape
    forces = call(
        functools.partial(potential_kernel, brick, sender, len(msgs)),
        jax.ShapeDtypeStruct((comps, size_x, size_z, size_y, atoms), F32),
        [SMEM] + [VMEM] * (7 + len(msgs)),
        [
            pltpu.VMEM((ext_x * rows_y, 128), F32),
            pltpu.VMEM((brick.px, brick.py, 128), F32),
        ],
        10**8,
        place,
        msg,
        *msgs,
        whole,
        short,
        xy_high,
        xy_low,
        jnp.asarray(along_z),
        jnp.asarray(coarse_z),
        out_spec=WHOLE,
    )
    return forces.transpose(0, 1, 3, 2, 4)


def solution(mesh):
    in_specs = (
        P(None, "space", "sub", None, None),
        P("space", "sub", None, None),
        P("space", "sub", None),
    )
    out_specs = P(None, "space", "sub", None, None)
    run = functools.partial(body, mesh.shape["space"], mesh.shape["sub"])
    return jax.shard_map(run, mesh=mesh, in_specs=in_specs, out_specs=out_specs, check_vma=False)
```

```python
import functools
import math

import jax
import jax.numpy as jnp
import numpy as np
from jax import lax
from jax.experimental import pallas as pl
from jax.experimental.pallas import tpu as pltpu
from jax.sharding import PartitionSpec as P

F32 = jnp.float32
BF16 = jnp.bfloat16
HIGHEST = lax.Precision.HIGHEST

POINTS = 4
REACH = 4
TAPS = POINTS + 3
SOFT_SQUARE = 0.0625
FINE_WIDTHS = (1.0, 2.0)
FINE_WEIGHTS = (2.0, 0.5)
COARSE_FRACTIONS = (8.0, 4.0)
COARSE_WEIGHTS = (4.0, 2.0)

DECAY = 0.11446730730706552
LEAD = 0.13637726630426547
SMOOTH = (1.0312317180277653, 0.44426879021665455, 0.1544174241571791, -0.004580112368867706)
SCALE = math.sqrt(DECAY * math.log2(math.e))
STRETCH = (LEAD / SCALE**3) ** 0.2
SHIFT = math.log2(STRETCH)
QUARTIC = (SMOOTH[0] * STRETCH**2, SMOOTH[1] * STRETCH**4, SMOOTH[2] * STRETCH)
LEVEL = SMOOTH[3] / SCALE**3
HALF_CONST = 0.5 * (SHIFT - SCALE * SCALE * SOFT_SQUARE)

FEATURES = 32
SOURCES = 16


def round_up(value, step):
    return -(-value // step) * step


def mul_t(left, right, precision=None):
    return lax.dot_general(
        left, right, (((1,), (1,)), ((), ())), precision=precision, preferred_element_type=F32
    )


def mul(left, right, precision=None):
    return lax.dot_general(
        left, right, (((1,), (0,)), ((), ())), precision=precision, preferred_element_type=F32
    )


def split(value, count):
    pieces = []
    for _ in range(count - 1):
        piece = value.astype(BF16).astype(F32)
        pieces.append(piece)
        value = value - piece
    pieces.append(value.astype(BF16).astype(F32))
    return pieces


class Brick:
    def __init__(self, shape, n_space, n_sub):
        self.bx, self.by, self.bz, self.atoms = shape
        self.n_space, self.n_sub = n_space, n_sub
        self.cols = self.bx * self.by
        self.lanes = self.bz * self.atoms
        self.wide = (self.bz + 2) * self.atoms
        self.px = POINTS * self.bx + 3
        self.py = round_up(POINTS * (self.by - 1) + 8, 8)
        self.pz = POINTS * self.bz
        self.zpad = round_up(self.pz, 16)
        self.group = 128 // self.zpad
        self.atom_rows = 4 * self.cols
        self.blocks = -(-self.px // self.group)
        self.msg_rows = round_up(self.atom_rows, 8) + self.py
        self.msg_lanes = max(self.lanes, self.blocks * 128)
        self.grid_row = round_up(self.atom_rows, 8)
        self.ci = 2 * self.bx + 2
        self.cj = 2 * self.by + 2
        self.ck = 2 * self.bz
        self.coarse_rows = round_up(self.ci, 8)
        self.coarse_lanes = round_up(self.cj * self.ck, 128)
        self.own_rows = round_up(self.cols, 8)
        self.columns = [
            (x, y) for x in range(-1, self.bx + 1) for y in range(-1, self.by + 1)
        ]
        self.ext_rows = round_up(len(self.columns), 8)
        self.kept = 2 * self.atoms * (1 + self.bz * (self.cols - 1))
        self.force_rows = round_up(3 * self.cols, 8)

    def col(self, x, y):
        return x * self.by + y


def spline(shifted):
    size = jnp.abs(shifted)
    outer = jnp.maximum(2.0 - size, 0.0)
    inner = jnp.maximum(1.0 - size, 0.0)
    return (outer * outer * outer) * (1.0 / 6.0) - (inner * inner * inner) * (4.0 / 6.0)


def spline_slope(shifted):
    size = jnp.abs(shifted)
    outer = jnp.maximum(2.0 - size, 0.0)
    inner = jnp.maximum(1.0 - size, 0.0)
    slope = 2.0 * (inner * inner) - 0.5 * (outer * outer)
    return jnp.where(shifted < 0.0, -slope, slope)


def shift_xy(brick, row):
    entry = lax.broadcasted_iota(jnp.int32, (8, brick.lanes), 0).astype(F32)
    return POINTS * row - (entry - 1.0)


def shift_z(brick, row):
    parts = []
    for cell in range(brick.bz):
        point = lax.broadcasted_iota(jnp.int32, (brick.zpad, brick.atoms), 0)
        entry = lax.rem(point - POINTS * cell + 1 + brick.pz, brick.pz) - 1
        entry = jnp.where(point < brick.pz, entry, 100)
        value = row[:, cell * brick.atoms : (cell + 1) * brick.atoms]
        parts.append(POINTS * value - entry.astype(F32))
    return jnp.concatenate(parts, axis=1)


def spread_kernel(brick, *refs):
    inputs, (msg_ref, coarse_ref), held = refs[0:3], refs[3:5], refs[5:8]
    grid_ref, arrived = refs[8:]
    counts_ref, pos_ref, charge_ref = held
    copies = [
        pltpu.make_async_copy(source, target, arrived.at[number])
        for number, (source, target) in enumerate(zip(inputs, held))
    ]
    for copy in copies:
        copy.start()
    grid_ref[...] = jnp.zeros(grid_ref.shape, F32)
    for copy in copies:
        copy.wait()
    atoms = brick.atoms
    lane = lax.broadcasted_iota(jnp.int32, (1, atoms), 1)
    for x in range(brick.bx):
        for y in range(brick.by):
            col = brick.col(x, y)
            for z in range(brick.bz):
                span = slice(z * atoms, (z + 1) * atoms)
                for comp in range(3):
                    row = comp * brick.cols + col
                    msg_ref[row : row + 1, span] = pos_ref[comp, x, z, y : y + 1, :]
                row = 3 * brick.cols + col
                charge = charge_ref[x, z, y : y + 1, :]
                msg_ref[row : row + 1, span] = jnp.where(lane < counts_ref[x, y, z], charge, 0.0)
    for x in range(brick.bx):
        for y in range(brick.by):
            col = brick.col(x, y)
            rows = [
                msg_ref[k * brick.cols + col : k * brick.cols + col + 1, 0 : brick.lanes]
                for k in range(4)
            ]
            along_x = spline(shift_xy(brick, rows[0])) * rows[3]
            along_y = spline(shift_xy(brick, rows[1]))
            along_z = spline(shift_z(brick, rows[2]))
            outer = jnp.concatenate(
                [along_x[e : e + 1, :] * along_y for e in range(TAPS)], axis=0
            )
            count = outer.shape[0]
            outer = jnp.concatenate(split(outer, 2), axis=0).astype(BF16)
            table = jnp.concatenate(split(along_z, 2), axis=0).astype(BF16)
            box = mul_t(outer, table)
            box = (
                box[:count, : brick.zpad] + box[:count, brick.zpad :] + box[count:, : brick.zpad]
            )
            for e in range(TAPS):
                place = (POINTS * x + e, slice(POINTS * y, POINTS * y + 8), slice(0, brick.zpad))
                grid_ref[place] = grid_ref[place] + box[8 * e : 8 * e + 8, :]
    for block in range(brick.msg_lanes // 128):
        total = jnp.zeros((brick.py, 128), F32)
        for spot in range(brick.group):
            x = block * brick.group + spot
            if x < brick.px:
                plane = grid_ref[x]
                total = total + (pltpu.roll(plane, spot * brick.zpad, 1) if spot else plane)
        msg_ref[brick.grid_row :, block * 128 : (block + 1) * 128] = total
    planes = []
    for idx in range(brick.ci):
        inside = [x for x in (2 * idx - 1, 2 * idx) if 0 <= x < brick.px]
        planes.append(sum(grid_ref[x, :, 0 : brick.zpad] for x in inside))
    stacked = jnp.concatenate(planes, axis=0)
    shape = (brick.zpad, brick.coarse_lanes)
    z_idx = lax.broadcasted_iota(jnp.int32, shape, 0)
    z_lane = lax.broadcasted_iota(jnp.int32, shape, 1)
    used = z_lane < brick.cj * brick.ck
    pairs = (z_idx // 2 == z_lane % brick.ck) & used & (z_idx < brick.pz)
    folded = mul(stacked, jnp.where(pairs, 0.125, 0.0).astype(F32), HIGHEST)
    shape = (brick.py, brick.coarse_lanes)
    y_idx = lax.broadcasted_iota(jnp.int32, shape, 0)
    y_lane = lax.broadcasted_iota(jnp.int32, shape, 1)
    mask = (y_lane // brick.ck == (y_idx + 1) // 2).astype(F32)
    sums = [
        jnp.sum(folded[i * brick.py : (i + 1) * brick.py] * mask, axis=0, keepdims=True)
        for i in range(brick.ci)
    ]
    if brick.coarse_rows > brick.ci:
        sums.append(jnp.zeros((brick.coarse_rows - brick.ci, brick.coarse_lanes), F32))
    coarse_ref[...] = jnp.broadcast_to(jnp.concatenate(sums, axis=0)[None], coarse_ref.shape)


def store_pieces(piece_ref, rows, arrays):
    for number, value in enumerate(arrays):
        for block in range(piece_ref.shape[0]):
            piece_ref[block, number * rows : (number + 1) * rows, :] = value[
                :, block * 128 : (block + 1) * 128
            ]


def load_pieces(piece_ref, rows, row, count):
    parts = [
        piece_ref[block, pl.ds(row, count, stride=rows), :] for block in range(piece_ref.shape[0])
    ]
    return jnp.concatenate(parts, axis=1)


def feature_arrays(coords, square, order, square_first):
    rows = coords[0].shape
    arrays = []
    for value in coords:
        pieces = split(value, 3)
        arrays += [pieces[piece] for piece in order]
    squares = split(square, 3)
    ones = [jnp.ones(rows, F32)] * 3
    arrays += squares + ones if square_first else ones + squares
    return arrays + [jnp.zeros(rows, F32)] * (FEATURES - len(arrays))


def source_arrays(coords, charge):
    arrays = []
    for value in [charge] + [charge * coord for coord in coords]:
        arrays += split(value, 3)
    return arrays + [jnp.zeros(charge.shape, F32)] * (SOURCES - len(arrays))


def minus_square(coords):
    return HALF_CONST - (coords[0] * coords[0] + coords[1] * coords[1] + coords[2] * coords[2])


def pair_factor(left, right):
    power = mul(left, right)
    inverse = lax.rsqrt(SHIFT - power)
    base = jnp.exp2(power)
    square = base * base
    smooth = ((square + QUARTIC[0]) * square + QUARTIC[1]) * (base + QUARTIC[2])
    factor = inverse * (inverse * inverse) - smooth
    high = factor.astype(BF16)
    low = (factor - high.astype(F32)).astype(BF16)
    return high, low


def moments(total, quantity):
    base = 3 * quantity
    return total[base : base + 1] + total[base + 1 : base + 2] + total[base + 2 : base + 3]


def pairs_kernel(brick, sender, n_msgs, *refs):
    atoms, lanes = brick.atoms, brick.lanes
    place_ref, msg_ref = refs[0:2]
    other_msgs = refs[2 : 2 + n_msgs]
    force_ref = refs[2 + n_msgs]
    (
        row_ref,
        other_piece_ref,
        source_piece_ref,
        own_piece_ref,
        own_source_ref,
        left_ref,
        source_ref,
        right_ref,
        back_ref,
        total_ref,
        kept_ref,
    ) = refs[3 + n_msgs :]
    even = place_ref[0] % 2 == 0
    half = 0.5 * brick.bz

    rows = brick.ext_rows
    if rows > len(brick.columns):
        row_ref[...] = jnp.zeros(row_ref.shape, F32)
    for place, (x, y) in enumerate(brick.columns):
        shift = (x // brick.bx, y // brick.by)
        col = brick.col(x % brick.bx, y % brick.by)
        for k in range(4):
            near = slice(k * brick.cols + col, k * brick.cols + col + 1)
            if shift == (0, 0):
                value = msg_ref[near, 0:lanes]
            else:
                value = near_rows(other_msgs, sender[shift], even, near, slice(0, lanes))
            row_ref[k * rows + place : k * rows + place + 1, :] = value
    index = lax.broadcasted_iota(jnp.int32, (rows, 1), 0)
    ext_y = brick.by + 2
    offset_x = (index // ext_y - 1).astype(F32) - 0.5 * brick.bx
    offset_y = (index % ext_y - 1).astype(F32) - 0.5 * brick.by
    lane_z = (lax.broadcasted_iota(jnp.int32, (1, lanes), 1) // atoms).astype(F32)
    coords = [
        (row_ref[0:rows, :] + offset_x) * SCALE,
        (row_ref[rows : 2 * rows, :] + offset_y) * SCALE,
        (row_ref[2 * rows : 3 * rows, :] + (lane_z - half)) * SCALE,
    ]
    charge = row_ref[3 * rows : 4 * rows, :]
    store_pieces(
        other_piece_ref,
        rows,
        feature_arrays(coords, minus_square(coords), (0, 1, 2, 0, 1, 0), False),
    )
    store_pieces(source_piece_ref, rows, source_arrays(coords, charge))
    level_sums = {}
    for place in range(len(brick.columns)):
        feature = load_pieces(other_piece_ref, rows, place, FEATURES)
        left_ref[place] = feature.T.astype(BF16)
        source = load_pieces(source_piece_ref, rows, place, SOURCES)
        for z in range(brick.bz):
            part = source[:, z * atoms : (z + 1) * atoms]
            level_sums[(place, z)] = -LEVEL * jnp.sum(part, axis=1, keepdims=True)
            part = part.astype(BF16)
            source_ref[place, z] = jnp.concatenate([part, part], axis=1)

    rows = brick.own_rows
    own = []
    for k in range(4):
        value = msg_ref[k * brick.cols : (k + 1) * brick.cols, 0:lanes]
        if rows > brick.cols:
            value = jnp.concatenate([value, jnp.zeros((rows - brick.cols, lanes), F32)], axis=0)
        own.append(value)
    index = lax.broadcasted_iota(jnp.int32, (rows, 1), 0)
    own_x = (own[0] + ((index // brick.by).astype(F32) - 0.5 * brick.bx)) * SCALE
    own_y = (own[1] + ((index % brick.by).astype(F32) - 0.5 * brick.by)) * SCALE
    own_z_coords = []
    for other_z in range(brick.bz):
        step = other_z - lane_z
        step = jnp.where(step > half, step - brick.bz, step)
        step = jnp.where(step < -half, step + brick.bz, step)
        own_z_coords.append((own[2] + (other_z - step - half)) * SCALE)
        coords = [own_x, own_y, own_z_coords[-1]]
        arrays = feature_arrays(coords, minus_square(coords), (0, 0, 0, 1, 1, 2), True)
        arrays = [2.0 * value for value in arrays[:18]] + arrays[18:]
        store_pieces(own_piece_ref, rows, arrays)
        store_pieces(own_source_ref, rows, source_arrays(coords, own[3]))
        for col in range(brick.cols):
            part = load_pieces(own_piece_ref, rows, col, FEATURES)
            right_ref[col, other_z] = part.astype(BF16)
            part = load_pieces(own_source_ref, rows, col, SOURCES).astype(BF16)
            for z in range(brick.bz):
                cell = part[:, z * atoms : (z + 1) * atoms]
                back_ref[col, other_z, z] = jnp.concatenate([cell, cell], axis=1)

    cells = [(x, y) for x in range(brick.bx) for y in range(brick.by)]
    tiles = []
    for place, (x, y) in sorted(enumerate(brick.columns), key=lambda item: item[1] not in cells):
        home = cells.index((x, y)) if (x, y) in cells else None
        for z in range(brick.bz):
            for col, (cell_x, cell_y) in enumerate(cells):
                if max(abs(cell_x - x), abs(cell_y - y)) > 1 or (home is not None and col > home):
                    continue
                if col == home:
                    tiles.append((place, z, col, z, None))
                    tiles.append((place, z, col, (z + 1) % brick.bz, home))
                else:
                    tiles += [(place, z, col, own_z, home) for own_z in range(brick.bz)]

    for col in range(brick.cols):
        for z in range(brick.bz):
            for own_z in range(brick.bz):
                level = sum(
                    level_sums[(tile[0], z)] for tile in tiles if tile[1:4] == (z, col, own_z)
                )
                span = slice(own_z * atoms, (own_z + 1) * atoms)
                total_ref[col, z, :, span] = jnp.broadcast_to(level, (SOURCES, atoms))

    mirrors = {(col, z): [] for col in range(brick.cols) for z in range(brick.bz)}
    for place, z, col, own_z, home in tiles:
        span = slice(own_z * atoms, (own_z + 1) * atoms)
        left = left_ref[place, z * atoms : (z + 1) * atoms, :]
        high, low = pair_factor(left, right_ref[col, z, :, span])
        total_ref[col, z, :, span] += mul(
            source_ref[place, z], jnp.concatenate([high, low], axis=0)
        )
        if home is not None:
            spot = 2 * atoms * len(mirrors[(home, z)])
            mirrors[(home, z)].append((col, own_z))
            kept_ref[home, z, :, spot : spot + atoms] = high
            kept_ref[home, z, :, spot + atoms : spot + 2 * atoms] = low
    back_sums = {}
    for (col, z), found in mirrors.items():
        back = jnp.concatenate([back_ref[c, z, own_z] for c, own_z in found], axis=1)
        level = (-0.5 * LEVEL) * jnp.sum(back.astype(F32), axis=1, keepdims=True)
        back_sums[(col, z)] = mul_t(kept_ref[col, z, :, 0 : back.shape[1]], back).T + level

    for col in range(brick.cols):
        forces = [0.0, 0.0, 0.0]
        for z in range(brick.bz):
            total = total_ref[col, z]
            weight = moments(total, 0)
            for comp, coord in enumerate((own_x, own_y, own_z_coords[z])):
                value = coord[col : col + 1] * weight - moments(total, 1 + comp)
                forces[comp] = forces[comp] + value
        total = jnp.concatenate([back_sums[(col, z)] for z in range(brick.bz)], axis=1)
        weight = moments(total, 0)
        home = (own[2] + (lane_z - half)) * SCALE
        for comp, coord in enumerate((own_x, own_y, home)):
            row = comp * brick.cols + col
            value = coord[col : col + 1] * weight - moments(total, 1 + comp)
            value = value + forces[comp]
            force_ref[row : row + 1, :] = value * (own[3][col : col + 1] * (SCALE * SCALE))


def fine_tables(brick):
    ext_x = brick.px + 2 * REACH
    rows_y = brick.py + POINTS * brick.by
    out_lanes = brick.blocks * 128
    in_lanes = round_up(max(ext_x * brick.zpad, out_lanes), 128)
    count = len(FINE_WIDTHS)
    along_xz = np.zeros((in_lanes, count * out_lanes), np.float32)
    along_y = np.zeros((brick.py, count * rows_y), np.float32)

    def tap(dist, width):
        return np.where(np.abs(dist) <= REACH, np.exp(-(dist * dist) / (2.0 * width * width)), 0.0)

    for number, (width, weight) in enumerate(zip(FINE_WIDTHS, FINE_WEIGHTS)):
        mat_z = np.zeros((brick.zpad, brick.zpad))
        for step in range(-REACH, REACH + 1):
            for z in range(brick.pz):
                mat_z[(z + step) % brick.pz, z] += weight * tap(np.float64(step), width)
        mat_x = tap(np.arange(ext_x)[:, None] - np.arange(brick.px)[None, :] - REACH, width)
        dense = np.kron(mat_x, mat_z)
        along_xz[: dense.shape[0], number * out_lanes : number * out_lanes + dense.shape[1]] = dense
        out_y = np.arange(POINTS * brick.by + 3) - 1.0
        in_y = np.arange(rows_y) - 1.0 - POINTS * brick.by
        along_y[: len(out_y), number * rows_y : (number + 1) * rows_y] = tap(
            out_y[:, None] - in_y[None, :], width
        )
    return along_xz, along_y


def coarse_table(brick):
    table = np.zeros((len(COARSE_WEIGHTS) * brick.coarse_lanes, 128), np.float32)
    length = brick.ck
    for number, (fraction, weight) in enumerate(zip(COARSE_FRACTIONS, COARSE_WEIGHTS)):
        width = length / fraction
        for row in range(brick.cj * brick.ck):
            for z in range(brick.pz):
                dist = (row - z // 2) % length
                dist = min(dist, length - dist)
                table[number * brick.coarse_lanes + row, z] = weight * math.exp(
                    -(dist * dist) / (2.0 * width * width)
                )
    return table


def gauss(row, col, length, fraction):
    dist = lax.rem(row - col + 2 * length, length)
    dist = jnp.minimum(dist, length - dist).astype(F32)
    width = length / fraction
    return jnp.exp(dist * dist * (-1.0 / (2.0 * width * width)))


def potential_kernel(brick, sender, n_msgs, *refs):
    atoms = brick.atoms
    place_ref, msg_ref = refs[0:2]
    other_msgs = refs[2 : 2 + n_msgs]
    (
        whole_ref,
        short_ref,
        xz_high_ref,
        xz_low_ref,
        y_ref,
        coarse_z_ref,
        out_ref,
        pot_ref,
    ) = refs[2 + n_msgs :]
    even = place_ref[0] % 2 == 0
    step_y = POINTS * brick.by
    rows_y = brick.py + step_y
    in_lanes = xz_high_ref.shape[0]
    out_lanes = brick.blocks * 128
    grid = None
    for dx in (-1, 0, 1):
        grids = []
        for dy in (-1, 0, 1):
            near = slice(brick.grid_row, brick.msg_rows)
            span = slice(0, out_lanes)
            if (dx, dy) == (0, 0):
                grids.append(msg_ref[near, span])
            else:
                grids.append(near_rows(other_msgs, sender[(dx, dy)], even, near, span))
        tiles = [None] * ((brick.py + 2 * step_y) // 8)
        for number, part in enumerate(grids):
            for tile in range(brick.py // 8):
                spot = tile + number * step_y // 8
                value = part[8 * tile : 8 * tile + 8]
                tiles[spot] = value if tiles[spot] is None else tiles[spot] + value
        column = jnp.concatenate(tiles[: rows_y // 8], axis=0)
        if in_lanes > out_lanes:
            column = jnp.concatenate(
                [column, jnp.zeros((rows_y, in_lanes - out_lanes), F32)], axis=1
            )
        shift = (REACH + POINTS * brick.bx * dx) * brick.zpad
        column = pltpu.roll(column, shift % in_lanes, 1)
        grid = column if grid is None else grid + column
    pieces = jnp.concatenate(split(grid, 2), axis=0).astype(BF16)
    mixed = mul(pieces, xz_high_ref[...]) + mul(pieces, xz_low_ref[...])
    mixed = mixed[:rows_y] + mixed[rows_y:]
    mixed = jnp.concatenate(
        [mixed[:, n * out_lanes : (n + 1) * out_lanes] for n in range(len(FINE_WIDTHS))], axis=0
    )
    fine = mul(y_ref[...], mixed, HIGHEST)

    total_x = 2 * brick.bx * brick.n_space
    total_y = 2 * brick.by * brick.n_sub
    first_x = place_ref[0] * (2 * brick.bx)
    first_y = place_ref[1] * (2 * brick.by)
    out_rows = round_up(brick.px, 8)
    shape = (out_rows, brick.n_space * brick.coarse_rows)
    point = lax.broadcasted_iota(jnp.int32, shape, 0)
    lane = lax.broadcasted_iota(jnp.int32, shape, 1)
    row_x = first_x + (point + 1) // 2 - 1
    col_x = lane // brick.coarse_rows * (2 * brick.bx) + lane % brick.coarse_rows - 1
    live = lane % brick.coarse_rows < brick.ci
    mats_x = jnp.concatenate(
        [
            jnp.where(live, gauss(row_x, col_x, total_x, fraction), 0.0)
            for fraction in COARSE_FRACTIONS
        ],
        axis=0,
    )
    shape = (brick.py, brick.coarse_lanes)
    point = lax.broadcasted_iota(jnp.int32, shape, 0)
    lane = lax.broadcasted_iota(jnp.int32, shape, 1)
    row_y = first_y + (point + 1) // 2 - 1
    live = lane < brick.cj * brick.ck
    lefts = [[None] * brick.px for _ in COARSE_FRACTIONS]
    for sub in range(brick.n_sub):
        part = whole_ref[:, sub].reshape(
            brick.n_space * brick.coarse_rows, brick.coarse_lanes
        )
        mixed = mul(mats_x, part, HIGHEST)
        col_y = sub * (2 * brick.by) + lane // brick.ck - 1
        for number, fraction in enumerate(COARSE_FRACTIONS):
            mat_y = jnp.where(live, gauss(row_y, col_y, total_y, fraction), 0.0)
            for x in range(brick.px):
                row = number * out_rows + x
                value = mixed[row : row + 1] * mat_y
                done = lefts[number][x]
                lefts[number][x] = value if done is None else done + value
    left = jnp.concatenate([jnp.concatenate(rows, axis=0) for rows in lefts], axis=1)
    coarse = mul(left, coarse_z_ref[...], HIGHEST)
    lane = lax.broadcasted_iota(jnp.int32, (brick.py, 128), 1)
    for x in range(brick.px):
        block, shift = divmod(x, brick.group)
        value = fine[:, block * 128 : (block + 1) * 128]
        if shift:
            value = pltpu.roll(value, 128 - shift * brick.zpad, 1)
        value = value + coarse[x * brick.py : (x + 1) * brick.py]
        high, low = split(jnp.where(lane < brick.zpad, value, 0.0), 2)
        pot_ref[x] = (
            high + pltpu.roll(high, brick.zpad, 1) + pltpu.roll(low, 2 * brick.zpad, 1)
        )

    for x in range(brick.bx):
        for y in range(brick.by):
            col = brick.col(x, y)
            rows = [
                msg_ref[k * brick.cols + col : k * brick.cols + col + 1, 0 : brick.lanes]
                for k in range(4)
            ]
            shifted = [
                shift_xy(brick, rows[0]),
                shift_xy(brick, rows[1]),
                shift_z(brick, rows[2]),
            ]
            weights = [spline(value) for value in shifted]
            slopes = [spline_slope(value) for value in shifted]
            box = jnp.concatenate(
                [
                    pot_ref[POINTS * x + e, POINTS * y : POINTS * y + 8, 0 : 3 * brick.zpad]
                    for e in range(TAPS)
                ],
                axis=0,
            )
            high, low = split(jnp.concatenate([weights[2], slopes[2]], axis=1), 2)
            tables = jnp.concatenate([high, low, high], axis=0).astype(BF16)
            both = mul(box.astype(BF16), tables)
            along_z = both[:, : brick.lanes]
            sloped_z = both[:, brick.lanes :]
            sums = [0.0, 0.0, 0.0]
            for e in range(TAPS):
                weight = weights[0][e : e + 1]
                slope = slopes[0][e : e + 1]
                flat = along_z[8 * e : 8 * e + 8]
                steep = sloped_z[8 * e : 8 * e + 8]
                sums[0] = sums[0] + flat * slope
                sums[1] = sums[1] + flat * weight
                sums[2] = sums[2] + steep * weight
            across = (weights[1], slopes[1], weights[1])
            for comp in range(3):
                force = jnp.sum(sums[comp] * across[comp], axis=0, keepdims=True)
                row = comp * brick.cols + col
                force = short_ref[row : row + 1, :] - POINTS * (rows[3] * force)
                for z in range(brick.bz):
                    out_ref[comp, x, z, y : y + 1, :] = force[:, z * atoms : (z + 1) * atoms]


VMEM = pl.BlockSpec(memory_space=pltpu.VMEM)
SMEM = pl.BlockSpec(memory_space=pltpu.SMEM)
ANY = pl.BlockSpec(memory_space=pl.ANY)
WHOLE = pl.BlockSpec()


def call(kernel, out_shape, in_specs, scratch, flops, *args, out_spec=VMEM, grant=40):
    single = not isinstance(out_shape, (list, tuple))
    return pl.pallas_call(
        kernel,
        out_shape=out_shape,
        in_specs=in_specs,
        out_specs=out_spec if single else [out_spec] * len(out_shape),
        scratch_shapes=scratch,
        compiler_params=pltpu.CompilerParams(vmem_limit_bytes=grant * 1024 * 1024),
        cost_estimate=pl.CostEstimate(flops=flops, bytes_accessed=10**5, transcendentals=0),
    )(*args)


def neighbours(brick, msg):
    size, wide = brick.n_space, brick.n_sub
    pairings = {
        0: lambda i: i,
        1: lambda i: i ^ 1,
        2: lambda i: (((i + 1) % size ^ 1) - 1) % size,
    }
    found = {}
    sender = {}
    msgs = []
    for dx in (0, -1, 1):
        for dy in (0, -1, 1):
            if (dx, dy) == (0, 0):
                continue
            numbers = []
            for parity in (0, 1):
                pairing = 0 if dx == 0 else 1 if (dx == 1) == (parity == 0) else 2
                key = (pairing, dy % wide)
                if key not in found:
                    found[key] = len(msgs)
                    pairs = [
                        (pairings[pairing](i) * wide + (j + dy) % wide, i * wide + j)
                        for i in range(size)
                        for j in range(wide)
                    ]
                    msgs.append(lax.ppermute(msg, ("space", "sub"), pairs))
                numbers.append(found[key])
            sender[(dx, dy)] = tuple(numbers)
    return sender, msgs


def near_rows(msgs, numbers, even, rows, span):
    first = msgs[numbers[0]][rows, span]
    if numbers[0] == numbers[1]:
        return first
    return jnp.where(even, first, msgs[numbers[1]][rows, span])


def body(n_space, n_sub, positions, charges, counts):
    brick = Brick(charges.shape, n_space, n_sub)
    n_dev = n_space * n_sub
    along_xz, along_y = fine_tables(brick)
    xz_high = along_xz.astype(BF16)
    xz_low = (along_xz - xz_high.astype(np.float32)).astype(BF16)
    coarse_z = coarse_table(brick)
    place = jnp.stack([lax.axis_index("space"), lax.axis_index("sub")]).astype(jnp.int32)

    turned = (positions.transpose(0, 1, 3, 2, 4), charges.transpose(0, 2, 1, 3))
    msg, coarse = call(
        functools.partial(spread_kernel, brick),
        [
            jax.ShapeDtypeStruct((brick.msg_rows, brick.msg_lanes), F32),
            jax.ShapeDtypeStruct((n_dev, brick.coarse_rows, brick.coarse_lanes), F32),
        ],
        [ANY, ANY, ANY],
        [
            pltpu.SMEM(counts.shape, jnp.int32),
            pltpu.VMEM(turned[0].shape, F32),
            pltpu.VMEM(turned[1].shape, F32),
            pltpu.VMEM((brick.px, brick.py, 128), F32),
            pltpu.SemaphoreType.DMA((3,)),
        ],
        10**7,
        counts,
        *turned,
        grant=64,
    )
    sender, msgs = neighbours(brick, msg)
    whole = lax.all_to_all(coarse, ("space", "sub"), 0, 0, tiled=True)
    whole = whole.reshape(n_space, n_sub, brick.coarse_rows, brick.coarse_lanes)

    n_col = len(brick.columns)
    short = call(
        functools.partial(pairs_kernel, brick, sender, len(msgs)),
        jax.ShapeDtypeStruct((brick.force_rows, brick.lanes), F32),
        [SMEM] + [VMEM] * (1 + len(msgs)),
        [
            pltpu.VMEM((4 * brick.ext_rows, brick.lanes), F32),
            pltpu.VMEM((brick.lanes // 128, FEATURES * brick.ext_rows, 128), F32),
            pltpu.VMEM((brick.lanes // 128, SOURCES * brick.ext_rows, 128), F32),
            pltpu.VMEM((brick.lanes // 128, FEATURES * brick.own_rows, 128), F32),
            pltpu.VMEM((brick.lanes // 128, SOURCES * brick.own_rows, 128), F32),
            pltpu.VMEM((n_col, brick.lanes, FEATURES), BF16),
            pltpu.VMEM((n_col, brick.bz, SOURCES, 2 * brick.atoms), BF16),
            pltpu.VMEM((brick.cols, brick.bz, FEATURES, brick.lanes), BF16),
            pltpu.VMEM((brick.cols, brick.bz, brick.bz, SOURCES, 2 * brick.atoms), BF16),
            pltpu.VMEM((brick.cols, brick.bz, SOURCES, brick.lanes), F32),
            pltpu.VMEM((brick.cols, brick.bz, brick.atoms, brick.kept), BF16),
        ],
        10**10,
        place,
        msg,
        *msgs,
    )
    comps, size_x, size_y, size_z, atoms = positions.shape
    forces = call(
        functools.partial(potential_kernel, brick, sender, len(msgs)),
        jax.ShapeDtypeStruct((comps, size_x, size_z, size_y, atoms), F32),
        [SMEM] + [VMEM] * (7 + len(msgs)),
        [
            pltpu.VMEM((brick.px, brick.py, 128), F32),
        ],
        10**8,
        place,
        msg,
        *msgs,
        whole,
        short,
        xz_high,
        xz_low,
        jnp.asarray(along_y),
        jnp.asarray(coarse_z),
        out_spec=WHOLE,
    )
    return forces.transpose(0, 1, 3, 2, 4)


def solution(mesh):
    in_specs = (
        P(None, "space", "sub", None, None),
        P("space", "sub", None, None),
        P("space", "sub", None),
    )
    out_specs = P(None, "space", "sub", None, None)
    run = functools.partial(body, mesh.shape["space"], mesh.shape["sub"])
    return jax.shard_map(run, mesh=mesh, in_specs=in_specs, out_specs=out_specs, check_vma=False)
```

```python
import functools
import math

import jax
import jax.numpy as jnp
import numpy as np
from jax import lax
from jax.experimental import pallas as pl
from jax.experimental.pallas import tpu as pltpu
from jax.sharding import PartitionSpec as P

F32 = jnp.float32
BF16 = jnp.bfloat16
HIGHEST = lax.Precision.HIGHEST

POINTS = 4
REACH = 4
TAPS = POINTS + 3
SOFT_SQUARE = 0.0625
FINE_WIDTHS = (1.0, 2.0)
FINE_WEIGHTS = (2.0, 0.5)
COARSE_FRACTIONS = (8.0, 4.0)
COARSE_WEIGHTS = (4.0, 2.0)

DECAY = 0.11446730730706552
LEAD = 0.13637726630426547
SMOOTH = (1.0312317180277653, 0.44426879021665455, 0.1544174241571791, -0.004580112368867706)
SCALE = math.sqrt(DECAY * math.log2(math.e))
STRETCH = (LEAD / SCALE**3) ** 0.2
SHIFT = math.log2(STRETCH)
QUARTIC = (SMOOTH[0] * STRETCH**2, SMOOTH[1] * STRETCH**4, SMOOTH[2] * STRETCH)
LEVEL = SMOOTH[3] / SCALE**3
HALF_CONST = 0.5 * (SHIFT - SCALE * SCALE * SOFT_SQUARE)

FEATURES = 32
SOURCES = 16


def round_up(value, step):
    return -(-value // step) * step


def mul_t(left, right, precision=None):
    return lax.dot_general(
        left, right, (((1,), (1,)), ((), ())), precision=precision, preferred_element_type=F32
    )


def mul(left, right, precision=None):
    return lax.dot_general(
        left, right, (((1,), (0,)), ((), ())), precision=precision, preferred_element_type=F32
    )


def split(value, count):
    pieces = []
    for _ in range(count - 1):
        piece = value.astype(BF16).astype(F32)
        pieces.append(piece)
        value = value - piece
    pieces.append(value.astype(BF16).astype(F32))
    return pieces


class Brick:
    def __init__(self, shape, n_space, n_sub):
        self.bx, self.by, self.bz, self.atoms = shape
        self.n_space, self.n_sub = n_space, n_sub
        self.cols = self.bx * self.by
        self.lanes = self.bz * self.atoms
        self.wide = (self.bz + 2) * self.atoms
        self.px = POINTS * self.bx + 3
        self.py = round_up(POINTS * (self.by - 1) + 8, 8)
        self.pz = POINTS * self.bz
        self.zpad = round_up(self.pz, 16)
        self.group = 128 // self.zpad
        self.atom_rows = 4 * self.cols
        self.blocks = -(-self.px // self.group)
        self.msg_rows = round_up(self.atom_rows, 8) + self.py
        self.msg_lanes = max(self.lanes, self.blocks * 128)
        self.grid_row = round_up(self.atom_rows, 8)
        self.ci = 2 * self.bx + 2
        self.cj = 2 * self.by + 2
        self.ck = 2 * self.bz
        self.coarse_rows = round_up(self.ci, 8)
        self.coarse_lanes = round_up(self.cj * self.ck, 128)
        self.own_rows = round_up(self.cols, 8)
        self.columns = [
            (x, y) for x in range(-1, self.bx + 1) for y in range(-1, self.by + 1)
        ]
        self.ext_rows = round_up(len(self.columns), 8)
        self.kept = 2 * self.atoms * (1 + self.bz * (self.cols - 1))
        self.force_rows = round_up(3 * self.cols, 8)

    def col(self, x, y):
        return x * self.by + y


def spline(shifted):
    size = jnp.abs(shifted)
    outer = jnp.maximum(2.0 - size, 0.0)
    inner = jnp.maximum(1.0 - size, 0.0)
    return (outer * outer * outer) * (1.0 / 6.0) - (inner * inner * inner) * (4.0 / 6.0)


def spline_slope(shifted):
    size = jnp.abs(shifted)
    outer = jnp.maximum(2.0 - size, 0.0)
    inner = jnp.maximum(1.0 - size, 0.0)
    slope = 2.0 * (inner * inner) - 0.5 * (outer * outer)
    return jnp.where(shifted < 0.0, -slope, slope)


def shift_xy(brick, row):
    entry = lax.broadcasted_iota(jnp.int32, (8, brick.lanes), 0).astype(F32)
    return POINTS * row - (entry - 1.0)


def shift_z(brick, row):
    parts = []
    for cell in range(brick.bz):
        point = lax.broadcasted_iota(jnp.int32, (brick.zpad, brick.atoms), 0)
        entry = lax.rem(point - POINTS * cell + 1 + brick.pz, brick.pz) - 1
        entry = jnp.where(point < brick.pz, entry, 100)
        value = row[:, cell * brick.atoms : (cell + 1) * brick.atoms]
        parts.append(POINTS * value - entry.astype(F32))
    return jnp.concatenate(parts, axis=1)


def spread_kernel(brick, *refs):
    inputs, (msg_ref, coarse_ref), held = refs[0:3], refs[3:5], refs[5:8]
    grid_ref, arrived = refs[8:]
    counts_ref, pos_ref, charge_ref = held
    copies = [
        pltpu.make_async_copy(source, target, arrived.at[number])
        for number, (source, target) in enumerate(zip(inputs, held))
    ]
    for copy in copies:
        copy.start()
    grid_ref[...] = jnp.zeros(grid_ref.shape, F32)
    for copy in copies:
        copy.wait()
    atoms = brick.atoms
    lane = lax.broadcasted_iota(jnp.int32, (1, atoms), 1)
    for x in range(brick.bx):
        for y in range(brick.by):
            col = brick.col(x, y)
            for z in range(brick.bz):
                span = slice(z * atoms, (z + 1) * atoms)
                for comp in range(3):
                    row = comp * brick.cols + col
                    msg_ref[row : row + 1, span] = pos_ref[comp, x, z, y : y + 1, :]
                row = 3 * brick.cols + col
                charge = charge_ref[x, z, y : y + 1, :]
                msg_ref[row : row + 1, span] = jnp.where(lane < counts_ref[x, y, z], charge, 0.0)
    for x in range(brick.bx):
        for y in range(brick.by):
            col = brick.col(x, y)
            rows = [
                msg_ref[k * brick.cols + col : k * brick.cols + col + 1, 0 : brick.lanes]
                for k in range(4)
            ]
            along_x = spline(shift_xy(brick, rows[0])) * rows[3]
            along_y = spline(shift_xy(brick, rows[1]))
            along_z = spline(shift_z(brick, rows[2]))
            outer = jnp.concatenate(
                [along_x[e : e + 1, :] * along_y for e in range(TAPS)], axis=0
            )
            count = outer.shape[0]
            outer = jnp.concatenate(split(outer, 2), axis=0).astype(BF16)
            table = jnp.concatenate(split(along_z, 2), axis=0).astype(BF16)
            box = mul_t(outer, table)
            box = (
                box[:count, : brick.zpad] + box[:count, brick.zpad :] + box[count:, : brick.zpad]
            )
            for e in range(TAPS):
                place = (POINTS * x + e, slice(POINTS * y, POINTS * y + 8), slice(0, brick.zpad))
                grid_ref[place] = grid_ref[place] + box[8 * e : 8 * e + 8, :]
    for block in range(brick.msg_lanes // 128):
        total = jnp.zeros((brick.py, 128), F32)
        for spot in range(brick.group):
            x = block * brick.group + spot
            if x < brick.px:
                plane = grid_ref[x]
                total = total + (pltpu.roll(plane, spot * brick.zpad, 1) if spot else plane)
        msg_ref[brick.grid_row :, block * 128 : (block + 1) * 128] = total
    planes = []
    for idx in range(brick.ci):
        inside = [x for x in (2 * idx - 1, 2 * idx) if 0 <= x < brick.px]
        planes.append(sum(grid_ref[x, :, 0 : brick.zpad] for x in inside))
    stacked = jnp.concatenate(planes, axis=0)
    shape = (brick.zpad, brick.coarse_lanes)
    z_idx = lax.broadcasted_iota(jnp.int32, shape, 0)
    z_lane = lax.broadcasted_iota(jnp.int32, shape, 1)
    used = z_lane < brick.cj * brick.ck
    pairs = (z_idx // 2 == z_lane % brick.ck) & used & (z_idx < brick.pz)
    folded = mul(stacked, jnp.where(pairs, 0.125, 0.0).astype(F32), HIGHEST)
    shape = (brick.py, brick.coarse_lanes)
    y_idx = lax.broadcasted_iota(jnp.int32, shape, 0)
    y_lane = lax.broadcasted_iota(jnp.int32, shape, 1)
    mask = (y_lane // brick.ck == (y_idx + 1) // 2).astype(F32)
    sums = [
        jnp.sum(folded[i * brick.py : (i + 1) * brick.py] * mask, axis=0, keepdims=True)
        for i in range(brick.ci)
    ]
    if brick.coarse_rows > brick.ci:
        sums.append(jnp.zeros((brick.coarse_rows - brick.ci, brick.coarse_lanes), F32))
    coarse_ref[...] = jnp.broadcast_to(jnp.concatenate(sums, axis=0)[None], coarse_ref.shape)


def store_pieces(piece_ref, rows, arrays):
    for number, value in enumerate(arrays):
        for block in range(piece_ref.shape[0]):
            piece_ref[block, number * rows : (number + 1) * rows, :] = value[
                :, block * 128 : (block + 1) * 128
            ]


def load_pieces(piece_ref, rows, row, count):
    parts = [
        piece_ref[block, pl.ds(row, count, stride=rows), :] for block in range(piece_ref.shape[0])
    ]
    return jnp.concatenate(parts, axis=1)


def feature_arrays(coords, square, order, square_first):
    rows = coords[0].shape
    arrays = []
    for value in coords:
        pieces = split(value, 3)
        arrays += [pieces[piece] for piece in order]
    squares = split(square, 3)
    ones = [jnp.ones(rows, F32)] * 3
    arrays += squares + ones if square_first else ones + squares
    return arrays + [jnp.zeros(rows, F32)] * (FEATURES - len(arrays))


def source_arrays(coords, charge):
    arrays = []
    for value in [charge] + [charge * coord for coord in coords]:
        arrays += split(value, 3)
    return arrays + [jnp.zeros(charge.shape, F32)] * (SOURCES - len(arrays))


def minus_square(coords):
    return HALF_CONST - (coords[0] * coords[0] + coords[1] * coords[1] + coords[2] * coords[2])


def pair_factor(left, right):
    power = mul(left, right)
    inverse = lax.rsqrt(SHIFT - power)
    base = jnp.exp2(power)
    square = base * base
    smooth = ((square + QUARTIC[0]) * square + QUARTIC[1]) * (base + QUARTIC[2])
    factor = inverse * (inverse * inverse) - smooth
    high = factor.astype(BF16)
    low = (factor - high.astype(F32)).astype(BF16)
    return high, low


def moments(total, quantity):
    base = 3 * quantity
    return total[base : base + 1] + total[base + 1 : base + 2] + total[base + 2 : base + 3]


def pairs_kernel(brick, sender, n_msgs, *refs):
    atoms, lanes = brick.atoms, brick.lanes
    msg_ref = refs[0]
    other_msgs = refs[1 : 1 + n_msgs]
    force_ref = refs[1 + n_msgs]
    (
        row_ref,
        other_piece_ref,
        source_piece_ref,
        own_piece_ref,
        own_source_ref,
        left_ref,
        source_ref,
        right_ref,
        back_ref,
        total_ref,
        kept_ref,
    ) = refs[2 + n_msgs :]
    half = 0.5 * brick.bz

    rows = brick.ext_rows
    if rows > len(brick.columns):
        row_ref[...] = jnp.zeros(row_ref.shape, F32)
    for place, (x, y) in enumerate(brick.columns):
        shift = (x // brick.bx, y // brick.by)
        col = brick.col(x % brick.bx, y % brick.by)
        for k in range(4):
            near = slice(k * brick.cols + col, k * brick.cols + col + 1)
            if shift == (0, 0):
                value = msg_ref[near, 0:lanes]
            else:
                value = other_msgs[sender[shift]][near, 0:lanes]
            row_ref[k * rows + place : k * rows + place + 1, :] = value
    index = lax.broadcasted_iota(jnp.int32, (rows, 1), 0)
    ext_y = brick.by + 2
    offset_x = (index // ext_y - 1).astype(F32) - 0.5 * brick.bx
    offset_y = (index % ext_y - 1).astype(F32) - 0.5 * brick.by
    lane_z = (lax.broadcasted_iota(jnp.int32, (1, lanes), 1) // atoms).astype(F32)
    coords = [
        (row_ref[0:rows, :] + offset_x) * SCALE,
        (row_ref[rows : 2 * rows, :] + offset_y) * SCALE,
        (row_ref[2 * rows : 3 * rows, :] + (lane_z - half)) * SCALE,
    ]
    charge = row_ref[3 * rows : 4 * rows, :]
    store_pieces(
        other_piece_ref,
        rows,
        feature_arrays(coords, minus_square(coords), (0, 1, 2, 0, 1, 0), False),
    )
    store_pieces(source_piece_ref, rows, source_arrays(coords, charge))
    level_sums = {}
    for place in range(len(brick.columns)):
        feature = load_pieces(other_piece_ref, rows, place, FEATURES)
        left_ref[place] = feature.T.astype(BF16)
        source = load_pieces(source_piece_ref, rows, place, SOURCES)
        for z in range(brick.bz):
            part = source[:, z * atoms : (z + 1) * atoms]
            level_sums[(place, z)] = -LEVEL * jnp.sum(part, axis=1, keepdims=True)
            part = part.astype(BF16)
            source_ref[place, z] = jnp.concatenate([part, part], axis=1)

    rows = brick.own_rows
    own = []
    for k in range(4):
        value = msg_ref[k * brick.cols : (k + 1) * brick.cols, 0:lanes]
        if rows > brick.cols:
            value = jnp.concatenate([value, jnp.zeros((rows - brick.cols, lanes), F32)], axis=0)
        own.append(value)
    index = lax.broadcasted_iota(jnp.int32, (rows, 1), 0)
    own_x = (own[0] + ((index // brick.by).astype(F32) - 0.5 * brick.bx)) * SCALE
    own_y = (own[1] + ((index % brick.by).astype(F32) - 0.5 * brick.by)) * SCALE
    own_z_coords = []
    for other_z in range(brick.bz):
        step = other_z - lane_z
        step = jnp.where(step > half, step - brick.bz, step)
        step = jnp.where(step < -half, step + brick.bz, step)
        own_z_coords.append((own[2] + (other_z - step - half)) * SCALE)
        coords = [own_x, own_y, own_z_coords[-1]]
        arrays = feature_arrays(coords, minus_square(coords), (0, 0, 0, 1, 1, 2), True)
        arrays = [2.0 * value for value in arrays[:18]] + arrays[18:]
        store_pieces(own_piece_ref, rows, arrays)
        store_pieces(own_source_ref, rows, source_arrays(coords, own[3]))
        for col in range(brick.cols):
            part = load_pieces(own_piece_ref, rows, col, FEATURES)
            right_ref[col, other_z] = part.astype(BF16)
            part = load_pieces(own_source_ref, rows, col, SOURCES).astype(BF16)
            for z in range(brick.bz):
                cell = part[:, z * atoms : (z + 1) * atoms]
                back_ref[col, other_z, z] = jnp.concatenate([cell, cell], axis=1)

    cells = [(x, y) for x in range(brick.bx) for y in range(brick.by)]
    tiles = []
    for place, (x, y) in sorted(enumerate(brick.columns), key=lambda item: item[1] not in cells):
        home = cells.index((x, y)) if (x, y) in cells else None
        for z in range(brick.bz):
            for col, (cell_x, cell_y) in enumerate(cells):
                if max(abs(cell_x - x), abs(cell_y - y)) > 1 or (home is not None and col > home):
                    continue
                if col == home:
                    tiles.append((place, z, col, z, None))
                    tiles.append((place, z, col, (z + 1) % brick.bz, home))
                else:
                    tiles += [(place, z, col, own_z, home) for own_z in range(brick.bz)]

    for col in range(brick.cols):
        for z in range(brick.bz):
            for own_z in range(brick.bz):
                level = sum(
                    level_sums[(tile[0], z)] for tile in tiles if tile[1:4] == (z, col, own_z)
                )
                span = slice(own_z * atoms, (own_z + 1) * atoms)
                total_ref[col, z, :, span] = jnp.broadcast_to(level, (SOURCES, atoms))

    mirrors = {(col, z): [] for col in range(brick.cols) for z in range(brick.bz)}
    for place, z, col, own_z, home in tiles:
        span = slice(own_z * atoms, (own_z + 1) * atoms)
        left = left_ref[place, z * atoms : (z + 1) * atoms, :]
        high, low = pair_factor(left, right_ref[col, z, :, span])
        total_ref[col, z, :, span] += mul(
            source_ref[place, z], jnp.concatenate([high, low], axis=0)
        )
        if home is not None:
            spot = 2 * atoms * len(mirrors[(home, z)])
            mirrors[(home, z)].append((col, own_z))
            kept_ref[home, z, :, spot : spot + atoms] = high
            kept_ref[home, z, :, spot + atoms : spot + 2 * atoms] = low
    back_sums = {}
    for (col, z), found in mirrors.items():
        back = jnp.concatenate([back_ref[c, z, own_z] for c, own_z in found], axis=1)
        level = (-0.5 * LEVEL) * jnp.sum(back.astype(F32), axis=1, keepdims=True)
        back_sums[(col, z)] = mul_t(kept_ref[col, z, :, 0 : back.shape[1]], back).T + level

    for col in range(brick.cols):
        forces = [0.0, 0.0, 0.0]
        for z in range(brick.bz):
            total = total_ref[col, z]
            weight = moments(total, 0)
            for comp, coord in enumerate((own_x, own_y, own_z_coords[z])):
                value = coord[col : col + 1] * weight - moments(total, 1 + comp)
                forces[comp] = forces[comp] + value
        total = jnp.concatenate([back_sums[(col, z)] for z in range(brick.bz)], axis=1)
        weight = moments(total, 0)
        home = (own[2] + (lane_z - half)) * SCALE
        for comp, coord in enumerate((own_x, own_y, home)):
            row = comp * brick.cols + col
            value = coord[col : col + 1] * weight - moments(total, 1 + comp)
            value = value + forces[comp]
            force_ref[row : row + 1, :] = value * (own[3][col : col + 1] * (SCALE * SCALE))


def fine_tables(brick):
    ext_x = brick.px + 2 * REACH
    rows_y = brick.py + POINTS * brick.by
    out_lanes = brick.blocks * 128
    in_lanes = round_up(max(ext_x * brick.zpad, out_lanes), 128)
    count = len(FINE_WIDTHS)
    along_xz = np.zeros((in_lanes, count * out_lanes), np.float32)
    along_y = np.zeros((brick.py, count * rows_y), np.float32)

    def tap(dist, width):
        return np.where(np.abs(dist) <= REACH, np.exp(-(dist * dist) / (2.0 * width * width)), 0.0)

    for number, (width, weight) in enumerate(zip(FINE_WIDTHS, FINE_WEIGHTS)):
        mat_z = np.zeros((brick.zpad, brick.zpad))
        for step in range(-REACH, REACH + 1):
            for z in range(brick.pz):
                mat_z[(z + step) % brick.pz, z] += weight * tap(np.float64(step), width)
        mat_x = tap(np.arange(ext_x)[:, None] - np.arange(brick.px)[None, :] - REACH, width)
        dense = np.kron(mat_x, mat_z)
        along_xz[: dense.shape[0], number * out_lanes : number * out_lanes + dense.shape[1]] = dense
        out_y = np.arange(POINTS * brick.by + 3) - 1.0
        in_y = np.arange(rows_y) - 1.0 - POINTS * brick.by
        along_y[: len(out_y), number * rows_y : (number + 1) * rows_y] = tap(
            out_y[:, None] - in_y[None, :], width
        )
    return along_xz, along_y


def coarse_table(brick):
    table = np.zeros((len(COARSE_WEIGHTS) * brick.coarse_lanes, 128), np.float32)
    length = brick.ck
    for number, (fraction, weight) in enumerate(zip(COARSE_FRACTIONS, COARSE_WEIGHTS)):
        width = length / fraction
        for row in range(brick.cj * brick.ck):
            for z in range(brick.pz):
                dist = (row - z // 2) % length
                dist = min(dist, length - dist)
                table[number * brick.coarse_lanes + row, z] = weight * math.exp(
                    -(dist * dist) / (2.0 * width * width)
                )
    return table


def gauss(row, col, length, fraction):
    dist = lax.rem(row - col + 2 * length, length)
    dist = jnp.minimum(dist, length - dist).astype(F32)
    width = length / fraction
    return jnp.exp(dist * dist * (-1.0 / (2.0 * width * width)))


def potential_kernel(brick, sender, n_msgs, *refs):
    atoms = brick.atoms
    place_ref, msg_ref = refs[0:2]
    other_msgs = refs[2 : 2 + n_msgs]
    (
        whole_ref,
        short_ref,
        xz_high_ref,
        xz_low_ref,
        y_ref,
        coarse_z_ref,
        out_ref,
        pot_ref,
    ) = refs[2 + n_msgs :]
    step_y = POINTS * brick.by
    rows_y = brick.py + step_y
    in_lanes = xz_high_ref.shape[0]
    out_lanes = brick.blocks * 128
    grid = None
    for dx in (-1, 0, 1):
        grids = []
        for dy in (-1, 0, 1):
            near = slice(brick.grid_row, brick.msg_rows)
            span = slice(0, out_lanes)
            if (dx, dy) == (0, 0):
                grids.append(msg_ref[near, span])
            else:
                grids.append(other_msgs[sender[(dx, dy)]][near, span])
        tiles = [None] * ((brick.py + 2 * step_y) // 8)
        for number, part in enumerate(grids):
            for tile in range(brick.py // 8):
                spot = tile + number * step_y // 8
                value = part[8 * tile : 8 * tile + 8]
                tiles[spot] = value if tiles[spot] is None else tiles[spot] + value
        column = jnp.concatenate(tiles[: rows_y // 8], axis=0)
        if in_lanes > out_lanes:
            column = jnp.concatenate(
                [column, jnp.zeros((rows_y, in_lanes - out_lanes), F32)], axis=1
            )
        shift = (REACH + POINTS * brick.bx * dx) * brick.zpad
        column = pltpu.roll(column, shift % in_lanes, 1)
        grid = column if grid is None else grid + column
    pieces = jnp.concatenate(split(grid, 2), axis=0).astype(BF16)
    mixed = mul(pieces, xz_high_ref[...]) + mul(pieces, xz_low_ref[...])
    mixed = mixed[:rows_y] + mixed[rows_y:]
    mixed = jnp.concatenate(
        [mixed[:, n * out_lanes : (n + 1) * out_lanes] for n in range(len(FINE_WIDTHS))], axis=0
    )
    fine = mul(y_ref[...], mixed, HIGHEST)

    total_x = 2 * brick.bx * brick.n_space
    total_y = 2 * brick.by * brick.n_sub
    first_x = place_ref[0] * (2 * brick.bx)
    first_y = place_ref[1] * (2 * brick.by)
    out_rows = round_up(brick.px, 8)
    shape = (out_rows, brick.n_space * brick.coarse_rows)
    point = lax.broadcasted_iota(jnp.int32, shape, 0)
    lane = lax.broadcasted_iota(jnp.int32, shape, 1)
    row_x = first_x + (point + 1) // 2 - 1
    col_x = lane // brick.coarse_rows * (2 * brick.bx) + lane % brick.coarse_rows - 1
    live = lane % brick.coarse_rows < brick.ci
    mats_x = jnp.concatenate(
        [
            jnp.where(live, gauss(row_x, col_x, total_x, fraction), 0.0)
            for fraction in COARSE_FRACTIONS
        ],
        axis=0,
    )
    shape = (brick.py, brick.coarse_lanes)
    point = lax.broadcasted_iota(jnp.int32, shape, 0)
    lane = lax.broadcasted_iota(jnp.int32, shape, 1)
    row_y = first_y + (point + 1) // 2 - 1
    live = lane < brick.cj * brick.ck
    lefts = [[None] * brick.px for _ in COARSE_FRACTIONS]
    for sub in range(brick.n_sub):
        part = whole_ref[:, sub].reshape(
            brick.n_space * brick.coarse_rows, brick.coarse_lanes
        )
        mixed = mul(mats_x, part, HIGHEST)
        col_y = sub * (2 * brick.by) + lane // brick.ck - 1
        for number, fraction in enumerate(COARSE_FRACTIONS):
            mat_y = jnp.where(live, gauss(row_y, col_y, total_y, fraction), 0.0)
            for x in range(brick.px):
                row = number * out_rows + x
                value = mixed[row : row + 1] * mat_y
                done = lefts[number][x]
                lefts[number][x] = value if done is None else done + value
    left = jnp.concatenate([jnp.concatenate(rows, axis=0) for rows in lefts], axis=1)
    coarse = mul(left, coarse_z_ref[...], HIGHEST)
    lane = lax.broadcasted_iota(jnp.int32, (brick.py, 128), 1)
    for x in range(brick.px):
        block, shift = divmod(x, brick.group)
        value = fine[:, block * 128 : (block + 1) * 128]
        if shift:
            value = pltpu.roll(value, 128 - shift * brick.zpad, 1)
        value = value + coarse[x * brick.py : (x + 1) * brick.py]
        high, low = split(jnp.where(lane < brick.zpad, value, 0.0), 2)
        pot_ref[x] = (
            high + pltpu.roll(high, brick.zpad, 1) + pltpu.roll(low, 2 * brick.zpad, 1)
        )

    for x in range(brick.bx):
        for y in range(brick.by):
            col = brick.col(x, y)
            rows = [
                msg_ref[k * brick.cols + col : k * brick.cols + col + 1, 0 : brick.lanes]
                for k in range(4)
            ]
            shifted = [
                shift_xy(brick, rows[0]),
                shift_xy(brick, rows[1]),
                shift_z(brick, rows[2]),
            ]
            weights = [spline(value) for value in shifted]
            slopes = [spline_slope(value) for value in shifted]
            box = jnp.concatenate(
                [
                    pot_ref[POINTS * x + e, POINTS * y : POINTS * y + 8, 0 : 3 * brick.zpad]
                    for e in range(TAPS)
                ],
                axis=0,
            )
            high, low = split(jnp.concatenate([weights[2], slopes[2]], axis=1), 2)
            tables = jnp.concatenate([high, low, high], axis=0).astype(BF16)
            both = mul(box.astype(BF16), tables)
            along_z = both[:, : brick.lanes]
            sloped_z = both[:, brick.lanes :]
            sums = [0.0, 0.0, 0.0]
            for e in range(TAPS):
                weight = weights[0][e : e + 1]
                slope = slopes[0][e : e + 1]
                flat = along_z[8 * e : 8 * e + 8]
                steep = sloped_z[8 * e : 8 * e + 8]
                sums[0] = sums[0] + flat * slope
                sums[1] = sums[1] + flat * weight
                sums[2] = sums[2] + steep * weight
            across = (weights[1], slopes[1], weights[1])
            for comp in range(3):
                force = jnp.sum(sums[comp] * across[comp], axis=0, keepdims=True)
                row = comp * brick.cols + col
                force = short_ref[row : row + 1, :] - POINTS * (rows[3] * force)
                for z in range(brick.bz):
                    out_ref[comp, x, z, y : y + 1, :] = force[:, z * atoms : (z + 1) * atoms]


VMEM = pl.BlockSpec(memory_space=pltpu.VMEM)
SMEM = pl.BlockSpec(memory_space=pltpu.SMEM)
ANY = pl.BlockSpec(memory_space=pl.ANY)
WHOLE = pl.BlockSpec()


def call(kernel, out_shape, in_specs, scratch, flops, *args, out_spec=VMEM, grant=40):
    single = not isinstance(out_shape, (list, tuple))
    return pl.pallas_call(
        kernel,
        out_shape=out_shape,
        in_specs=in_specs,
        out_specs=out_spec if single else [out_spec] * len(out_shape),
        scratch_shapes=scratch,
        compiler_params=pltpu.CompilerParams(vmem_limit_bytes=grant * 1024 * 1024),
        cost_estimate=pl.CostEstimate(flops=flops, bytes_accessed=10**5, transcendentals=0),
    )(*args)


def neighbours(brick, msg):
    size, wide = brick.n_space, brick.n_sub
    found = {}
    sender = {}
    msgs = []
    for dx in (1, 0, -1):
        for dy in (0, -1, 1):
            if (dx, dy) == (0, 0):
                continue
            key = (dx % size, dy % wide)
            if key not in found:
                found[key] = len(msgs)
                pairs = [
                    ((i + dx) % size * wide + (j + dy) % wide, i * wide + j)
                    for i in range(size)
                    for j in range(wide)
                ]
                msgs.append(lax.ppermute(msg, ("space", "sub"), pairs))
            sender[(dx, dy)] = found[key]
    return sender, msgs


def body(n_space, n_sub, positions, charges, counts):
    brick = Brick(charges.shape, n_space, n_sub)
    n_dev = n_space * n_sub
    along_xz, along_y = fine_tables(brick)
    xz_high = along_xz.astype(BF16)
    xz_low = (along_xz - xz_high.astype(np.float32)).astype(BF16)
    coarse_z = coarse_table(brick)
    place = jnp.stack([lax.axis_index("space"), lax.axis_index("sub")]).astype(jnp.int32)

    turned = (positions.transpose(0, 1, 3, 2, 4), charges.transpose(0, 2, 1, 3))
    msg, coarse = call(
        functools.partial(spread_kernel, brick),
        [
            jax.ShapeDtypeStruct((brick.msg_rows, brick.msg_lanes), F32),
            jax.ShapeDtypeStruct((n_dev, brick.coarse_rows, brick.coarse_lanes), F32),
        ],
        [ANY, ANY, ANY],
        [
            pltpu.SMEM(counts.shape, jnp.int32),
            pltpu.VMEM(turned[0].shape, F32),
            pltpu.VMEM(turned[1].shape, F32),
            pltpu.VMEM((brick.px, brick.py, 128), F32),
            pltpu.SemaphoreType.DMA((3,)),
        ],
        10**7,
        counts,
        *turned,
        grant=64,
    )
    sender, msgs = neighbours(brick, msg)
    whole = lax.all_to_all(coarse, ("space", "sub"), 0, 0, tiled=True)
    whole = whole.reshape(n_space, n_sub, brick.coarse_rows, brick.coarse_lanes)

    n_col = len(brick.columns)
    short = call(
        functools.partial(pairs_kernel, brick, sender, len(msgs)),
        jax.ShapeDtypeStruct((brick.force_rows, brick.lanes), F32),
        [VMEM] * (1 + len(msgs)),
        [
            pltpu.VMEM((4 * brick.ext_rows, brick.lanes), F32),
            pltpu.VMEM((brick.lanes // 128, FEATURES * brick.ext_rows, 128), F32),
            pltpu.VMEM((brick.lanes // 128, SOURCES * brick.ext_rows, 128), F32),
            pltpu.VMEM((brick.lanes // 128, FEATURES * brick.own_rows, 128), F32),
            pltpu.VMEM((brick.lanes // 128, SOURCES * brick.own_rows, 128), F32),
            pltpu.VMEM((n_col, brick.lanes, FEATURES), BF16),
            pltpu.VMEM((n_col, brick.bz, SOURCES, 2 * brick.atoms), BF16),
            pltpu.VMEM((brick.cols, brick.bz, FEATURES, brick.lanes), BF16),
            pltpu.VMEM((brick.cols, brick.bz, brick.bz, SOURCES, 2 * brick.atoms), BF16),
            pltpu.VMEM((brick.cols, brick.bz, SOURCES, brick.lanes), F32),
            pltpu.VMEM((brick.cols, brick.bz, brick.atoms, brick.kept), BF16),
        ],
        10**10,
        msg,
        *msgs,
    )
    comps, size_x, size_y, size_z, atoms = positions.shape
    forces = call(
        functools.partial(potential_kernel, brick, sender, len(msgs)),
        jax.ShapeDtypeStruct((comps, size_x, size_z, size_y, atoms), F32),
        [SMEM] + [VMEM] * (7 + len(msgs)),
        [
            pltpu.VMEM((brick.px, brick.py, 128), F32),
        ],
        10**8,
        place,
        msg,
        *msgs,
        whole,
        short,
        xz_high,
        xz_low,
        jnp.asarray(along_y),
        jnp.asarray(coarse_z),
        out_spec=WHOLE,
    )
    return forces.transpose(0, 1, 3, 2, 4)


def solution(mesh):
    in_specs = (
        P(None, "space", "sub", None, None),
        P("space", "sub", None, None),
        P("space", "sub", None),
    )
    out_specs = P(None, "space", "sub", None, None)
    run = functools.partial(body, mesh.shape["space"], mesh.shape["sub"])
    return jax.shard_map(run, mesh=mesh, in_specs=in_specs, out_specs=out_specs, check_vma=False)
```

```python
import functools
import math

import jax
import jax.numpy as jnp
import numpy as np
from jax import lax
from jax.experimental import pallas as pl
from jax.experimental.pallas import tpu as pltpu
from jax.sharding import PartitionSpec as P

F32 = jnp.float32
BF16 = jnp.bfloat16
HIGHEST = lax.Precision.HIGHEST

POINTS = 4
REACH = 4
TAPS = POINTS + 3
SOFT_SQUARE = 0.0625
FINE_WIDTHS = (1.0, 2.0)
FINE_WEIGHTS = (2.0, 0.5)
COARSE_FRACTIONS = (8.0, 4.0)
COARSE_WEIGHTS = (4.0, 2.0)

DECAY = 0.11446730730706552
LEAD = 0.13637726630426547
SMOOTH = (1.0312317180277653, 0.44426879021665455, 0.1544174241571791, -0.004580112368867706)
SCALE = math.sqrt(DECAY * math.log2(math.e))
STRETCH = (LEAD / SCALE**3) ** 0.2
SHIFT = math.log2(STRETCH)
QUARTIC = (SMOOTH[0] * STRETCH**2, SMOOTH[1] * STRETCH**4, SMOOTH[2] * STRETCH)
LEVEL = SMOOTH[3] / SCALE**3
HALF_CONST = 0.5 * (SHIFT - SCALE * SCALE * SOFT_SQUARE)

FEATURES = 32
SOURCES = 16


def round_up(value, step):
    return -(-value // step) * step


def mul_t(left, right, precision=None):
    return lax.dot_general(
        left, right, (((1,), (1,)), ((), ())), precision=precision, preferred_element_type=F32
    )


def mul(left, right, precision=None):
    return lax.dot_general(
        left, right, (((1,), (0,)), ((), ())), precision=precision, preferred_element_type=F32
    )


def split(value, count):
    pieces = []
    for _ in range(count - 1):
        piece = value.astype(BF16).astype(F32)
        pieces.append(piece)
        value = value - piece
    pieces.append(value.astype(BF16).astype(F32))
    return pieces


class Brick:
    def __init__(self, shape, n_space, n_sub):
        self.bx, self.by, self.bz, self.atoms = shape
        self.n_space, self.n_sub = n_space, n_sub
        self.cols = self.bx * self.by
        self.lanes = self.bz * self.atoms
        self.wide = (self.bz + 2) * self.atoms
        self.px = POINTS * self.bx + 3
        self.py = round_up(POINTS * (self.by - 1) + 8, 8)
        self.pz = POINTS * self.bz
        self.zpad = round_up(self.pz, 16)
        self.group = 128 // self.zpad
        self.atom_rows = 4 * self.cols
        self.blocks = -(-self.px // self.group)
        self.msg_rows = round_up(self.atom_rows, 8) + self.py
        self.msg_lanes = max(self.lanes, self.blocks * 128)
        self.grid_row = round_up(self.atom_rows, 8)
        self.ci = 2 * self.bx + 2
        self.cj = 2 * self.by + 2
        self.ck = 2 * self.bz
        self.coarse_rows = round_up(self.ci, 8)
        self.coarse_lanes = round_up(self.cj * self.ck, 128)
        self.own_rows = round_up(self.cols, 8)
        self.columns = [
            (x, y) for x in range(-1, self.bx + 1) for y in range(-1, self.by + 1)
        ]
        self.ext_rows = round_up(len(self.columns), 8)
        self.kept = 2 * self.atoms * (1 + self.bz * (self.cols - 1))
        self.force_rows = round_up(3 * self.cols, 8)

    def col(self, x, y):
        return x * self.by + y


def spline(shifted):
    size = jnp.abs(shifted)
    outer = jnp.maximum(2.0 - size, 0.0)
    inner = jnp.maximum(1.0 - size, 0.0)
    return (outer * outer * outer) * (1.0 / 6.0) - (inner * inner * inner) * (4.0 / 6.0)


def spline_slope(shifted):
    size = jnp.abs(shifted)
    outer = jnp.maximum(2.0 - size, 0.0)
    inner = jnp.maximum(1.0 - size, 0.0)
    slope = 2.0 * (inner * inner) - 0.5 * (outer * outer)
    return jnp.where(shifted < 0.0, -slope, slope)


def shift_xy(brick, row):
    entry = lax.broadcasted_iota(jnp.int32, (8, brick.lanes), 0).astype(F32)
    return POINTS * row - (entry - 1.0)


def shift_z(brick, row):
    parts = []
    for cell in range(brick.bz):
        point = lax.broadcasted_iota(jnp.int32, (brick.zpad, brick.atoms), 0)
        entry = lax.rem(point - POINTS * cell + 1 + brick.pz, brick.pz) - 1
        entry = jnp.where(point < brick.pz, entry, 100)
        value = row[:, cell * brick.atoms : (cell + 1) * brick.atoms]
        parts.append(POINTS * value - entry.astype(F32))
    return jnp.concatenate(parts, axis=1)


def spread_kernel(brick, *refs):
    inputs, outputs, held = refs[0:3], refs[3:5], refs[5:8]
    msg_ref, coarse_ref, grid_ref, arrived, sent = refs[8:]
    counts_ref, pos_ref, charge_ref = held
    copies = [
        pltpu.make_async_copy(source, target, arrived.at[number])
        for number, (source, target) in enumerate(zip(inputs, held))
    ]
    for copy in copies:
        copy.start()
    grid_ref[...] = jnp.zeros(grid_ref.shape, F32)
    for copy in copies:
        copy.wait()
    atoms = brick.atoms
    lane = lax.broadcasted_iota(jnp.int32, (1, atoms), 1)
    for x in range(brick.bx):
        for y in range(brick.by):
            col = brick.col(x, y)
            for z in range(brick.bz):
                span = slice(z * atoms, (z + 1) * atoms)
                for comp in range(3):
                    row = comp * brick.cols + col
                    msg_ref[row : row + 1, span] = pos_ref[comp, x, z, y : y + 1, :]
                row = 3 * brick.cols + col
                charge = charge_ref[x, z, y : y + 1, :]
                msg_ref[row : row + 1, span] = jnp.where(lane < counts_ref[x, y, z], charge, 0.0)
    for x in range(brick.bx):
        for y in range(brick.by):
            col = brick.col(x, y)
            rows = [
                msg_ref[k * brick.cols + col : k * brick.cols + col + 1, 0 : brick.lanes]
                for k in range(4)
            ]
            along_x = spline(shift_xy(brick, rows[0])) * rows[3]
            along_y = spline(shift_xy(brick, rows[1]))
            along_z = spline(shift_z(brick, rows[2]))
            outer = jnp.concatenate(
                [along_x[e : e + 1, :] * along_y for e in range(TAPS)], axis=0
            )
            count = outer.shape[0]
            outer = jnp.concatenate(split(outer, 2), axis=0).astype(BF16)
            table = jnp.concatenate(split(along_z, 2), axis=0).astype(BF16)
            box = mul_t(outer, table)
            box = (
                box[:count, : brick.zpad] + box[:count, brick.zpad :] + box[count:, : brick.zpad]
            )
            for e in range(TAPS):
                place = (POINTS * x + e, slice(POINTS * y, POINTS * y + 8), slice(0, brick.zpad))
                grid_ref[place] = grid_ref[place] + box[8 * e : 8 * e + 8, :]
    for block in range(brick.msg_lanes // 128):
        total = jnp.zeros((brick.py, 128), F32)
        for spot in range(brick.group):
            x = block * brick.group + spot
            if x < brick.px:
                plane = grid_ref[x]
                total = total + (pltpu.roll(plane, spot * brick.zpad, 1) if spot else plane)
        msg_ref[brick.grid_row :, block * 128 : (block + 1) * 128] = total
    send_msg = pltpu.make_async_copy(msg_ref, outputs[0], sent.at[0])
    send_msg.start()
    planes = []
    for idx in range(brick.ci):
        inside = [x for x in (2 * idx - 1, 2 * idx) if 0 <= x < brick.px]
        planes.append(sum(grid_ref[x, :, 0 : brick.zpad] for x in inside))
    stacked = jnp.concatenate(planes, axis=0)
    shape = (brick.zpad, brick.coarse_lanes)
    z_idx = lax.broadcasted_iota(jnp.int32, shape, 0)
    z_lane = lax.broadcasted_iota(jnp.int32, shape, 1)
    used = z_lane < brick.cj * brick.ck
    pairs = (z_idx // 2 == z_lane % brick.ck) & used & (z_idx < brick.pz)
    folded = mul(stacked, jnp.where(pairs, 0.125, 0.0).astype(F32), HIGHEST)
    shape = (brick.py, brick.coarse_lanes)
    y_idx = lax.broadcasted_iota(jnp.int32, shape, 0)
    y_lane = lax.broadcasted_iota(jnp.int32, shape, 1)
    mask = (y_lane // brick.ck == (y_idx + 1) // 2).astype(F32)
    sums = [
        jnp.sum(folded[i * brick.py : (i + 1) * brick.py] * mask, axis=0, keepdims=True)
        for i in range(brick.ci)
    ]
    if brick.coarse_rows > brick.ci:
        sums.append(jnp.zeros((brick.coarse_rows - brick.ci, brick.coarse_lanes), F32))
    coarse_ref[...] = jnp.broadcast_to(jnp.concatenate(sums, axis=0)[None], coarse_ref.shape)
    send_coarse = pltpu.make_async_copy(coarse_ref, outputs[1], sent.at[1])
    send_coarse.start()
    send_msg.wait()
    send_coarse.wait()


def store_pieces(piece_ref, rows, arrays, first=0):
    for number, value in enumerate(arrays, first):
        for block in range(piece_ref.shape[0]):
            piece_ref[block, number * rows : (number + 1) * rows, :] = value[
                :, block * 128 : (block + 1) * 128
            ]


def load_pieces(piece_ref, rows, row, count, first=0):
    parts = [
        piece_ref[block, pl.ds(first * rows + row, count, stride=rows), :]
        for block in range(piece_ref.shape[0])
    ]
    return jnp.concatenate(parts, axis=1)


def product_pieces(value, order):
    pieces = split(value, 3)
    return [pieces[piece] for piece in order]


def source_arrays(coords, charge):
    arrays = []
    for value in [charge] + [charge * coord for coord in coords]:
        arrays += split(value, 3)
    return arrays + [jnp.zeros(charge.shape, F32)] * (SOURCES - len(arrays))


def minus_square(coords):
    return HALF_CONST - (coords[0] * coords[0] + coords[1] * coords[1] + coords[2] * coords[2])


def pair_factor(left, right):
    power = mul(left, right)
    inverse = lax.rsqrt(SHIFT - power)
    base = jnp.exp2(power)
    square = base * base
    smooth = ((square + QUARTIC[0]) * square + QUARTIC[1]) * (base + QUARTIC[2])
    factor = inverse * (inverse * inverse) - smooth
    high = factor.astype(BF16)
    low = (factor - high.astype(F32)).astype(BF16)
    return high, low


def moments(total, quantity):
    base = 3 * quantity
    return total[base : base + 1] + total[base + 1 : base + 2] + total[base + 2 : base + 3]


def pairs_kernel(brick, sender, n_msgs, *refs):
    atoms, lanes = brick.atoms, brick.lanes
    msg_ref = refs[0]
    other_msgs = refs[1 : 1 + n_msgs]
    force_ref = refs[1 + n_msgs]
    (
        row_ref,
        other_piece_ref,
        source_piece_ref,
        own_piece_ref,
        own_source_ref,
        left_ref,
        source_ref,
        right_ref,
        back_ref,
        total_ref,
        kept_ref,
    ) = refs[2 + n_msgs :]
    half = 0.5 * brick.bz

    rows = brick.ext_rows
    if rows > len(brick.columns):
        row_ref[...] = jnp.zeros(row_ref.shape, F32)
    for place, (x, y) in enumerate(brick.columns):
        shift = (x // brick.bx, y // brick.by)
        col = brick.col(x % brick.bx, y % brick.by)
        for k in range(4):
            near = slice(k * brick.cols + col, k * brick.cols + col + 1)
            if shift == (0, 0):
                value = msg_ref[near, 0:lanes]
            else:
                value = other_msgs[sender[shift]][near, 0:lanes]
            row_ref[k * rows + place : k * rows + place + 1, :] = value
    index = lax.broadcasted_iota(jnp.int32, (rows, 1), 0)
    ext_y = brick.by + 2
    offset_x = (index // ext_y - 1).astype(F32) - 0.5 * brick.bx
    offset_y = (index % ext_y - 1).astype(F32) - 0.5 * brick.by
    lane_z = (lax.broadcasted_iota(jnp.int32, (1, lanes), 1) // atoms).astype(F32)
    coords = [
        (row_ref[0:rows, :] + offset_x) * SCALE,
        (row_ref[rows : 2 * rows, :] + offset_y) * SCALE,
        (row_ref[2 * rows : 3 * rows, :] + (lane_z - half)) * SCALE,
    ]
    charge = row_ref[3 * rows : 4 * rows, :]
    order = (0, 1, 2, 0, 1, 0)
    zero = jnp.zeros((rows, lanes), F32)
    one = jnp.ones((rows, lanes), F32)
    arrays = product_pieces(coords[0], order) + product_pieces(coords[1], order)
    arrays += split(minus_square(coords), 3) + [zero]
    arrays += product_pieces(coords[2], order) + [one] * 3
    store_pieces(other_piece_ref, rows, arrays + [zero] * (FEATURES - len(arrays)))
    store_pieces(source_piece_ref, rows, source_arrays(coords, charge))
    level_sums = {}
    for place in range(len(brick.columns)):
        feature = load_pieces(other_piece_ref, rows, place, FEATURES)
        left_ref[place] = feature.T.astype(BF16)
        source = load_pieces(source_piece_ref, rows, place, SOURCES)
        for z in range(brick.bz):
            part = source[:, z * atoms : (z + 1) * atoms]
            level_sums[(place, z)] = -LEVEL * jnp.sum(part, axis=1, keepdims=True)
            part = part.astype(BF16)
            source_ref[place, z] = jnp.concatenate([part, part], axis=1)

    rows = brick.own_rows
    own = []
    for k in range(4):
        value = msg_ref[k * brick.cols : (k + 1) * brick.cols, 0:lanes]
        if rows > brick.cols:
            value = jnp.concatenate([value, jnp.zeros((rows - brick.cols, lanes), F32)], axis=0)
        own.append(value)
    index = lax.broadcasted_iota(jnp.int32, (rows, 1), 0)
    own_x = (own[0] + ((index // brick.by).astype(F32) - 0.5 * brick.bx)) * SCALE
    own_y = (own[1] + ((index % brick.by).astype(F32) - 0.5 * brick.by)) * SCALE
    order = (0, 0, 0, 1, 1, 2)
    zero = jnp.zeros((rows, lanes), F32)
    one = jnp.ones((rows, lanes), F32)
    fixed = product_pieces(2.0 * own_x, order) + product_pieces(2.0 * own_y, order)
    fixed += [one] * 3 + [zero]
    own_half = len(fixed)
    store_pieces(own_piece_ref, rows, fixed)
    store_pieces(own_piece_ref, rows, [zero] * (FEATURES - own_half - 9), own_half + 9)
    store_pieces(
        own_source_ref, rows, split(own[3], 3) + split(own[3] * own_x, 3) + split(own[3] * own_y, 3)
    )
    store_pieces(own_source_ref, rows, [zero] * (SOURCES - 12), 12)
    own_z_coords = []
    for other_z in range(brick.bz):
        step = other_z - lane_z
        step = jnp.where(step > half, step - brick.bz, step)
        step = jnp.where(step < -half, step + brick.bz, step)
        own_z = (own[2] + (other_z - step - half)) * SCALE
        own_z_coords.append(own_z)
        arrays = product_pieces(2.0 * own_z, order)
        arrays += split(minus_square([own_x, own_y, own_z]), 3)
        store_pieces(own_piece_ref, rows, arrays, own_half)
        store_pieces(own_source_ref, rows, split(own[3] * own_z, 3), 9)
        for col in range(brick.cols):
            if other_z == 0:
                part = load_pieces(own_piece_ref, rows, col, own_half).astype(BF16)
                for z in range(brick.bz):
                    right_ref[col, z, 0:own_half] = part
            part = load_pieces(own_piece_ref, rows, col, FEATURES - own_half, own_half)
            right_ref[col, other_z, own_half:] = part.astype(BF16)
            part = load_pieces(own_source_ref, rows, col, SOURCES).astype(BF16)
            for z in range(brick.bz):
                cell = part[:, z * atoms : (z + 1) * atoms]
                back_ref[col, other_z, z] = jnp.concatenate([cell, cell], axis=1)

    cells = [(x, y) for x in range(brick.bx) for y in range(brick.by)]
    tiles = []
    for place, (x, y) in sorted(enumerate(brick.columns), key=lambda item: item[1] not in cells):
        home = cells.index((x, y)) if (x, y) in cells else None
        for z in range(brick.bz):
            for col, (cell_x, cell_y) in enumerate(cells):
                if max(abs(cell_x - x), abs(cell_y - y)) > 1 or (home is not None and col > home):
                    continue
                if col == home:
                    tiles.append((place, z, col, z, None))
                    tiles.append((place, z, col, (z + 1) % brick.bz, home))
                else:
                    tiles += [(place, z, col, own_z, home) for own_z in range(brick.bz)]

    for col in range(brick.cols):
        for z in range(brick.bz):
            for own_z in range(brick.bz):
                level = sum(
                    level_sums[(tile[0], z)] for tile in tiles if tile[1:4] == (z, col, own_z)
                )
                span = slice(own_z * atoms, (own_z + 1) * atoms)
                total_ref[col, z, :, span] = jnp.broadcast_to(level, (SOURCES, atoms))

    mirrors = {(col, z): [] for col in range(brick.cols) for z in range(brick.bz)}
    for place, z, col, own_z, home in tiles:
        span = slice(own_z * atoms, (own_z + 1) * atoms)
        left = left_ref[place, z * atoms : (z + 1) * atoms, :]
        high, low = pair_factor(left, right_ref[col, z, :, span])
        total_ref[col, z, :, span] += mul(
            source_ref[place, z], jnp.concatenate([high, low], axis=0)
        )
        if home is not None:
            spot = 2 * atoms * len(mirrors[(home, z)])
            mirrors[(home, z)].append((col, own_z))
            kept_ref[home, z, :, spot : spot + atoms] = high
            kept_ref[home, z, :, spot + atoms : spot + 2 * atoms] = low
    back_sums = {}
    back_lifts = {}
    for (col, z), found in mirrors.items():
        back = jnp.concatenate([back_ref[c, z, own_z] for c, own_z in found], axis=1)
        level = 0.0
        lift = jnp.zeros((1, 1), F32)
        for c, own_z in found:
            value = level_sums[(brick.columns.index(cells[c]), own_z)]
            level = level + value
            turns = round((z - own_z) / brick.bz)
            if turns:
                lift = lift + (turns * brick.bz * SCALE) * moments(value, 0)
        back_sums[(col, z)] = mul_t(kept_ref[col, z, :, 0 : back.shape[1]], back).T + level
        back_lifts[(col, z)] = jnp.broadcast_to(lift, (1, atoms))

    for col in range(brick.cols):
        forces = [0.0, 0.0, 0.0]
        for z in range(brick.bz):
            total = total_ref[col, z]
            weight = moments(total, 0)
            for comp, coord in enumerate((own_x, own_y, own_z_coords[z])):
                value = coord[col : col + 1] * weight - moments(total, 1 + comp)
                forces[comp] = forces[comp] + value
        total = jnp.concatenate([back_sums[(col, z)] for z in range(brick.bz)], axis=1)
        weight = moments(total, 0)
        home = (own[2] + (lane_z - half)) * SCALE
        for comp, coord in enumerate((own_x, own_y, home)):
            row = comp * brick.cols + col
            value = coord[col : col + 1] * weight - moments(total, 1 + comp)
            if comp == 2:
                value = value - jnp.concatenate(
                    [back_lifts[(col, z)] for z in range(brick.bz)], axis=1
                )
            value = value + forces[comp]
            force_ref[row : row + 1, :] = value * (own[3][col : col + 1] * (SCALE * SCALE))


def fine_tables(brick):
    ext_x = brick.px + 2 * REACH
    rows_y = brick.py + POINTS * brick.by
    out_lanes = brick.blocks * 128
    in_lanes = round_up(max(ext_x * brick.zpad, out_lanes), 128)
    count = len(FINE_WIDTHS)
    along_xz = np.zeros((in_lanes, count * out_lanes), np.float32)
    along_y = np.zeros((brick.py, count * rows_y), np.float32)

    def tap(dist, width):
        return np.where(np.abs(dist) <= REACH, np.exp(-(dist * dist) / (2.0 * width * width)), 0.0)

    for number, (width, weight) in enumerate(zip(FINE_WIDTHS, FINE_WEIGHTS)):
        mat_z = np.zeros((brick.zpad, brick.zpad))
        for step in range(-REACH, REACH + 1):
            for z in range(brick.pz):
                mat_z[(z + step) % brick.pz, z] += weight * tap(np.float64(step), width)
        mat_x = tap(np.arange(ext_x)[:, None] - np.arange(brick.px)[None, :] - REACH, width)
        dense = np.kron(mat_x, mat_z)
        along_xz[: dense.shape[0], number * out_lanes : number * out_lanes + dense.shape[1]] = dense
        out_y = np.arange(POINTS * brick.by + 3) - 1.0
        in_y = np.arange(rows_y) - 1.0 - POINTS * brick.by
        along_y[: len(out_y), number * rows_y : (number + 1) * rows_y] = tap(
            out_y[:, None] - in_y[None, :], width
        )
    return along_xz, along_y


def coarse_table(brick):
    table = np.zeros((len(COARSE_WEIGHTS) * brick.coarse_lanes, 128), np.float32)
    length = brick.ck
    for number, (fraction, weight) in enumerate(zip(COARSE_FRACTIONS, COARSE_WEIGHTS)):
        width = length / fraction
        for row in range(brick.cj * brick.ck):
            for z in range(brick.pz):
                dist = (row - z // 2) % length
                dist = min(dist, length - dist)
                table[number * brick.coarse_lanes + row, z] = weight * math.exp(
                    -(dist * dist) / (2.0 * width * width)
                )
    return table


def gauss(row, col, length, fraction):
    dist = lax.rem(row - col + 2 * length, length)
    dist = jnp.minimum(dist, length - dist).astype(F32)
    width = length / fraction
    return jnp.exp(dist * dist * (-1.0 / (2.0 * width * width)))


def potential_kernel(brick, sender, n_msgs, *refs):
    atoms = brick.atoms
    place_ref, msg_ref = refs[0:2]
    other_msgs = refs[2 : 2 + n_msgs]
    (
        whole_ref,
        short_ref,
        xz_high_ref,
        xz_low_ref,
        y_ref,
        coarse_z_ref,
        out_ref,
        pot_ref,
    ) = refs[2 + n_msgs :]
    step_y = POINTS * brick.by
    rows_y = brick.py + step_y
    in_lanes = xz_high_ref.shape[0]
    out_lanes = brick.blocks * 128
    grid = None
    for dx in (-1, 0, 1):
        grids = []
        for dy in (-1, 0, 1):
            near = slice(brick.grid_row, brick.msg_rows)
            span = slice(0, out_lanes)
            if (dx, dy) == (0, 0):
                grids.append(msg_ref[near, span])
            else:
                grids.append(other_msgs[sender[(dx, dy)]][near, span])
        tiles = [None] * ((brick.py + 2 * step_y) // 8)
        for number, part in enumerate(grids):
            for tile in range(brick.py // 8):
                spot = tile + number * step_y // 8
                value = part[8 * tile : 8 * tile + 8]
                tiles[spot] = value if tiles[spot] is None else tiles[spot] + value
        column = jnp.concatenate(tiles[: rows_y // 8], axis=0)
        if in_lanes > out_lanes:
            column = jnp.concatenate(
                [column, jnp.zeros((rows_y, in_lanes - out_lanes), F32)], axis=1
            )
        shift = (REACH + POINTS * brick.bx * dx) * brick.zpad
        column = pltpu.roll(column, shift % in_lanes, 1)
        grid = column if grid is None else grid + column
    pieces = jnp.concatenate(split(grid, 2), axis=0).astype(BF16)
    mixed = mul(pieces, xz_high_ref[...]) + mul(pieces, xz_low_ref[...])
    mixed = mixed[:rows_y] + mixed[rows_y:]
    mixed = jnp.concatenate(
        [mixed[:, n * out_lanes : (n + 1) * out_lanes] for n in range(len(FINE_WIDTHS))], axis=0
    )
    fine = mul(y_ref[...], mixed, HIGHEST)

    total_x = 2 * brick.bx * brick.n_space
    total_y = 2 * brick.by * brick.n_sub
    first_x = place_ref[0] * (2 * brick.bx)
    first_y = place_ref[1] * (2 * brick.by)
    out_rows = round_up(brick.px, 8)
    shape = (out_rows, brick.n_space * brick.coarse_rows)
    point = lax.broadcasted_iota(jnp.int32, shape, 0)
    lane = lax.broadcasted_iota(jnp.int32, shape, 1)
    row_x = first_x + (point + 1) // 2 - 1
    col_x = lane // brick.coarse_rows * (2 * brick.bx) + lane % brick.coarse_rows - 1
    live = lane % brick.coarse_rows < brick.ci
    mats_x = jnp.concatenate(
        [
            jnp.where(live, gauss(row_x, col_x, total_x, fraction), 0.0)
            for fraction in COARSE_FRACTIONS
        ],
        axis=0,
    )
    shape = (brick.py, brick.coarse_lanes)
    point = lax.broadcasted_iota(jnp.int32, shape, 0)
    lane = lax.broadcasted_iota(jnp.int32, shape, 1)
    row_y = first_y + (point + 1) // 2 - 1
    live = lane < brick.cj * brick.ck
    lefts = [[None] * brick.px for _ in COARSE_FRACTIONS]
    for sub in range(brick.n_sub):
        part = whole_ref[:, sub].reshape(
            brick.n_space * brick.coarse_rows, brick.coarse_lanes
        )
        mixed = mul(mats_x, part, HIGHEST)
        col_y = sub * (2 * brick.by) + lane // brick.ck - 1
        for number, fraction in enumerate(COARSE_FRACTIONS):
            mat_y = jnp.where(live, gauss(row_y, col_y, total_y, fraction), 0.0)
            for x in range(brick.px):
                row = number * out_rows + x
                value = mixed[row : row + 1] * mat_y
                done = lefts[number][x]
                lefts[number][x] = value if done is None else done + value
    left = jnp.concatenate([jnp.concatenate(rows, axis=0) for rows in lefts], axis=1)
    coarse = mul(left, coarse_z_ref[...], HIGHEST)
    lane = lax.broadcasted_iota(jnp.int32, (brick.py, 128), 1)
    for x in range(brick.px):
        block, shift = divmod(x, brick.group)
        value = fine[:, block * 128 : (block + 1) * 128]
        if shift:
            value = pltpu.roll(value, 128 - shift * brick.zpad, 1)
        value = value + coarse[x * brick.py : (x + 1) * brick.py]
        high, low = split(jnp.where(lane < brick.zpad, value, 0.0), 2)
        pot_ref[x] = (
            high + pltpu.roll(high, brick.zpad, 1) + pltpu.roll(low, 2 * brick.zpad, 1)
        )

    for x in range(brick.bx):
        for y in range(brick.by):
            col = brick.col(x, y)
            rows = [
                msg_ref[k * brick.cols + col : k * brick.cols + col + 1, 0 : brick.lanes]
                for k in range(4)
            ]
            shifted = [
                shift_xy(brick, rows[0]),
                shift_xy(brick, rows[1]),
                shift_z(brick, rows[2]),
            ]
            weights = [spline(value) for value in shifted]
            slopes = [spline_slope(value) for value in shifted]
            box = jnp.concatenate(
                [
                    pot_ref[POINTS * x + e, POINTS * y : POINTS * y + 8, 0 : 3 * brick.zpad]
                    for e in range(TAPS)
                ],
                axis=0,
            )
            high, low = split(jnp.concatenate([weights[2], slopes[2]], axis=1), 2)
            tables = jnp.concatenate([high, low, high], axis=0).astype(BF16)
            both = mul(box.astype(BF16), tables)
            along_z = both[:, : brick.lanes]
            sloped_z = both[:, brick.lanes :]
            sums = [0.0, 0.0, 0.0]
            for e in range(TAPS):
                weight = weights[0][e : e + 1]
                slope = slopes[0][e : e + 1]
                flat = along_z[8 * e : 8 * e + 8]
                steep = sloped_z[8 * e : 8 * e + 8]
                sums[0] = sums[0] + flat * slope
                sums[1] = sums[1] + flat * weight
                sums[2] = sums[2] + steep * weight
            across = (weights[1], slopes[1], weights[1])
            for comp in range(3):
                force = jnp.sum(sums[comp] * across[comp], axis=0, keepdims=True)
                row = comp * brick.cols + col
                force = short_ref[row : row + 1, :] - POINTS * (rows[3] * force)
                for z in range(brick.bz):
                    out_ref[comp, x, z, y : y + 1, :] = force[:, z * atoms : (z + 1) * atoms]


VMEM = pl.BlockSpec(memory_space=pltpu.VMEM)
SMEM = pl.BlockSpec(memory_space=pltpu.SMEM)
ANY = pl.BlockSpec(memory_space=pl.ANY)
WHOLE = pl.BlockSpec()


def call(kernel, out_shape, in_specs, scratch, flops, *args, out_spec=VMEM, grant=40):
    single = not isinstance(out_shape, (list, tuple))
    return pl.pallas_call(
        kernel,
        out_shape=out_shape,
        in_specs=in_specs,
        out_specs=out_spec if single else [out_spec] * len(out_shape),
        scratch_shapes=scratch,
        compiler_params=pltpu.CompilerParams(vmem_limit_bytes=grant * 1024 * 1024),
        cost_estimate=pl.CostEstimate(flops=flops, bytes_accessed=10**5, transcendentals=0),
    )(*args)


def neighbours(brick, msg):
    size, wide = brick.n_space, brick.n_sub
    found = {}
    sender = {}
    msgs = []
    for dx in (0, 1, -1):
        for dy in (0, -1, 1):
            if (dx, dy) == (0, 0):
                continue
            key = (dx % size, dy % wide)
            if key not in found:
                found[key] = len(msgs)
                pairs = [
                    ((i + dx) % size * wide + (j + dy) % wide, i * wide + j)
                    for i in range(size)
                    for j in range(wide)
                ]
                msgs.append(lax.ppermute(msg, ("space", "sub"), pairs))
            sender[(dx, dy)] = found[key]
    return sender, msgs


def body(n_space, n_sub, positions, charges, counts):
    brick = Brick(charges.shape, n_space, n_sub)
    n_dev = n_space * n_sub
    along_xz, along_y = fine_tables(brick)
    xz_high = along_xz.astype(BF16)
    xz_low = (along_xz - xz_high.astype(np.float32)).astype(BF16)
    coarse_z = coarse_table(brick)
    place = jnp.stack([lax.axis_index("space"), lax.axis_index("sub")]).astype(jnp.int32)

    turned = (positions.transpose(0, 1, 3, 2, 4), charges.transpose(0, 2, 1, 3))
    msg, coarse = call(
        functools.partial(spread_kernel, brick),
        [
            jax.ShapeDtypeStruct((brick.msg_rows, brick.msg_lanes), F32),
            jax.ShapeDtypeStruct((n_dev, brick.coarse_rows, brick.coarse_lanes), F32),
        ],
        [ANY, ANY, ANY],
        [
            pltpu.SMEM(counts.shape, jnp.int32),
            pltpu.VMEM(turned[0].shape, F32),
            pltpu.VMEM(turned[1].shape, F32),
            pltpu.VMEM((brick.msg_rows, brick.msg_lanes), F32),
            pltpu.VMEM((n_dev, brick.coarse_rows, brick.coarse_lanes), F32),
            pltpu.VMEM((brick.px, brick.py, 128), F32),
            pltpu.SemaphoreType.DMA((3,)),
            pltpu.SemaphoreType.DMA((2,)),
        ],
        10**7,
        counts,
        *turned,
        out_spec=ANY,
        grant=64,
    )
    sender, msgs = neighbours(brick, msg)
    whole = lax.all_to_all(coarse, ("space", "sub"), 0, 0, tiled=True)
    whole = whole.reshape(n_space, n_sub, brick.coarse_rows, brick.coarse_lanes)

    n_col = len(brick.columns)
    short = call(
        functools.partial(pairs_kernel, brick, sender, len(msgs)),
        jax.ShapeDtypeStruct((brick.force_rows, brick.lanes), F32),
        [VMEM] * (1 + len(msgs)),
        [
            pltpu.VMEM((4 * brick.ext_rows, brick.lanes), F32),
            pltpu.VMEM((brick.lanes // 128, FEATURES * brick.ext_rows, 128), F32),
            pltpu.VMEM((brick.lanes // 128, SOURCES * brick.ext_rows, 128), F32),
            pltpu.VMEM((brick.lanes // 128, FEATURES * brick.own_rows, 128), F32),
            pltpu.VMEM((brick.lanes // 128, SOURCES * brick.own_rows, 128), F32),
            pltpu.VMEM((n_col, brick.lanes, FEATURES), BF16),
            pltpu.VMEM((n_col, brick.bz, SOURCES, 2 * brick.atoms), BF16),
            pltpu.VMEM((brick.cols, brick.bz, FEATURES, brick.lanes), BF16),
            pltpu.VMEM((brick.cols, brick.bz, brick.bz, SOURCES, 2 * brick.atoms), BF16),
            pltpu.VMEM((brick.cols, brick.bz, SOURCES, brick.lanes), F32),
            pltpu.VMEM((brick.cols, brick.bz, brick.atoms, brick.kept), BF16),
        ],
        10**10,
        msg,
        *msgs,
    )
    comps, size_x, size_y, size_z, atoms = positions.shape
    forces = call(
        functools.partial(potential_kernel, brick, sender, len(msgs)),
        jax.ShapeDtypeStruct((comps, size_x, size_z, size_y, atoms), F32),
        [SMEM] + [VMEM] * (7 + len(msgs)),
        [
            pltpu.VMEM((brick.px, brick.py, 128), F32),
        ],
        10**8,
        place,
        msg,
        *msgs,
        whole,
        short,
        xz_high,
        xz_low,
        jnp.asarray(along_y),
        jnp.asarray(coarse_z),
        out_spec=WHOLE,
    )
    return forces.transpose(0, 1, 3, 2, 4)


def solution(mesh):
    in_specs = (
        P(None, "space", "sub", None, None),
        P("space", "sub", None, None),
        P("space", "sub", None),
    )
    out_specs = P(None, "space", "sub", None, None)
    run = functools.partial(body, mesh.shape["space"], mesh.shape["sub"])
    return jax.shard_map(run, mesh=mesh, in_specs=in_specs, out_specs=out_specs, check_vma=False)
```

```python
import functools
import math

import jax
import jax.numpy as jnp
import numpy as np
from jax import lax
from jax.experimental import pallas as pl
from jax.experimental.pallas import tpu as pltpu
from jax.sharding import PartitionSpec as P

F32 = jnp.float32
BF16 = jnp.bfloat16
HIGHEST = lax.Precision.HIGHEST

POINTS = 4
REACH = 4
TAPS = POINTS + 3
SOFT_SQUARE = 0.0625
FINE_WIDTHS = (1.0, 2.0)
FINE_WEIGHTS = (2.0, 0.5)
COARSE_FRACTIONS = (8.0, 4.0)
COARSE_WEIGHTS = (4.0, 2.0)

DECAY = 0.11446730730706552
LEAD = 0.13637726630426547
SMOOTH = (1.0312317180277653, 0.44426879021665455, 0.1544174241571791, -0.004580112368867706)
SCALE = math.sqrt(DECAY * math.log2(math.e))
STRETCH = (LEAD / SCALE**3) ** 0.2
SHIFT = math.log2(STRETCH)
QUARTIC = (SMOOTH[0] * STRETCH**2, SMOOTH[1] * STRETCH**4, SMOOTH[2] * STRETCH)
LEVEL = SMOOTH[3] / SCALE**3
HALF_CONST = 0.5 * (SHIFT - SCALE * SCALE * SOFT_SQUARE)

FEATURES = 32
SOURCES = 16


def round_up(value, step):
    return -(-value // step) * step


def mul_t(left, right, precision=None):
    return lax.dot_general(
        left, right, (((1,), (1,)), ((), ())), precision=precision, preferred_element_type=F32
    )


def mul(left, right, precision=None):
    return lax.dot_general(
        left, right, (((1,), (0,)), ((), ())), precision=precision, preferred_element_type=F32
    )


def split(value, count):
    pieces = []
    for _ in range(count - 1):
        piece = value.astype(BF16).astype(F32)
        pieces.append(piece)
        value = value - piece
    pieces.append(value.astype(BF16).astype(F32))
    return pieces


class Brick:
    def __init__(self, shape, n_space, n_sub):
        self.bx, self.by, self.bz, self.atoms = shape
        self.n_space, self.n_sub = n_space, n_sub
        self.cols = self.bx * self.by
        self.lanes = self.bz * self.atoms
        self.wide = (self.bz + 2) * self.atoms
        self.px = POINTS * self.bx + 3
        self.py = round_up(POINTS * (self.by - 1) + 8, 8)
        self.pz = POINTS * self.bz
        self.zpad = round_up(self.pz, 16)
        self.group = 128 // self.zpad
        self.atom_rows = 4 * self.cols
        self.blocks = -(-self.px // self.group)
        self.msg_rows = round_up(self.atom_rows, 8) + self.py
        self.msg_lanes = max(self.lanes, self.blocks * 128)
        self.grid_row = round_up(self.atom_rows, 8)
        self.ci = 2 * self.bx + 2
        self.cj = 2 * self.by + 2
        self.ck = 2 * self.bz
        self.coarse_rows = round_up(self.ci, 8)
        self.coarse_lanes = round_up(self.cj * self.ck, 128)
        self.own_rows = round_up(self.cols, 8)
        self.columns = [
            (x, y) for x in range(-1, self.bx + 1) for y in range(-1, self.by + 1)
        ]
        self.ext_rows = round_up(len(self.columns), 8)
        self.kept = 2 * self.atoms * (1 + self.bz * (self.cols - 1))
        self.force_rows = round_up(3 * self.cols, 8)

    def col(self, x, y):
        return x * self.by + y


def spline(shifted):
    size = jnp.abs(shifted)
    outer = jnp.maximum(2.0 - size, 0.0)
    inner = jnp.maximum(1.0 - size, 0.0)
    return (outer * outer * outer) * (1.0 / 6.0) - (inner * inner * inner) * (4.0 / 6.0)


def spline_slope(shifted):
    size = jnp.abs(shifted)
    outer = jnp.maximum(2.0 - size, 0.0)
    inner = jnp.maximum(1.0 - size, 0.0)
    slope = 2.0 * (inner * inner) - 0.5 * (outer * outer)
    return jnp.where(shifted < 0.0, -slope, slope)


def shift_xy(brick, row):
    entry = lax.broadcasted_iota(jnp.int32, (8, brick.lanes), 0).astype(F32)
    return POINTS * row - (entry - 1.0)


def shift_z(brick, row):
    parts = []
    for cell in range(brick.bz):
        point = lax.broadcasted_iota(jnp.int32, (brick.zpad, brick.atoms), 0)
        entry = lax.rem(point - POINTS * cell + 1 + brick.pz, brick.pz) - 1
        entry = jnp.where(point < brick.pz, entry, 100)
        value = row[:, cell * brick.atoms : (cell + 1) * brick.atoms]
        parts.append(POINTS * value - entry.astype(F32))
    return jnp.concatenate(parts, axis=1)


def spread_kernel(brick, *refs):
    inputs, (msg_ref, coarse_ref), held = refs[0:3], refs[3:5], refs[5:8]
    grid_ref, arrived = refs[8:]
    counts_ref, pos_ref, charge_ref = held
    copies = [
        pltpu.make_async_copy(source, target, arrived.at[number])
        for number, (source, target) in enumerate(zip(inputs, held))
    ]
    for copy in copies:
        copy.start()
    grid_ref[...] = jnp.zeros(grid_ref.shape, F32)
    for copy in copies:
        copy.wait()
    atoms = brick.atoms
    lane = lax.broadcasted_iota(jnp.int32, (1, atoms), 1)
    for x in range(brick.bx):
        for y in range(brick.by):
            col = brick.col(x, y)
            for z in range(brick.bz):
                span = slice(z * atoms, (z + 1) * atoms)
                for comp in range(3):
                    row = comp * brick.cols + col
                    msg_ref[row : row + 1, span] = pos_ref[comp, x, z, y : y + 1, :]
                row = 3 * brick.cols + col
                charge = charge_ref[x, z, y : y + 1, :]
                msg_ref[row : row + 1, span] = jnp.where(lane < counts_ref[x, y, z], charge, 0.0)
    for x in range(brick.bx):
        for y in range(brick.by):
            col = brick.col(x, y)
            rows = [
                msg_ref[k * brick.cols + col : k * brick.cols + col + 1, 0 : brick.lanes]
                for k in range(4)
            ]
            along_x = spline(shift_xy(brick, rows[0])) * rows[3]
            along_y = spline(shift_xy(brick, rows[1]))
            along_z = spline(shift_z(brick, rows[2]))
            outer = jnp.concatenate(
                [along_x[e : e + 1, :] * along_y for e in range(TAPS)], axis=0
            )
            count = outer.shape[0]
            outer = jnp.concatenate(split(outer, 2), axis=0).astype(BF16)
            table = jnp.concatenate(split(along_z, 2), axis=0).astype(BF16)
            box = mul_t(outer, table)
            box = (
                box[:count, : brick.zpad] + box[:count, brick.zpad :] + box[count:, : brick.zpad]
            )
            for e in range(TAPS):
                place = (POINTS * x + e, slice(POINTS * y, POINTS * y + 8), slice(0, brick.zpad))
                grid_ref[place] = grid_ref[place] + box[8 * e : 8 * e + 8, :]
    for block in range(brick.msg_lanes // 128):
        total = jnp.zeros((brick.py, 128), F32)
        for spot in range(brick.group):
            x = block * brick.group + spot
            if x < brick.px:
                plane = grid_ref[x]
                total = total + (pltpu.roll(plane, spot * brick.zpad, 1) if spot else plane)
        msg_ref[brick.grid_row :, block * 128 : (block + 1) * 128] = total
    planes = []
    for idx in range(brick.ci):
        inside = [x for x in (2 * idx - 1, 2 * idx) if 0 <= x < brick.px]
        planes.append(sum(grid_ref[x, :, 0 : brick.zpad] for x in inside))
    stacked = jnp.concatenate(planes, axis=0)
    shape = (brick.zpad, brick.coarse_lanes)
    z_idx = lax.broadcasted_iota(jnp.int32, shape, 0)
    z_lane = lax.broadcasted_iota(jnp.int32, shape, 1)
    used = z_lane < brick.cj * brick.ck
    pairs = (z_idx // 2 == z_lane % brick.ck) & used & (z_idx < brick.pz)
    folded = mul(stacked, jnp.where(pairs, 0.125, 0.0).astype(F32), HIGHEST)
    shape = (brick.py, brick.coarse_lanes)
    y_idx = lax.broadcasted_iota(jnp.int32, shape, 0)
    y_lane = lax.broadcasted_iota(jnp.int32, shape, 1)
    mask = (y_lane // brick.ck == (y_idx + 1) // 2).astype(F32)
    sums = [
        jnp.sum(folded[i * brick.py : (i + 1) * brick.py] * mask, axis=0, keepdims=True)
        for i in range(brick.ci)
    ]
    if brick.coarse_rows > brick.ci:
        sums.append(jnp.zeros((brick.coarse_rows - brick.ci, brick.coarse_lanes), F32))
    coarse_ref[...] = jnp.broadcast_to(jnp.concatenate(sums, axis=0)[None], coarse_ref.shape)


def store_pieces(piece_ref, rows, arrays):
    for number, value in enumerate(arrays):
        for block in range(piece_ref.shape[0]):
            piece_ref[block, number * rows : (number + 1) * rows, :] = value[
                :, block * 128 : (block + 1) * 128
            ]


def load_pieces(piece_ref, rows, row, count):
    parts = [
        piece_ref[block, pl.ds(row, count, stride=rows), :] for block in range(piece_ref.shape[0])
    ]
    return jnp.concatenate(parts, axis=1)


def feature_arrays(coords, square, order, square_first):
    rows = coords[0].shape
    arrays = []
    for value in coords:
        pieces = split(value, 3)
        arrays += [pieces[piece] for piece in order]
    squares = split(square, 3)
    ones = [jnp.ones(rows, F32)] * 3
    arrays += squares + ones if square_first else ones + squares
    return arrays + [jnp.zeros(rows, F32)] * (FEATURES - len(arrays))


def source_arrays(coords, charge):
    arrays = []
    for value in [charge] + [charge * coord for coord in coords]:
        arrays += split(value, 3)
    return arrays + [jnp.zeros(charge.shape, F32)] * (SOURCES - len(arrays))


def minus_square(coords):
    return HALF_CONST - (coords[0] * coords[0] + coords[1] * coords[1] + coords[2] * coords[2])


def pair_factor(left, right):
    power = mul(left, right)
    inverse = lax.rsqrt(SHIFT - power)
    base = jnp.exp2(power)
    square = base * base
    smooth = ((square + QUARTIC[0]) * square + QUARTIC[1]) * (base + QUARTIC[2])
    factor = inverse * (inverse * inverse) - smooth
    high = factor.astype(BF16)
    low = (factor - high.astype(F32)).astype(BF16)
    return high, low


def moments(total, quantity):
    base = 3 * quantity
    return total[base : base + 1] + total[base + 1 : base + 2] + total[base + 2 : base + 3]


def pairs_kernel(brick, sender, n_msgs, *refs):
    atoms, lanes = brick.atoms, brick.lanes
    msg_ref = refs[0]
    other_msgs = refs[1 : 1 + n_msgs]
    force_ref = refs[1 + n_msgs]
    (
        row_ref,
        other_piece_ref,
        source_piece_ref,
        own_piece_ref,
        own_source_ref,
        left_ref,
        source_ref,
        right_ref,
        back_ref,
        total_ref,
        kept_ref,
    ) = refs[2 + n_msgs :]
    half = 0.5 * brick.bz

    rows = brick.ext_rows
    if rows > len(brick.columns):
        row_ref[...] = jnp.zeros(row_ref.shape, F32)
    for place, (x, y) in enumerate(brick.columns):
        shift = (x // brick.bx, y // brick.by)
        col = brick.col(x % brick.bx, y % brick.by)
        for k in range(4):
            near = slice(k * brick.cols + col, k * brick.cols + col + 1)
            if shift == (0, 0):
                value = msg_ref[near, 0:lanes]
            else:
                value = other_msgs[sender[shift]][near, 0:lanes]
            row_ref[k * rows + place : k * rows + place + 1, :] = value
    index = lax.broadcasted_iota(jnp.int32, (rows, 1), 0)
    ext_y = brick.by + 2
    offset_x = (index // ext_y - 1).astype(F32) - 0.5 * brick.bx
    offset_y = (index % ext_y - 1).astype(F32) - 0.5 * brick.by
    lane_z = (lax.broadcasted_iota(jnp.int32, (1, lanes), 1) // atoms).astype(F32)
    coords = [
        (row_ref[0:rows, :] + offset_x) * SCALE,
        (row_ref[rows : 2 * rows, :] + offset_y) * SCALE,
        (row_ref[2 * rows : 3 * rows, :] + (lane_z - half)) * SCALE,
    ]
    charge = row_ref[3 * rows : 4 * rows, :]
    store_pieces(
        other_piece_ref,
        rows,
        feature_arrays(coords, minus_square(coords), (0, 1, 2, 0, 1, 0), False),
    )
    store_pieces(source_piece_ref, rows, source_arrays(coords, charge))
    level_sums = {}
    for place in range(len(brick.columns)):
        feature = load_pieces(other_piece_ref, rows, place, FEATURES)
        left_ref[place] = feature.T.astype(BF16)
        source = load_pieces(source_piece_ref, rows, place, SOURCES)
        for z in range(brick.bz):
            part = source[:, z * atoms : (z + 1) * atoms]
            level_sums[(place, z)] = -LEVEL * jnp.sum(part, axis=1, keepdims=True)
            part = part.astype(BF16)
            source_ref[place, z] = jnp.concatenate([part, part], axis=1)

    rows = brick.own_rows
    own = []
    for k in range(4):
        value = msg_ref[k * brick.cols : (k + 1) * brick.cols, 0:lanes]
        if rows > brick.cols:
            value = jnp.concatenate([value, jnp.zeros((rows - brick.cols, lanes), F32)], axis=0)
        own.append(value)
    index = lax.broadcasted_iota(jnp.int32, (rows, 1), 0)
    own_x = (own[0] + ((index // brick.by).astype(F32) - 0.5 * brick.bx)) * SCALE
    own_y = (own[1] + ((index % brick.by).astype(F32) - 0.5 * brick.by)) * SCALE
    own_z_coords = []
    for other_z in range(brick.bz):
        step = other_z - lane_z
        step = jnp.where(step > half, step - brick.bz, step)
        step = jnp.where(step < -half, step + brick.bz, step)
        own_z_coords.append((own[2] + (other_z - step - half)) * SCALE)
        coords = [own_x, own_y, own_z_coords[-1]]
        arrays = feature_arrays(coords, minus_square(coords), (0, 0, 0, 1, 1, 2), True)
        arrays = [2.0 * value for value in arrays[:18]] + arrays[18:]
        store_pieces(own_piece_ref, rows, arrays)
        store_pieces(own_source_ref, rows, source_arrays(coords, own[3]))
        for col in range(brick.cols):
            part = load_pieces(own_piece_ref, rows, col, FEATURES)
            right_ref[col, other_z] = part.astype(BF16)
            part = load_pieces(own_source_ref, rows, col, SOURCES).astype(BF16)
            for z in range(brick.bz):
                cell = part[:, z * atoms : (z + 1) * atoms]
                back_ref[col, other_z, z] = jnp.concatenate([cell, cell], axis=1)

    cells = [(x, y) for x in range(brick.bx) for y in range(brick.by)]
    tiles = []
    for place, (x, y) in sorted(enumerate(brick.columns), key=lambda item: item[1] not in cells):
        home = cells.index((x, y)) if (x, y) in cells else None
        for z in range(brick.bz):
            for col, (cell_x, cell_y) in enumerate(cells):
                if max(abs(cell_x - x), abs(cell_y - y)) > 1 or (home is not None and col > home):
                    continue
                if col == home:
                    tiles.append((place, z, col, z, None))
                    tiles.append((place, z, col, (z + 1) % brick.bz, home))
                else:
                    tiles += [(place, z, col, own_z, home) for own_z in range(brick.bz)]

    for col in range(brick.cols):
        for z in range(brick.bz):
            for own_z in range(brick.bz):
                level = sum(
                    level_sums[(tile[0], z)] for tile in tiles if tile[1:4] == (z, col, own_z)
                )
                span = slice(own_z * atoms, (own_z + 1) * atoms)
                total_ref[col, z, :, span] = jnp.broadcast_to(level, (SOURCES, atoms))

    mirrors = {(col, z): [] for col in range(brick.cols) for z in range(brick.bz)}
    for place, z, col, own_z, home in tiles:
        span = slice(own_z * atoms, (own_z + 1) * atoms)
        left = left_ref[place, z * atoms : (z + 1) * atoms, :]
        high, low = pair_factor(left, right_ref[col, z, :, span])
        total_ref[col, z, :, span] += mul(
            source_ref[place, z], jnp.concatenate([high, low], axis=0)
        )
        if home is not None:
            spot = 2 * atoms * len(mirrors[(home, z)])
            mirrors[(home, z)].append((col, own_z))
            kept_ref[home, z, :, spot : spot + atoms] = high
            kept_ref[home, z, :, spot + atoms : spot + 2 * atoms] = low
    back_sums = {}
    for (col, z), found in mirrors.items():
        back = jnp.concatenate([back_ref[c, z, own_z] for c, own_z in found], axis=1)
        level = (-0.5 * LEVEL) * jnp.sum(back.astype(F32), axis=1, keepdims=True)
        back_sums[(col, z)] = mul_t(kept_ref[col, z, :, 0 : back.shape[1]], back).T + level

    for col in range(brick.cols):
        forces = [0.0, 0.0, 0.0]
        for z in range(brick.bz):
            total = total_ref[col, z]
            weight = moments(total, 0)
            for comp, coord in enumerate((own_x, own_y, own_z_coords[z])):
                value = coord[col : col + 1] * weight - moments(total, 1 + comp)
                forces[comp] = forces[comp] + value
        total = jnp.concatenate([back_sums[(col, z)] for z in range(brick.bz)], axis=1)
        weight = moments(total, 0)
        home = (own[2] + (lane_z - half)) * SCALE
        for comp, coord in enumerate((own_x, own_y, home)):
            row = comp * brick.cols + col
            value = coord[col : col + 1] * weight - moments(total, 1 + comp)
            value = value + forces[comp]
            force_ref[row : row + 1, :] = value * (own[3][col : col + 1] * (SCALE * SCALE))


def fine_tables(brick):
    ext_x = brick.px + 2 * REACH
    rows_y = brick.py + POINTS * brick.by
    out_lanes = brick.blocks * 128
    in_lanes = round_up(max(ext_x * brick.zpad, out_lanes), 128)
    count = len(FINE_WIDTHS)
    along_xz = np.zeros((in_lanes, count * out_lanes), np.float32)
    along_y = np.zeros((brick.py, count * rows_y), np.float32)

    def tap(dist, width):
        return np.where(np.abs(dist) <= REACH, np.exp(-(dist * dist) / (2.0 * width * width)), 0.0)

    for number, (width, weight) in enumerate(zip(FINE_WIDTHS, FINE_WEIGHTS)):
        mat_z = np.zeros((brick.zpad, brick.zpad))
        for step in range(-REACH, REACH + 1):
            for z in range(brick.pz):
                mat_z[(z + step) % brick.pz, z] += weight * tap(np.float64(step), width)
        mat_x = tap(np.arange(ext_x)[:, None] - np.arange(brick.px)[None, :] - REACH, width)
        dense = np.kron(mat_x, mat_z)
        along_xz[: dense.shape[0], number * out_lanes : number * out_lanes + dense.shape[1]] = dense
        out_y = np.arange(POINTS * brick.by + 3) - 1.0
        in_y = np.arange(rows_y) - 1.0 - POINTS * brick.by
        along_y[: len(out_y), number * rows_y : (number + 1) * rows_y] = tap(
            out_y[:, None] - in_y[None, :], width
        )
    return along_xz, along_y


def coarse_table(brick):
    table = np.zeros((len(COARSE_WEIGHTS) * brick.coarse_lanes, 128), np.float32)
    length = brick.ck
    for number, (fraction, weight) in enumerate(zip(COARSE_FRACTIONS, COARSE_WEIGHTS)):
        width = length / fraction
        for row in range(brick.cj * brick.ck):
            for z in range(brick.pz):
                dist = (row - z // 2) % length
                dist = min(dist, length - dist)
                table[number * brick.coarse_lanes + row, z] = weight * math.exp(
                    -(dist * dist) / (2.0 * width * width)
                )
    return table


def gauss(row, col, length, fraction):
    dist = lax.rem(row - col + 2 * length, length)
    dist = jnp.minimum(dist, length - dist).astype(F32)
    width = length / fraction
    return jnp.exp(dist * dist * (-1.0 / (2.0 * width * width)))


def potential_kernel(brick, sender, n_msgs, *refs):
    atoms = brick.atoms
    place_ref, msg_ref = refs[0:2]
    other_msgs = refs[2 : 2 + n_msgs]
    (
        whole_ref,
        short_ref,
        xz_high_ref,
        xz_low_ref,
        y_ref,
        coarse_z_ref,
        out_ref,
        pot_ref,
    ) = refs[2 + n_msgs :]
    step_y = POINTS * brick.by
    rows_y = brick.py + step_y
    in_lanes = xz_high_ref.shape[0]
    out_lanes = brick.blocks * 128
    grid = None
    for dx in (-1, 0, 1):
        grids = []
        for dy in (-1, 0, 1):
            near = slice(brick.grid_row, brick.msg_rows)
            span = slice(0, out_lanes)
            if (dx, dy) == (0, 0):
                grids.append(msg_ref[near, span])
            else:
                grids.append(other_msgs[sender[(dx, dy)]][near, span])
        tiles = [None] * ((brick.py + 2 * step_y) // 8)
        for number, part in enumerate(grids):
            for tile in range(brick.py // 8):
                spot = tile + number * step_y // 8
                value = part[8 * tile : 8 * tile + 8]
                tiles[spot] = value if tiles[spot] is None else tiles[spot] + value
        column = jnp.concatenate(tiles[: rows_y // 8], axis=0)
        if in_lanes > out_lanes:
            column = jnp.concatenate(
                [column, jnp.zeros((rows_y, in_lanes - out_lanes), F32)], axis=1
            )
        shift = (REACH + POINTS * brick.bx * dx) * brick.zpad
        column = pltpu.roll(column, shift % in_lanes, 1)
        grid = column if grid is None else grid + column
    pieces = jnp.concatenate(split(grid, 2), axis=0).astype(BF16)
    mixed = mul(pieces, xz_high_ref[...]) + mul(pieces, xz_low_ref[...])
    mixed = mixed[:rows_y] + mixed[rows_y:]
    mixed = jnp.concatenate(
        [mixed[:, n * out_lanes : (n + 1) * out_lanes] for n in range(len(FINE_WIDTHS))], axis=0
    )
    fine = mul(y_ref[...], mixed, HIGHEST)

    total_x = 2 * brick.bx * brick.n_space
    total_y = 2 * brick.by * brick.n_sub
    first_x = place_ref[0] * (2 * brick.bx)
    first_y = place_ref[1] * (2 * brick.by)
    out_rows = round_up(brick.px, 8)
    shape = (out_rows, brick.n_space * brick.coarse_rows)
    point = lax.broadcasted_iota(jnp.int32, shape, 0)
    lane = lax.broadcasted_iota(jnp.int32, shape, 1)
    row_x = first_x + (point + 1) // 2 - 1
    col_x = lane // brick.coarse_rows * (2 * brick.bx) + lane % brick.coarse_rows - 1
    live = lane % brick.coarse_rows < brick.ci
    mats_x = jnp.concatenate(
        [
            jnp.where(live, gauss(row_x, col_x, total_x, fraction), 0.0)
            for fraction in COARSE_FRACTIONS
        ],
        axis=0,
    )
    shape = (brick.py, brick.coarse_lanes)
    point = lax.broadcasted_iota(jnp.int32, shape, 0)
    lane = lax.broadcasted_iota(jnp.int32, shape, 1)
    row_y = first_y + (point + 1) // 2 - 1
    live = lane < brick.cj * brick.ck
    lefts = [[None] * brick.px for _ in COARSE_FRACTIONS]
    for sub in range(brick.n_sub):
        part = whole_ref[:, sub].reshape(
            brick.n_space * brick.coarse_rows, brick.coarse_lanes
        )
        mixed = mul(mats_x, part, HIGHEST)
        col_y = sub * (2 * brick.by) + lane // brick.ck - 1
        for number, fraction in enumerate(COARSE_FRACTIONS):
            mat_y = jnp.where(live, gauss(row_y, col_y, total_y, fraction), 0.0)
            for x in range(brick.px):
                row = number * out_rows + x
                value = mixed[row : row + 1] * mat_y
                done = lefts[number][x]
                lefts[number][x] = value if done is None else done + value
    left = jnp.concatenate([jnp.concatenate(rows, axis=0) for rows in lefts], axis=1)
    parts = mul(jnp.concatenate(split(left, 2), axis=0).astype(BF16), coarse_z_ref[...])
    count = left.shape[0]
    coarse = parts[:count] + pltpu.roll(parts[:count], 128 - brick.zpad, 1) + parts[count:]
    lane = lax.broadcasted_iota(jnp.int32, (brick.py, 128), 1)
    for x in range(brick.px):
        block, shift = divmod(x, brick.group)
        value = fine[:, block * 128 : (block + 1) * 128]
        if shift:
            value = pltpu.roll(value, 128 - shift * brick.zpad, 1)
        value = value + coarse[x * brick.py : (x + 1) * brick.py]
        high, low = split(jnp.where(lane < brick.zpad, value, 0.0), 2)
        pot_ref[x] = (
            high + pltpu.roll(high, brick.zpad, 1) + pltpu.roll(low, 2 * brick.zpad, 1)
        )

    for x in range(brick.bx):
        for y in range(brick.by):
            col = brick.col(x, y)
            rows = [
                msg_ref[k * brick.cols + col : k * brick.cols + col + 1, 0 : brick.lanes]
                for k in range(4)
            ]
            shifted = [
                shift_xy(brick, rows[0]),
                shift_xy(brick, rows[1]),
                shift_z(brick, rows[2]),
            ]
            weights = [spline(value) for value in shifted]
            slopes = [spline_slope(value) for value in shifted]
            box = jnp.concatenate(
                [
                    pot_ref[POINTS * x + e, POINTS * y : POINTS * y + 8, 0 : 3 * brick.zpad]
                    for e in range(TAPS)
                ],
                axis=0,
            )
            high, low = split(jnp.concatenate([weights[2], slopes[2]], axis=1), 2)
            tables = jnp.concatenate([high, low, high], axis=0).astype(BF16)
            both = mul(box.astype(BF16), tables)
            along_z = both[:, : brick.lanes]
            sloped_z = both[:, brick.lanes :]
            sums = [0.0, 0.0, 0.0]
            for e in range(TAPS):
                weight = weights[0][e : e + 1]
                slope = slopes[0][e : e + 1]
                flat = along_z[8 * e : 8 * e + 8]
                steep = sloped_z[8 * e : 8 * e + 8]
                sums[0] = sums[0] + flat * slope
                sums[1] = sums[1] + flat * weight
                sums[2] = sums[2] + steep * weight
            across = (weights[1], slopes[1], weights[1])
            for comp in range(3):
                force = jnp.sum(sums[comp] * across[comp], axis=0, keepdims=True)
                row = comp * brick.cols + col
                force = short_ref[row : row + 1, :] - POINTS * (rows[3] * force)
                for z in range(brick.bz):
                    out_ref[comp, x, z, y : y + 1, :] = force[:, z * atoms : (z + 1) * atoms]


VMEM = pl.BlockSpec(memory_space=pltpu.VMEM)
SMEM = pl.BlockSpec(memory_space=pltpu.SMEM)
ANY = pl.BlockSpec(memory_space=pl.ANY)
WHOLE = pl.BlockSpec()


def call(kernel, out_shape, in_specs, scratch, flops, *args, out_spec=VMEM, grant=40):
    single = not isinstance(out_shape, (list, tuple))
    return pl.pallas_call(
        kernel,
        out_shape=out_shape,
        in_specs=in_specs,
        out_specs=out_spec if single else [out_spec] * len(out_shape),
        scratch_shapes=scratch,
        compiler_params=pltpu.CompilerParams(vmem_limit_bytes=grant * 1024 * 1024),
        cost_estimate=pl.CostEstimate(flops=flops, bytes_accessed=10**5, transcendentals=0),
    )(*args)


def neighbours(brick, msg):
    size, wide = brick.n_space, brick.n_sub
    found = {}
    sender = {}
    msgs = []
    for dx in (1, -1, 0):
        for dy in (0, -1, 1):
            if (dx, dy) == (0, 0):
                continue
            key = (dx % size, dy % wide)
            if key not in found:
                found[key] = len(msgs)
                pairs = [
                    ((i + dx) % size * wide + (j + dy) % wide, i * wide + j)
                    for i in range(size)
                    for j in range(wide)
                ]
                msgs.append(lax.ppermute(msg, ("space", "sub"), pairs))
            sender[(dx, dy)] = found[key]
    return sender, msgs


def body(n_space, n_sub, positions, charges, counts):
    brick = Brick(charges.shape, n_space, n_sub)
    n_dev = n_space * n_sub
    along_xz, along_y = fine_tables(brick)
    xz_high = along_xz.astype(BF16)
    xz_low = (along_xz - xz_high.astype(np.float32)).astype(BF16)
    coarse_z = coarse_table(brick)
    coarse_high = coarse_z.astype(BF16)
    coarse_low = (coarse_z - coarse_high.astype(np.float32)).astype(BF16)
    coarse_pair = coarse_high.copy()
    coarse_pair[:, brick.zpad : 2 * brick.zpad] = coarse_low[:, : brick.zpad]
    place = jnp.stack([lax.axis_index("space"), lax.axis_index("sub")]).astype(jnp.int32)

    turned = (positions.transpose(0, 1, 3, 2, 4), charges.transpose(0, 2, 1, 3))
    msg, coarse = call(
        functools.partial(spread_kernel, brick),
        [
            jax.ShapeDtypeStruct((brick.msg_rows, brick.msg_lanes), F32),
            jax.ShapeDtypeStruct((n_dev, brick.coarse_rows, brick.coarse_lanes), F32),
        ],
        [ANY, ANY, ANY],
        [
            pltpu.SMEM(counts.shape, jnp.int32),
            pltpu.VMEM(turned[0].shape, F32),
            pltpu.VMEM(turned[1].shape, F32),
            pltpu.VMEM((brick.px, brick.py, 128), F32),
            pltpu.SemaphoreType.DMA((3,)),
        ],
        10**7,
        counts,
        *turned,
        grant=64,
    )
    sender, msgs = neighbours(brick, msg)
    whole = lax.all_to_all(coarse, ("space", "sub"), 0, 0, tiled=True)
    whole = whole.reshape(n_space, n_sub, brick.coarse_rows, brick.coarse_lanes)

    n_col = len(brick.columns)
    short = call(
        functools.partial(pairs_kernel, brick, sender, len(msgs)),
        jax.ShapeDtypeStruct((brick.force_rows, brick.lanes), F32),
        [VMEM] * (1 + len(msgs)),
        [
            pltpu.VMEM((4 * brick.ext_rows, brick.lanes), F32),
            pltpu.VMEM((brick.lanes // 128, FEATURES * brick.ext_rows, 128), F32),
            pltpu.VMEM((brick.lanes // 128, SOURCES * brick.ext_rows, 128), F32),
            pltpu.VMEM((brick.lanes // 128, FEATURES * brick.own_rows, 128), F32),
            pltpu.VMEM((brick.lanes // 128, SOURCES * brick.own_rows, 128), F32),
            pltpu.VMEM((n_col, brick.lanes, FEATURES), BF16),
            pltpu.VMEM((n_col, brick.bz, SOURCES, 2 * brick.atoms), BF16),
            pltpu.VMEM((brick.cols, brick.bz, FEATURES, brick.lanes), BF16),
            pltpu.VMEM((brick.cols, brick.bz, brick.bz, SOURCES, 2 * brick.atoms), BF16),
            pltpu.VMEM((brick.cols, brick.bz, SOURCES, brick.lanes), F32),
            pltpu.VMEM((brick.cols, brick.bz, brick.atoms, brick.kept), BF16),
        ],
        10**10,
        msg,
        *msgs,
    )
    comps, size_x, size_y, size_z, atoms = positions.shape
    forces = call(
        functools.partial(potential_kernel, brick, sender, len(msgs)),
        jax.ShapeDtypeStruct((comps, size_x, size_z, size_y, atoms), F32),
        [SMEM] + [VMEM] * (7 + len(msgs)),
        [
            pltpu.VMEM((brick.px, brick.py, 128), F32),
        ],
        10**8,
        place,
        msg,
        *msgs,
        whole,
        short,
        xz_high,
        xz_low,
        jnp.asarray(along_y),
        coarse_pair,
        out_spec=WHOLE,
    )
    return forces.transpose(0, 1, 3, 2, 4)


def solution(mesh):
    in_specs = (
        P(None, "space", "sub", None, None),
        P("space", "sub", None, None),
        P("space", "sub", None),
    )
    out_specs = P(None, "space", "sub", None, None)
    run = functools.partial(body, mesh.shape["space"], mesh.shape["sub"])
    return jax.shard_map(run, mesh=mesh, in_specs=in_specs, out_specs=out_specs, check_vma=False)
```

```python
import functools
import math

import jax
import jax.numpy as jnp
import numpy as np
from jax import lax
from jax.experimental import pallas as pl
from jax.experimental.pallas import tpu as pltpu
from jax.sharding import PartitionSpec as P

F32 = jnp.float32
BF16 = jnp.bfloat16
HIGHEST = lax.Precision.HIGHEST

POINTS = 4
REACH = 4
TAPS = POINTS + 3
SOFT_SQUARE = 0.0625
FINE_WIDTHS = (1.0, 2.0)
FINE_WEIGHTS = (2.0, 0.5)
COARSE_FRACTIONS = (8.0, 4.0)
COARSE_WEIGHTS = (4.0, 2.0)

DECAY = 0.11446730730706552
LEAD = 0.13637726630426547
SMOOTH = (1.0312317180277653, 0.44426879021665455, 0.1544174241571791, -0.004580112368867706)
SCALE = math.sqrt(DECAY * math.log2(math.e))
STRETCH = (LEAD / SCALE**3) ** 0.2
SHIFT = math.log2(STRETCH)
QUARTIC = (SMOOTH[0] * STRETCH**2, SMOOTH[1] * STRETCH**4, SMOOTH[2] * STRETCH)
LEVEL = SMOOTH[3] / SCALE**3
HALF_CONST = 0.5 * (SHIFT - SCALE * SCALE * SOFT_SQUARE)

FEATURES = 32
SOURCES = 16


def round_up(value, step):
    return -(-value // step) * step


def mul_t(left, right, precision=None):
    return lax.dot_general(
        left, right, (((1,), (1,)), ((), ())), precision=precision, preferred_element_type=F32
    )


def mul(left, right, precision=None):
    return lax.dot_general(
        left, right, (((1,), (0,)), ((), ())), precision=precision, preferred_element_type=F32
    )


def split(value, count):
    pieces = []
    for _ in range(count - 1):
        piece = value.astype(BF16).astype(F32)
        pieces.append(piece)
        value = value - piece
    pieces.append(value.astype(BF16).astype(F32))
    return pieces


class Brick:
    def __init__(self, shape, n_space, n_sub):
        self.bx, self.by, self.bz, self.atoms = shape
        self.n_space, self.n_sub = n_space, n_sub
        self.cols = self.bx * self.by
        self.lanes = self.bz * self.atoms
        self.wide = (self.bz + 2) * self.atoms
        self.px = POINTS * self.bx + 3
        self.py = round_up(POINTS * (self.by - 1) + 8, 8)
        self.pz = POINTS * self.bz
        self.zpad = round_up(self.pz, 16)
        self.group = 128 // self.zpad
        self.atom_rows = 4 * self.cols
        self.blocks = -(-self.px // self.group)
        self.msg_rows = round_up(self.atom_rows, 8) + self.py
        self.msg_lanes = max(self.lanes, self.blocks * 128)
        self.grid_row = round_up(self.atom_rows, 8)
        self.ci = 2 * self.bx + 2
        self.cj = 2 * self.by + 2
        self.ck = 2 * self.bz
        self.coarse_rows = round_up(self.ci, 8)
        self.coarse_lanes = round_up(self.cj * self.ck, 128)
        self.own_rows = round_up(self.cols, 8)
        self.columns = [
            (x, y) for x in range(-1, self.bx + 1) for y in range(-1, self.by + 1)
        ]
        self.ext_rows = round_up(len(self.columns), 8)
        self.kept = 2 * self.atoms * (1 + self.bz * (self.cols - 1))
        self.force_rows = round_up(3 * self.cols, 8)

    def col(self, x, y):
        return x * self.by + y


def spline(shifted):
    size = jnp.abs(shifted)
    outer = jnp.maximum(2.0 - size, 0.0)
    inner = jnp.maximum(1.0 - size, 0.0)
    return (outer * outer * outer) * (1.0 / 6.0) - (inner * inner * inner) * (4.0 / 6.0)


def spline_slope(shifted):
    size = jnp.abs(shifted)
    outer = jnp.maximum(2.0 - size, 0.0)
    inner = jnp.maximum(1.0 - size, 0.0)
    slope = 2.0 * (inner * inner) - 0.5 * (outer * outer)
    return jnp.where(shifted < 0.0, -slope, slope)


def shift_xy(brick, row):
    entry = lax.broadcasted_iota(jnp.int32, (8, brick.lanes), 0).astype(F32)
    return POINTS * row - (entry - 1.0)


def shift_z(brick, row):
    parts = []
    for cell in range(brick.bz):
        point = lax.broadcasted_iota(jnp.int32, (brick.zpad, brick.atoms), 0)
        entry = lax.rem(point - POINTS * cell + 1 + brick.pz, brick.pz) - 1
        entry = jnp.where(point < brick.pz, entry, 100)
        value = row[:, cell * brick.atoms : (cell + 1) * brick.atoms]
        parts.append(POINTS * value - entry.astype(F32))
    return jnp.concatenate(parts, axis=1)


def spread_kernel(brick, *refs):
    inputs, (msg_ref, coarse_ref), held = refs[0:3], refs[3:5], refs[5:8]
    grid_ref, arrived = refs[8:]
    counts_ref, pos_ref, charge_ref = held
    copies = [
        pltpu.make_async_copy(source, target, arrived.at[number])
        for number, (source, target) in enumerate(zip(inputs, held))
    ]
    for copy in copies:
        copy.start()
    grid_ref[...] = jnp.zeros(grid_ref.shape, F32)
    for copy in copies:
        copy.wait()
    atoms = brick.atoms
    lane = lax.broadcasted_iota(jnp.int32, (1, atoms), 1)
    for x in range(brick.bx):
        for y in range(brick.by):
            col = brick.col(x, y)
            for z in range(brick.bz):
                span = slice(z * atoms, (z + 1) * atoms)
                for comp in range(3):
                    row = comp * brick.cols + col
                    msg_ref[row : row + 1, span] = pos_ref[comp, x, z, y : y + 1, :]
                row = 3 * brick.cols + col
                charge = charge_ref[x, z, y : y + 1, :]
                msg_ref[row : row + 1, span] = jnp.where(lane < counts_ref[x, y, z], charge, 0.0)
    for x in range(brick.bx):
        for y in range(brick.by):
            col = brick.col(x, y)
            rows = [
                msg_ref[k * brick.cols + col : k * brick.cols + col + 1, 0 : brick.lanes]
                for k in range(4)
            ]
            along_x = spline(shift_xy(brick, rows[0])) * rows[3]
            along_y = spline(shift_xy(brick, rows[1]))
            along_z = spline(shift_z(brick, rows[2]))
            outer = jnp.concatenate(
                [along_x[e : e + 1, :] * along_y for e in range(TAPS)], axis=0
            )
            count = outer.shape[0]
            outer = jnp.concatenate(split(outer, 2), axis=0).astype(BF16)
            table = jnp.concatenate(split(along_z, 2), axis=0).astype(BF16)
            box = mul_t(outer, table)
            box = (
                box[:count, : brick.zpad] + box[:count, brick.zpad :] + box[count:, : brick.zpad]
            )
            for e in range(TAPS):
                place = (POINTS * x + e, slice(POINTS * y, POINTS * y + 8), slice(0, brick.zpad))
                grid_ref[place] = grid_ref[place] + box[8 * e : 8 * e + 8, :]
    for block in range(brick.msg_lanes // 128):
        total = jnp.zeros((brick.py, 128), F32)
        for spot in range(brick.group):
            x = block * brick.group + spot
            if x < brick.px:
                plane = grid_ref[x]
                total = total + (pltpu.roll(plane, spot * brick.zpad, 1) if spot else plane)
        msg_ref[brick.grid_row :, block * 128 : (block + 1) * 128] = total
    planes = []
    for idx in range(brick.ci):
        inside = [x for x in (2 * idx - 1, 2 * idx) if 0 <= x < brick.px]
        planes.append(sum(grid_ref[x, :, 0 : brick.zpad] for x in inside))
    stacked = jnp.concatenate(planes, axis=0)
    shape = (brick.zpad, brick.coarse_lanes)
    z_idx = lax.broadcasted_iota(jnp.int32, shape, 0)
    z_lane = lax.broadcasted_iota(jnp.int32, shape, 1)
    used = z_lane < brick.cj * brick.ck
    pairs = (z_idx // 2 == z_lane % brick.ck) & used & (z_idx < brick.pz)
    folded = mul(stacked, jnp.where(pairs, 0.125, 0.0).astype(F32), HIGHEST)
    shape = (brick.py, brick.coarse_lanes)
    y_idx = lax.broadcasted_iota(jnp.int32, shape, 0)
    y_lane = lax.broadcasted_iota(jnp.int32, shape, 1)
    mask = (y_lane // brick.ck == (y_idx + 1) // 2).astype(F32)
    sums = [
        jnp.sum(folded[i * brick.py : (i + 1) * brick.py] * mask, axis=0, keepdims=True)
        for i in range(brick.ci)
    ]
    if brick.coarse_rows > brick.ci:
        sums.append(jnp.zeros((brick.coarse_rows - brick.ci, brick.coarse_lanes), F32))
    coarse_ref[...] = jnp.broadcast_to(jnp.concatenate(sums, axis=0)[None], coarse_ref.shape)


def store_pieces(piece_ref, rows, arrays):
    for number, value in enumerate(arrays):
        for block in range(piece_ref.shape[0]):
            piece_ref[block, number * rows : (number + 1) * rows, :] = value[
                :, block * 128 : (block + 1) * 128
            ]


def load_pieces(piece_ref, rows, row, count):
    parts = [
        piece_ref[block, pl.ds(row, count, stride=rows), :] for block in range(piece_ref.shape[0])
    ]
    return jnp.concatenate(parts, axis=1)


def feature_arrays(coords, square, order, square_first):
    rows = coords[0].shape
    arrays = []
    for value in coords:
        pieces = split(value, 3)
        arrays += [pieces[piece] for piece in order]
    squares = split(square, 3)
    ones = [jnp.ones(rows, F32)] * 3
    arrays += squares + ones if square_first else ones + squares
    return arrays + [jnp.zeros(rows, F32)] * (FEATURES - len(arrays))


def source_arrays(coords, charge):
    arrays = []
    for value in [charge] + [charge * coord for coord in coords]:
        arrays += split(value, 3)
    return arrays + [jnp.zeros(charge.shape, F32)] * (SOURCES - len(arrays))


def minus_square(coords):
    return HALF_CONST - (coords[0] * coords[0] + coords[1] * coords[1] + coords[2] * coords[2])


def pair_factor(left, right):
    power = mul(left, right)
    inverse = lax.rsqrt(SHIFT - power)
    base = jnp.exp2(power)
    square = base * base
    smooth = ((square + QUARTIC[0]) * square + QUARTIC[1]) * (base + QUARTIC[2])
    factor = inverse * (inverse * inverse) - smooth
    high = factor.astype(BF16)
    low = (factor - high.astype(F32)).astype(BF16)
    return high, low


def moments(total, quantity):
    base = 3 * quantity
    return total[base : base + 1] + total[base + 1 : base + 2] + total[base + 2 : base + 3]


def pairs_kernel(brick, sender, n_msgs, *refs):
    atoms, lanes = brick.atoms, brick.lanes
    msg_ref = refs[0]
    other_msgs = refs[1 : 1 + n_msgs]
    force_ref = refs[1 + n_msgs]
    (
        row_ref,
        other_piece_ref,
        source_piece_ref,
        own_piece_ref,
        own_source_ref,
        left_ref,
        source_ref,
        right_ref,
        back_ref,
        total_ref,
        kept_ref,
    ) = refs[2 + n_msgs :]
    half = 0.5 * brick.bz

    rows = brick.ext_rows
    if rows > len(brick.columns):
        row_ref[...] = jnp.zeros(row_ref.shape, F32)
    for place, (x, y) in enumerate(brick.columns):
        shift = (x // brick.bx, y // brick.by)
        col = brick.col(x % brick.bx, y % brick.by)
        for k in range(4):
            near = slice(k * brick.cols + col, k * brick.cols + col + 1)
            if shift == (0, 0):
                value = msg_ref[near, 0:lanes]
            else:
                value = other_msgs[sender[shift]][near, 0:lanes]
            row_ref[k * rows + place : k * rows + place + 1, :] = value
    index = lax.broadcasted_iota(jnp.int32, (rows, 1), 0)
    ext_y = brick.by + 2
    offset_x = (index // ext_y - 1).astype(F32) - 0.5 * brick.bx
    offset_y = (index % ext_y - 1).astype(F32) - 0.5 * brick.by
    lane_z = (lax.broadcasted_iota(jnp.int32, (1, lanes), 1) // atoms).astype(F32)
    coords = [
        (row_ref[0:rows, :] + offset_x) * SCALE,
        (row_ref[rows : 2 * rows, :] + offset_y) * SCALE,
        (row_ref[2 * rows : 3 * rows, :] + (lane_z - half)) * SCALE,
    ]
    charge = row_ref[3 * rows : 4 * rows, :]
    store_pieces(
        other_piece_ref,
        rows,
        feature_arrays(coords, minus_square(coords), (0, 1, 2, 0, 1, 0), False),
    )
    store_pieces(source_piece_ref, rows, source_arrays(coords, charge))
    level_sums = {}
    for place in range(len(brick.columns)):
        feature = load_pieces(other_piece_ref, rows, place, FEATURES)
        left_ref[place] = feature.T.astype(BF16)
        source = load_pieces(source_piece_ref, rows, place, SOURCES)
        for z in range(brick.bz):
            part = source[:, z * atoms : (z + 1) * atoms]
            level_sums[(place, z)] = -LEVEL * jnp.sum(part, axis=1, keepdims=True)
            part = part.astype(BF16)
            source_ref[place, z] = jnp.concatenate([part, part], axis=1)

    rows = brick.own_rows
    own = []
    for k in range(4):
        value = msg_ref[k * brick.cols : (k + 1) * brick.cols, 0:lanes]
        if rows > brick.cols:
            value = jnp.concatenate([value, jnp.zeros((rows - brick.cols, lanes), F32)], axis=0)
        own.append(value)
    index = lax.broadcasted_iota(jnp.int32, (rows, 1), 0)
    own_x = (own[0] + ((index // brick.by).astype(F32) - 0.5 * brick.bx)) * SCALE
    own_y = (own[1] + ((index % brick.by).astype(F32) - 0.5 * brick.by)) * SCALE
    own_z_coords = []
    for other_z in range(brick.bz):
        step = other_z - lane_z
        step = jnp.where(step > half, step - brick.bz, step)
        step = jnp.where(step < -half, step + brick.bz, step)
        own_z_coords.append((own[2] + (other_z - step - half)) * SCALE)
        coords = [own_x, own_y, own_z_coords[-1]]
        arrays = feature_arrays(coords, minus_square(coords), (0, 0, 0, 1, 1, 2), True)
        arrays = [2.0 * value for value in arrays[:18]] + arrays[18:]
        store_pieces(own_piece_ref, rows, arrays)
        store_pieces(own_source_ref, rows, source_arrays(coords, own[3]))
        for col in range(brick.cols):
            part = load_pieces(own_piece_ref, rows, col, FEATURES)
            right_ref[col, other_z] = part.astype(BF16)
            part = load_pieces(own_source_ref, rows, col, SOURCES).astype(BF16)
            for z in range(brick.bz):
                cell = part[:, z * atoms : (z + 1) * atoms]
                back_ref[col, other_z, z] = jnp.concatenate([cell, cell], axis=1)

    cells = [(x, y) for x in range(brick.bx) for y in range(brick.by)]
    tiles = []
    for place, (x, y) in sorted(enumerate(brick.columns), key=lambda item: item[1] not in cells):
        home = cells.index((x, y)) if (x, y) in cells else None
        for z in range(brick.bz):
            for col, (cell_x, cell_y) in enumerate(cells):
                if max(abs(cell_x - x), abs(cell_y - y)) > 1 or (home is not None and col > home):
                    continue
                if col == home:
                    tiles.append((place, z, col, z, None))
                    tiles.append((place, z, col, (z + 1) % brick.bz, home))
                else:
                    tiles += [(place, z, col, own_z, home) for own_z in range(brick.bz)]

    for col in range(brick.cols):
        for z in range(brick.bz):
            for own_z in range(brick.bz):
                level = sum(
                    level_sums[(tile[0], z)] for tile in tiles if tile[1:4] == (z, col, own_z)
                )
                span = slice(own_z * atoms, (own_z + 1) * atoms)
                total_ref[col, z, :, span] = jnp.broadcast_to(level, (SOURCES, atoms))

    mirrors = {(col, z): [] for col in range(brick.cols) for z in range(brick.bz)}
    for place, z, col, own_z, home in tiles:
        span = slice(own_z * atoms, (own_z + 1) * atoms)
        left = left_ref[place, z * atoms : (z + 1) * atoms, :]
        high, low = pair_factor(left, right_ref[col, z, :, span])
        total_ref[col, z, :, span] += mul(
            source_ref[place, z], jnp.concatenate([high, low], axis=0)
        )
        if home is not None:
            spot = 2 * atoms * len(mirrors[(home, z)])
            mirrors[(home, z)].append((col, own_z))
            kept_ref[home, z, :, spot : spot + atoms] = high
            kept_ref[home, z, :, spot + atoms : spot + 2 * atoms] = low
    back_sums = {}
    for (col, z), found in mirrors.items():
        back = jnp.concatenate([back_ref[c, z, own_z] for c, own_z in found], axis=1)
        level = (-0.5 * LEVEL) * jnp.sum(back.astype(F32), axis=1, keepdims=True)
        back_sums[(col, z)] = mul_t(kept_ref[col, z, :, 0 : back.shape[1]], back).T + level

    for col in range(brick.cols):
        forces = [0.0, 0.0, 0.0]
        for z in range(brick.bz):
            total = total_ref[col, z]
            weight = moments(total, 0)
            for comp, coord in enumerate((own_x, own_y, own_z_coords[z])):
                value = coord[col : col + 1] * weight - moments(total, 1 + comp)
                forces[comp] = forces[comp] + value
        total = jnp.concatenate([back_sums[(col, z)] for z in range(brick.bz)], axis=1)
        weight = moments(total, 0)
        home = (own[2] + (lane_z - half)) * SCALE
        for comp, coord in enumerate((own_x, own_y, home)):
            row = comp * brick.cols + col
            value = coord[col : col + 1] * weight - moments(total, 1 + comp)
            value = value + forces[comp]
            force_ref[row : row + 1, :] = value * (own[3][col : col + 1] * (SCALE * SCALE))


def fine_tables(brick):
    ext_x = brick.px + 2 * REACH
    rows_y = brick.py + POINTS * brick.by
    out_lanes = brick.blocks * 128
    in_lanes = round_up(max(ext_x * brick.zpad, out_lanes), 128)
    count = len(FINE_WIDTHS)
    along_xz = np.zeros((in_lanes, count * out_lanes), np.float32)
    along_y = np.zeros((brick.py, count * rows_y), np.float32)

    def tap(dist, width):
        return np.where(np.abs(dist) <= REACH, np.exp(-(dist * dist) / (2.0 * width * width)), 0.0)

    for number, (width, weight) in enumerate(zip(FINE_WIDTHS, FINE_WEIGHTS)):
        mat_z = np.zeros((brick.zpad, brick.zpad))
        for step in range(-REACH, REACH + 1):
            for z in range(brick.pz):
                mat_z[(z + step) % brick.pz, z] += weight * tap(np.float64(step), width)
        mat_x = tap(np.arange(ext_x)[:, None] - np.arange(brick.px)[None, :] - REACH, width)
        dense = np.kron(mat_x, mat_z)
        along_xz[: dense.shape[0], number * out_lanes : number * out_lanes + dense.shape[1]] = dense
        out_y = np.arange(POINTS * brick.by + 3) - 1.0
        in_y = np.arange(rows_y) - 1.0 - POINTS * brick.by
        along_y[: len(out_y), number * rows_y : (number + 1) * rows_y] = tap(
            out_y[:, None] - in_y[None, :], width
        )
    return along_xz, along_y


def coarse_table(brick):
    table = np.zeros((len(COARSE_WEIGHTS) * brick.coarse_lanes, 128), np.float32)
    length = brick.ck
    for number, (fraction, weight) in enumerate(zip(COARSE_FRACTIONS, COARSE_WEIGHTS)):
        width = length / fraction
        for row in range(brick.cj * brick.ck):
            for z in range(brick.pz):
                dist = (row - z // 2) % length
                dist = min(dist, length - dist)
                table[number * brick.coarse_lanes + row, z] = weight * math.exp(
                    -(dist * dist) / (2.0 * width * width)
                )
    return table


def gauss(row, col, length, fraction):
    dist = lax.rem(row - col + 2 * length, length)
    dist = jnp.minimum(dist, length - dist).astype(F32)
    width = length / fraction
    return jnp.exp(dist * dist * (-1.0 / (2.0 * width * width)))


def potential_kernel(brick, sender, n_msgs, *refs):
    atoms = brick.atoms
    msg_ref = refs[0]
    other_msgs = refs[1 : 1 + n_msgs]
    (
        whole_ref,
        short_ref,
        xz_high_ref,
        xz_low_ref,
        y_ref,
        coarse_z_ref,
        out_ref,
        pot_ref,
    ) = refs[1 + n_msgs :]
    step_y = POINTS * brick.by
    rows_y = brick.py + step_y
    in_lanes = xz_high_ref.shape[0]
    out_lanes = brick.blocks * 128
    grid = None
    for dx in (-1, 0, 1):
        grids = []
        for dy in (-1, 0, 1):
            near = slice(brick.grid_row, brick.msg_rows)
            span = slice(0, out_lanes)
            if (dx, dy) == (0, 0):
                grids.append(msg_ref[near, span])
            else:
                grids.append(other_msgs[sender[(dx, dy)]][near, span])
        tiles = [None] * ((brick.py + 2 * step_y) // 8)
        for number, part in enumerate(grids):
            for tile in range(brick.py // 8):
                spot = tile + number * step_y // 8
                value = part[8 * tile : 8 * tile + 8]
                tiles[spot] = value if tiles[spot] is None else tiles[spot] + value
        column = jnp.concatenate(tiles[: rows_y // 8], axis=0)
        if in_lanes > out_lanes:
            column = jnp.concatenate(
                [column, jnp.zeros((rows_y, in_lanes - out_lanes), F32)], axis=1
            )
        shift = (REACH + POINTS * brick.bx * dx) * brick.zpad
        column = pltpu.roll(column, shift % in_lanes, 1)
        grid = column if grid is None else grid + column
    pieces = jnp.concatenate(split(grid, 2), axis=0).astype(BF16)
    mixed = mul(pieces, xz_high_ref[...]) + mul(pieces, xz_low_ref[...])
    mixed = mixed[:rows_y] + mixed[rows_y:]
    mixed = jnp.concatenate(
        [mixed[:, n * out_lanes : (n + 1) * out_lanes] for n in range(len(FINE_WIDTHS))], axis=0
    )
    fine = mul(y_ref[...], mixed, HIGHEST)

    total_x = 2 * brick.bx * brick.n_space
    total_y = 2 * brick.by * brick.n_sub
    first_x = lax.axis_index("space") * (2 * brick.bx)
    first_y = lax.axis_index("sub") * (2 * brick.by)
    out_rows = round_up(brick.px, 8)
    shape = (out_rows, brick.n_space * brick.coarse_rows)
    point = lax.broadcasted_iota(jnp.int32, shape, 0)
    lane = lax.broadcasted_iota(jnp.int32, shape, 1)
    row_x = first_x + (point + 1) // 2 - 1
    col_x = lane // brick.coarse_rows * (2 * brick.bx) + lane % brick.coarse_rows - 1
    live = lane % brick.coarse_rows < brick.ci
    mats_x = jnp.concatenate(
        [
            jnp.where(live, gauss(row_x, col_x, total_x, fraction), 0.0)
            for fraction in COARSE_FRACTIONS
        ],
        axis=0,
    )
    shape = (brick.py, brick.coarse_lanes)
    point = lax.broadcasted_iota(jnp.int32, shape, 0)
    lane = lax.broadcasted_iota(jnp.int32, shape, 1)
    row_y = first_y + (point + 1) // 2 - 1
    live = lane < brick.cj * brick.ck
    lefts = [[None] * brick.px for _ in COARSE_FRACTIONS]
    for sub in range(brick.n_sub):
        part = whole_ref[:, sub].reshape(
            brick.n_space * brick.coarse_rows, brick.coarse_lanes
        )
        mixed = mul(mats_x, part, HIGHEST)
        col_y = sub * (2 * brick.by) + lane // brick.ck - 1
        for number, fraction in enumerate(COARSE_FRACTIONS):
            mat_y = jnp.where(live, gauss(row_y, col_y, total_y, fraction), 0.0)
            for x in range(brick.px):
                row = number * out_rows + x
                value = mixed[row : row + 1] * mat_y
                done = lefts[number][x]
                lefts[number][x] = value if done is None else done + value
    left = jnp.concatenate([jnp.concatenate(rows, axis=0) for rows in lefts], axis=1)
    parts = mul(jnp.concatenate(split(left, 2), axis=0).astype(BF16), coarse_z_ref[...])
    count = left.shape[0]
    coarse = parts[:count] + pltpu.roll(parts[:count], 128 - brick.zpad, 1) + parts[count:]
    lane = lax.broadcasted_iota(jnp.int32, (brick.py, 128), 1)
    for x in range(brick.px):
        block, shift = divmod(x, brick.group)
        value = fine[:, block * 128 : (block + 1) * 128]
        if shift:
            value = pltpu.roll(value, 128 - shift * brick.zpad, 1)
        value = value + coarse[x * brick.py : (x + 1) * brick.py]
        high, low = split(jnp.where(lane < brick.zpad, value, 0.0), 2)
        pot_ref[x] = (
            high + pltpu.roll(high, brick.zpad, 1) + pltpu.roll(low, 2 * brick.zpad, 1)
        )

    for x in range(brick.bx):
        for y in range(brick.by):
            col = brick.col(x, y)
            rows = [
                msg_ref[k * brick.cols + col : k * brick.cols + col + 1, 0 : brick.lanes]
                for k in range(4)
            ]
            shifted = [
                shift_xy(brick, rows[0]),
                shift_xy(brick, rows[1]),
                shift_z(brick, rows[2]),
            ]
            weights = [spline(value) for value in shifted]
            slopes = [spline_slope(value) for value in shifted]
            box = jnp.concatenate(
                [
                    pot_ref[POINTS * x + e, POINTS * y : POINTS * y + 8, 0 : 3 * brick.zpad]
                    for e in range(TAPS)
                ],
                axis=0,
            )
            high, low = split(jnp.concatenate([weights[2], slopes[2]], axis=1), 2)
            tables = jnp.concatenate([high, low, high], axis=0).astype(BF16)
            both = mul(box.astype(BF16), tables)
            along_z = both[:, : brick.lanes]
            sloped_z = both[:, brick.lanes :]
            sums = [0.0, 0.0, 0.0]
            for e in range(TAPS):
                weight = weights[0][e : e + 1]
                slope = slopes[0][e : e + 1]
                flat = along_z[8 * e : 8 * e + 8]
                steep = sloped_z[8 * e : 8 * e + 8]
                sums[0] = sums[0] + flat * slope
                sums[1] = sums[1] + flat * weight
                sums[2] = sums[2] + steep * weight
            across = (weights[1], slopes[1], weights[1])
            for comp in range(3):
                force = jnp.sum(sums[comp] * across[comp], axis=0, keepdims=True)
                row = comp * brick.cols + col
                force = short_ref[row : row + 1, :] - POINTS * (rows[3] * force)
                for z in range(brick.bz):
                    out_ref[comp, x, z, y : y + 1, :] = force[:, z * atoms : (z + 1) * atoms]


VMEM = pl.BlockSpec(memory_space=pltpu.VMEM)
SMEM = pl.BlockSpec(memory_space=pltpu.SMEM)
ANY = pl.BlockSpec(memory_space=pl.ANY)
WHOLE = pl.BlockSpec()


def call(kernel, out_shape, in_specs, scratch, flops, *args, out_spec=VMEM, grant=40):
    single = not isinstance(out_shape, (list, tuple))
    return pl.pallas_call(
        kernel,
        out_shape=out_shape,
        in_specs=in_specs,
        out_specs=out_spec if single else [out_spec] * len(out_shape),
        scratch_shapes=scratch,
        compiler_params=pltpu.CompilerParams(vmem_limit_bytes=grant * 1024 * 1024),
        cost_estimate=pl.CostEstimate(flops=flops, bytes_accessed=10**5, transcendentals=0),
    )(*args)


def neighbours(brick, msg):
    size, wide = brick.n_space, brick.n_sub
    found = {}
    sender = {}
    msgs = []
    for dx in (1, 0, -1):
        for dy in (0, -1, 1):
            if (dx, dy) == (0, 0):
                continue
            key = (dx % size, dy % wide)
            if key not in found:
                found[key] = len(msgs)
                pairs = [
                    ((i + dx) % size * wide + (j + dy) % wide, i * wide + j)
                    for i in range(size)
                    for j in range(wide)
                ]
                msgs.append(lax.ppermute(msg, ("space", "sub"), pairs))
            sender[(dx, dy)] = found[key]
    return sender, msgs


def body(n_space, n_sub, positions, charges, counts):
    brick = Brick(charges.shape, n_space, n_sub)
    n_dev = n_space * n_sub
    along_xz, along_y = fine_tables(brick)
    xz_high = along_xz.astype(BF16)
    xz_low = (along_xz - xz_high.astype(np.float32)).astype(BF16)
    coarse_z = coarse_table(brick)
    coarse_high = coarse_z.astype(BF16)
    coarse_low = (coarse_z - coarse_high.astype(np.float32)).astype(BF16)
    coarse_pair = coarse_high.copy()
    coarse_pair[:, brick.zpad : 2 * brick.zpad] = coarse_low[:, : brick.zpad]

    turned = (positions.transpose(0, 1, 3, 2, 4), charges.transpose(0, 2, 1, 3))
    msg, coarse = call(
        functools.partial(spread_kernel, brick),
        [
            jax.ShapeDtypeStruct((brick.msg_rows, brick.msg_lanes), F32),
            jax.ShapeDtypeStruct((n_dev, brick.coarse_rows, brick.coarse_lanes), F32),
        ],
        [ANY, ANY, ANY],
        [
            pltpu.SMEM(counts.shape, jnp.int32),
            pltpu.VMEM(turned[0].shape, F32),
            pltpu.VMEM(turned[1].shape, F32),
            pltpu.VMEM((brick.px, brick.py, 128), F32),
            pltpu.SemaphoreType.DMA((3,)),
        ],
        10**7,
        counts,
        *turned,
        grant=64,
    )
    sender, msgs = neighbours(brick, msg)
    whole = lax.all_to_all(coarse, ("space", "sub"), 0, 0, tiled=True)
    whole = whole.reshape(n_space, n_sub, brick.coarse_rows, brick.coarse_lanes)

    n_col = len(brick.columns)
    short = call(
        functools.partial(pairs_kernel, brick, sender, len(msgs)),
        jax.ShapeDtypeStruct((brick.force_rows, brick.lanes), F32),
        [VMEM] * (1 + len(msgs)),
        [
            pltpu.VMEM((4 * brick.ext_rows, brick.lanes), F32),
            pltpu.VMEM((brick.lanes // 128, FEATURES * brick.ext_rows, 128), F32),
            pltpu.VMEM((brick.lanes // 128, SOURCES * brick.ext_rows, 128), F32),
            pltpu.VMEM((brick.lanes // 128, FEATURES * brick.own_rows, 128), F32),
            pltpu.VMEM((brick.lanes // 128, SOURCES * brick.own_rows, 128), F32),
            pltpu.VMEM((n_col, brick.lanes, FEATURES), BF16),
            pltpu.VMEM((n_col, brick.bz, SOURCES, 2 * brick.atoms), BF16),
            pltpu.VMEM((brick.cols, brick.bz, FEATURES, brick.lanes), BF16),
            pltpu.VMEM((brick.cols, brick.bz, brick.bz, SOURCES, 2 * brick.atoms), BF16),
            pltpu.VMEM((brick.cols, brick.bz, SOURCES, brick.lanes), F32),
            pltpu.VMEM((brick.cols, brick.bz, brick.atoms, brick.kept), BF16),
        ],
        10**10,
        msg,
        *msgs,
    )
    comps, size_x, size_y, size_z, atoms = positions.shape
    forces = call(
        functools.partial(potential_kernel, brick, sender, len(msgs)),
        jax.ShapeDtypeStruct((comps, size_x, size_z, size_y, atoms), F32),
        [VMEM] * (7 + len(msgs)),
        [
            pltpu.VMEM((brick.px, brick.py, 128), F32),
        ],
        10**8,
        msg,
        *msgs,
        whole,
        short,
        xz_high,
        xz_low,
        jnp.asarray(along_y),
        coarse_pair,
        out_spec=WHOLE,
    )
    return forces.transpose(0, 1, 3, 2, 4)


def solution(mesh):
    in_specs = (
        P(None, "space", "sub", None, None),
        P("space", "sub", None, None),
        P("space", "sub", None),
    )
    out_specs = P(None, "space", "sub", None, None)
    run = functools.partial(body, mesh.shape["space"], mesh.shape["sub"])
    return jax.shard_map(run, mesh=mesh, in_specs=in_specs, out_specs=out_specs, check_vma=False)
```
